32 devices in a mesh: wide: 8 (over y, x, core), narrow: 4 (over z).
Axes of the slice: x: 2, y: 2, z: 4, core: 2. Of those that a mesh axis runs over, the one named last changes fastest.
Arguments:
- fractions: float32 [3, 16384], P(None, ('wide', 'narrow')), may hold values from 0 to 1
- cell_lengths: float32 [3], replicated, may hold values from 18 to 30
- features: bfloat16 [16384, 128], P(('wide', 'narrow')), may hold values from -6 to 6
- atom_counts: int32 [32], P(('wide', 'narrow')), may hold values from 384 to 512, as said below
- send_index: int32 [128, 384], P(('wide', 'narrow')), may hold values from 0 to 511, as said below
- senders: int32 [16, 16384], P(None, ('wide', 'narrow')), may hold values from 0 to 2047, as said below
- radial: float32 [16, 16384], P(None, ('wide', 'narrow')), may hold values from -1.5 to 1.5
- self_weight: bfloat16 [2, 128, 128], replicated, may hold values from -0.5 to 0.5
- message_weight: bfloat16 [2, 128, 128], replicated, may hold values from -0.5 to 0.5
- charge_weight: bfloat16 [128, 4], replicated, may hold values from -0.5 to 0.5
- wave_numbers: int32 [3, 8192], replicated, may hold values from -8 to 8, as said below
Outputs:
- forces: float32 [3, 16384], P(None, ('wide', 'narrow'))
- born_charges: float32 [3, 16384], P(None, ('wide', 'narrow'))
- energy: float32 [], replicated
The draws below stay inside these ranges and needn't reach their ends.
Inputs may be any that keep to these rules, and one draw needn't show every extreme that they name: `atom_counts`: every value lies between 384 and 512; some device holds exactly 512; slots at or above a device's count are padding. `send_index`: every entry of device d's four blocks is below atom_counts[d]. `senders`: for an atom slot of device d an entry is either a live local atom (below atom_counts[d]) or 512 + b * 384 + g, ghost row g of received block b. `wave_numbers`: the first component is 1 to 8, the others -8 to 8.
All inputs are finite; a program needn't handle non-finite values.
Results may differ from the reference program's by a relative error of at most 0.014.
Values sent between devices are 32-bit elements; how exact they have to be, the bound alone decides.
No kernel may reach another device: no remote copies, remote signals or barrier semaphores. Data moves between devices by JAX's collectives and lax.ppermute only.
A program may use at most 192 MiB of HBM per device.

```python
import math
import jax
import jax.numpy as jnp
from jax import lax

F = 128
CHAN = 4
KVEC = 8192
KMAX = 8
LAYERS = 2
NEIGH = 16
ATOM_DEV = 512
GHOST = 384
EXT = 2048
ATOMS = 16384
N_WIDE = 8
N_NARROW = 4
DEVICES = 32


def shared_counts(key):
    values = jax.random.randint(jax.random.fold_in(key, 11), (DEVICES,), GHOST, ATOM_DEV + 1)
    full = jax.random.randint(jax.random.fold_in(key, 12), (), 0, DEVICES)
    return jnp.where(jnp.arange(DEVICES) == full, ATOM_DEV, values).astype(jnp.int32)


def draw_atom_counts(key, part):
    return shared_counts(key)


def draw_send_index(key, part):
    counts_now = shared_counts(key)
    values = jax.random.randint(jax.random.fold_in(key, 21), (DEVICES, 4, GHOST), 0, counts_now[:, None, None])
    return values.reshape(4 * DEVICES, GHOST).astype(jnp.int32)


def draw_senders(key, part):
    counts_now = shared_counts(key)
    shape_all = (NEIGH, DEVICES, ATOM_DEV)
    local_rows = jax.random.randint(jax.random.fold_in(key, 31), shape_all, 0, counts_now[None, :, None])
    ghost_rows = jax.random.randint(jax.random.fold_in(key, 32), shape_all, ATOM_DEV, ATOM_DEV + 4 * GHOST)
    choose_local = jax.random.randint(jax.random.fold_in(key, 33), shape_all, 0, 5) < 3
    return jnp.where(choose_local, local_rows, ghost_rows).reshape(NEIGH, DEVICES * ATOM_DEV).astype(jnp.int32)


def draw_wave_numbers(key, part):
    first = jax.random.randint(jax.random.fold_in(key, 41), (1, KVEC), 1, KMAX + 1)
    others = jax.random.randint(jax.random.fold_in(key, 42), (2, KVEC), -KMAX, KMAX + 1)
    return jnp.concatenate([first, others], axis=0).astype(jnp.int32)


def levels(stream_key, extent, cuts, least, high):
    factor_of = 1.0
    for dim, parts in cuts:
        steps = jax.random.uniform(jax.random.fold_in(jax.random.fold_in(stream_key, 6), dim), (parts,), jnp.float32, least / len(cuts), high / len(cuts))
        factor_of = factor_of * jnp.repeat(jnp.exp(steps), extent[dim] // parts).reshape((-1,) + (1,) * (len(extent) - 1 - dim))
    return factor_of


def scatter_about(key, shape, scale, most, shards=(), kind=jnp.bfloat16):
    loudness = levels(key, shape, shards, -0.22, 0.18) if shards else 1.0
    entries = jax.random.normal(key, shape, jnp.float32) * scale * loudness
    return jnp.minimum(jnp.maximum(entries, -most), most).astype(kind)


def setup_inputs(seed: int = 0) -> dict:
    streams_of = jax.random.split(jax.random.key(seed), 12)
    return {
        "fractions": jnp.clip(1.0 * jax.random.uniform(streams_of[0], (3, ATOMS), jnp.float32) ** levels(streams_of[0], (3, ATOMS), ((1, 32),), -0.2, 0.2), 0.0, 1.0),
        "cell_lengths": jnp.clip(jax.random.uniform(streams_of[1], (3,), jnp.float32, 18.0, 30.0), 18.0, 30.0),
        "features": scatter_about(streams_of[2], (ATOMS, F), 1.0, 6.0, ((0, 32),)),
        "atom_counts": draw_atom_counts(jax.random.fold_in(streams_of[11], 71), 0),
        "send_index": draw_send_index(jax.random.fold_in(streams_of[11], 71), 0),
        "senders": draw_senders(jax.random.fold_in(streams_of[11], 71), 0),
        "radial": scatter_about(streams_of[6], (NEIGH, ATOMS), 0.25, 1.5, ((1, 32),), jnp.float32),
        "self_weight": scatter_about(streams_of[7], (LAYERS, F, F), F ** -0.5, 0.5),
        "message_weight": scatter_about(streams_of[8], (LAYERS, F, F), F ** -0.5, 0.5),
        "charge_weight": scatter_about(streams_of[9], (F, CHAN), F ** -0.5, 0.5),
        "wave_numbers": draw_wave_numbers(jax.random.fold_in(streams_of[11], 71), 0),
    }


smearing = 0.5
two_pi = 2.0 * math.pi
highest = lax.Precision.HIGHEST

def phase_angles(fractions, numbers):
    return two_pi * (fractions[0][:, None] * numbers[0][None, :] + fractions[1][:, None] * numbers[1][None, :] + fractions[2][:, None] * numbers[2][None, :])

def wave_weights(cell_lengths, numbers):
    wave = two_pi * numbers / cell_lengths[:, None]
    squared = lax.optimization_barrier(jnp.sum(wave * wave, axis=0))
    return jnp.exp(-0.5 * smearing * smearing * squared) / squared

def factor_terms(fractions, charges, numbers):
    angles = phase_angles(fractions, numbers)
    cosine = jnp.cos(angles).astype(jnp.bfloat16)
    sine_part = jnp.sin(angles).astype(jnp.bfloat16)
    charge_rows = charges.astype(jnp.bfloat16)
    real_part = jnp.dot(charge_rows, cosine, preferred_element_type=jnp.float32)
    imag_part = jnp.dot(charge_rows, sine_part, preferred_element_type=jnp.float32)
    return jnp.stack([real_part, imag_part])

def gradient_terms(fractions, charges, numbers, factors, weights):
    angles = phase_angles(fractions, numbers)
    cosine = jnp.cos(angles)
    sine_part = jnp.sin(angles)
    dims = (((0,), (0,)), ((), ()))
    with_real = lax.dot_general(charges, weights * factors[0], dims, precision=highest, preferred_element_type=jnp.float32)
    with_imag = lax.dot_general(charges, weights * factors[1], dims, precision=highest, preferred_element_type=jnp.float32)
    joined = (with_imag * cosine - with_real * sine_part).astype(jnp.bfloat16)
    return lax.dot_general(numbers.astype(jnp.bfloat16), joined, (((1,), (1,)), ((), ())), preferred_element_type=jnp.float32)

def aggregate(inputs):
    extended, sender_rows, radial_rows = inputs
    gathered = jnp.take(extended, sender_rows, axis=0)
    return lax.optimization_barrier(jnp.sum(radial_rows[:, :, None] * gathered, axis=0))

def pick_block(message_rows, pick_rows):
    return jnp.take(message_rows, pick_rows, axis=0)

def reference(fractions, cell_lengths, features, atom_counts, send_index, senders, radial, self_weight, message_weight, charge_weight, wave_numbers):
    slot_ids = jnp.arange(ATOM_DEV, dtype=jnp.int32)
    alive_mask = (slot_ids[None, :] < atom_counts[:, None]).reshape(ATOMS)
    sends = send_index.reshape(N_WIDE, N_NARROW, 4, GHOST)
    sender_blocks = senders.reshape(NEIGH, DEVICES, ATOM_DEV).transpose(1, 0, 2)
    radial_blocks = radial.reshape(NEIGH, DEVICES, ATOM_DEV).transpose(1, 0, 2)
    hidden = features
    for layer_index in range(LAYERS):
        message = jnp.dot(hidden, message_weight[layer_index], preferred_element_type=jnp.float32)
        blocks = message.reshape(N_WIDE, N_NARROW, ATOM_DEV, F)
        sent_rows = jax.vmap(jax.vmap(pick_block))(blocks, sends)
        lower_wide = jnp.roll(sent_rows[:, :, 1], 1, axis=0)
        upper_wide = jnp.roll(sent_rows[:, :, 0], -1, axis=0)
        lower_narrow = jnp.roll(sent_rows[:, :, 3], 1, axis=1)
        upper_narrow = jnp.roll(sent_rows[:, :, 2], -1, axis=1)
        extended = jnp.concatenate([blocks, lower_wide, upper_wide, lower_narrow, upper_narrow], axis=2).reshape(DEVICES, EXT, F)
        combined = lax.map(aggregate, (extended, sender_blocks, radial_blocks)).reshape(ATOMS, F)
        self_term = jnp.dot(hidden, self_weight[layer_index], preferred_element_type=jnp.float32)
        hidden = (hidden.astype(jnp.float32) + jax.nn.silu(self_term + combined)).astype(jnp.bfloat16)
    charges = jnp.dot(hidden, charge_weight, preferred_element_type=jnp.float32)
    charges = jnp.where(alive_mask[:, None], charges, 0.0).T
    numbers = wave_numbers.astype(jnp.float32)
    frac_blocks = fractions.reshape(3, DEVICES, ATOM_DEV).transpose(1, 0, 2)
    charge_blocks = charges.reshape(CHAN, DEVICES, ATOM_DEV).transpose(1, 0, 2)

    def add_factors(running, inputs):
        return (running + factor_terms(inputs[0], inputs[1], numbers), None)
    factors, _ = lax.scan(add_factors, jnp.zeros((2, CHAN, KVEC), jnp.float32), (frac_blocks, charge_blocks))
    weights = wave_weights(cell_lengths, numbers)
    energy_scale = 4.0 / math.sqrt(ATOMS * KVEC)
    energy = 0.5 * energy_scale * jnp.sum(weights * (factors[0] * factors[0] + factors[1] * factors[1]))

    def device_gradient(inputs):
        return gradient_terms(inputs[0], inputs[1], numbers, factors, weights)
    gradient = lax.map(device_gradient, (frac_blocks, charge_blocks)).transpose(1, 0, 2).reshape(3, ATOMS)
    forces = jnp.where(alive_mask[None, :], -(two_pi * energy_scale / cell_lengths[:, None]) * gradient, 0.0)
    charge_total = lax.optimization_barrier(jnp.sum(charges, axis=0))
    born_charges = jnp.where(alive_mask[None, :], charge_total[None, :] * jnp.cos(two_pi * fractions), 0.0)
    return (forces, born_charges, energy)
```

```python
import functools
import math

import jax
import jax.numpy as jnp
from jax import lax
from jax.experimental import pallas as pl
from jax.experimental.pallas import tpu as pltpu
from jax.sharding import PartitionSpec as P

smearing = 0.5
two_pi = 2.0 * math.pi
kmax = 8
grid_rows = (2 * kmax + 1) * kmax
f32 = jnp.float32
bf16 = jnp.bfloat16
highest = lax.Precision.HIGHEST
params = pltpu.CompilerParams(vmem_limit_bytes=48 * 1024 * 1024)


def dot_nn(a, b):
    return lax.dot_general(a, b, (((1,), (0,)), ((), ())), preferred_element_type=f32)


def dot_tn(a, b):
    return lax.dot_general(a, b, (((0,), (0,)), ((), ())), preferred_element_type=f32)


def dot_nt(a, b, precision=None):
    return lax.dot_general(
        a, b, (((1,), (1,)), ((), ())), precision=precision, preferred_element_type=f32
    )


def pick_columns(hidden, index_ref, block):
    atoms = hidden.shape[1]
    ghosts = index_ref.shape[1]
    row_ids = lax.broadcasted_iota(jnp.int32, (atoms, ghosts), 0)
    one_hot = jnp.where(row_ids == index_ref[block : block + 1, :], 1.0, 0.0).astype(bf16)
    return dot_nn(hidden, one_hot)


def first_kernel(features_ref, index_ref, hidden_ref, *picked_refs):
    hidden = jnp.transpose(features_ref[...].astype(f32)).astype(bf16)
    hidden_ref[...] = hidden
    for block in (2, 3, 0, 1):
        picked_refs[block][...] = pick_columns(hidden, index_ref, block)


def edge_kernel(senders_ref, radial_ref, edges_ref):
    slots, atoms = senders_ref.shape
    rows = 128
    lanes = 128
    row_ids = lax.broadcasted_iota(jnp.int32, (rows, lanes), 0).astype(f32).astype(bf16)

    def one_tile(tile, carry):
        first = pl.multiple_of(tile * rows, rows)
        for part in range(atoms // lanes):
            window = pl.ds(part * lanes, lanes)
            local = jnp.clip(senders_ref[:, window] - first, -1, rows)
            local = local.astype(f32).astype(bf16)
            weight = radial_ref[:, window].astype(bf16)
            total = jnp.zeros((rows, lanes), bf16)
            for slot in range(slots):
                total = total + jnp.where(
                    row_ids == local[slot : slot + 1, :],
                    weight[slot : slot + 1, :],
                    jnp.zeros((), bf16),
                )
            edges_ref[pl.ds(first, rows), window] = total
        return carry

    lax.fori_loop(0, edges_ref.shape[0] // rows, one_tile, 0)


def interact(hidden, ghost_refs, edges_ref, self_ref, message_ref):
    atoms = hidden.shape[1]
    ghosts = ghost_refs[0].shape[1]
    gathered = dot_nn(hidden, edges_ref[0:atoms, :])
    for block, ghost_ref in enumerate(ghost_refs):
        start = atoms + block * ghosts
        gathered = gathered + dot_nn(
            ghost_ref[...].astype(bf16), edges_ref[start : start + ghosts, :]
        )
    high = gathered.astype(bf16)
    low = (gathered - high.astype(f32)).astype(bf16)
    message = message_ref[...]
    total = dot_tn(self_ref[...], hidden) + dot_tn(message, high) + dot_tn(message, low)
    return (hidden.astype(f32) + total * (1.0 / (1.0 + jnp.exp(-total)))).astype(bf16)


def layer_kernel(
    hidden_ref, g0, g1, g2, g3, edges_ref, self_ref, message_ref, index_ref, out_ref, *picked_refs
):
    hidden = interact(hidden_ref[...], (g0, g1, g2, g3), edges_ref, self_ref, message_ref)
    out_ref[...] = hidden
    for block in (2, 3, 0, 1):
        picked_refs[block][...] = pick_columns(hidden, index_ref, block)


def last_kernel(
    hidden_ref,
    g0,
    g1,
    g2,
    g3,
    edges_ref,
    self_ref,
    message_ref,
    readout_ref,
    count_ref,
    real_ref,
    imag_ref,
    third_ref,
    sums_ref,
    charges_ref,
    lattice_ref,
):
    hidden = interact(hidden_ref[...], (g0, g1, g2, g3), edges_ref, self_ref, message_ref)
    atoms = hidden.shape[1]
    slot_ids = lax.broadcasted_iota(jnp.int32, (8, atoms), 1)
    charges = jnp.where(slot_ids < count_ref[0], dot_tn(readout_ref[...], hidden), 0.0)
    charges_ref[...] = charges
    cosine = third_ref[0:8, :]
    sine = third_ref[8:16, :]
    for c in range(4):
        lattice_ref[8 * c : 8 * c + 8, :] = charges[c : c + 1, :] * cosine
        lattice_ref[32 + 8 * c : 40 + 8 * c, :] = charges[c : c + 1, :] * sine
    with_cos = lattice_ref[0:32, :].astype(bf16)
    with_sin = lattice_ref[32:64, :].astype(bf16)
    none = jnp.zeros((64, atoms), bf16)
    real = real_ref[...]
    imag = imag_ref[...]
    sums_ref[0:grid_rows, :] = dot_nt(real, jnp.concatenate([with_cos, with_sin, none])) + dot_nt(
        imag, jnp.concatenate([none, with_sin, with_cos])
    )
    flat = charges.astype(bf16)
    flat_real = dot_nt(flat, real)
    flat_imag = dot_nt(flat, imag)
    sums_ref[grid_rows : grid_rows + 4, :] = flat_real[0:4, 0:128]
    sums_ref[grid_rows + 4 : grid_rows + 8, :] = flat_imag[0:4, 0:128]
    sums_ref[grid_rows + 8 : grid_rows + 16, :] = jnp.zeros((8, 128), f32)
    sums_ref[grid_rows + 8 : grid_rows + 12, 0:8] = flat_real[0:4, 128:grid_rows]
    sums_ref[grid_rows + 12 : grid_rows + 16, 0:8] = flat_imag[0:4, 128:grid_rows]


def wave_weight(m0, m1, m2, cell_ref):
    w0 = two_pi * m0 / cell_ref[0]
    w1 = two_pi * m1 / cell_ref[1]
    w2 = two_pi * m2 / cell_ref[2]
    squared = w0 * w0 + w1 * w1 + w2 * w2
    return jnp.exp(-0.5 * smearing * smearing * squared) / squared


def table_kernel(
    fractions_ref, cell_ref, numbers_ref, real_ref, imag_ref, third_ref, factor_ref, flat_ref, acc, acc0
):
    atoms = fractions_ref.shape[1]
    orders = lax.broadcasted_iota(jnp.int32, (8, atoms), 0).astype(f32) + 1.0
    cosines, sines = [], []
    for axis in range(3):
        turns = orders * fractions_ref[axis : axis + 1, :]
        angle = two_pi * (turns - jnp.round(turns))
        cosines.append(jnp.cos(angle))
        sines.append(jnp.sin(angle))
    third_ref[0:8, :] = cosines[2]
    third_ref[8:16, :] = sines[2]
    for axis in range(3):
        third_ref[16 + axis : 17 + axis, :] = cosines[axis][0:1, :]
    c0, s0 = cosines[0], sines[0]
    for m in range(-kmax, kmax + 1):
        window = pl.ds((m + kmax) * kmax, kmax)
        if m == 0:
            re, im = c0, s0
        else:
            row = abs(m) - 1
            c1 = cosines[1][row : row + 1, :]
            s1 = sines[1][row : row + 1, :]
            if m < 0:
                s1 = -s1
            re, im = c0 * c1 - s0 * s1, s0 * c1 + c0 * s1
        real_ref[window, :] = re.astype(bf16)
        imag_ref[window, :] = im.astype(bf16)

    acc[...] = jnp.zeros_like(acc)
    acc0[...] = jnp.zeros_like(acc0)
    width = math.gcd(numbers_ref.shape[1], 1024)
    plane_ids = lax.broadcasted_iota(jnp.int32, (grid_rows, width), 0)
    third_ids = lax.broadcasted_iota(jnp.int32, (32, width), 0)
    third_ids = jnp.where(third_ids < 8, third_ids + 1, jnp.where(third_ids < 16, 7 - third_ids, 0))
    zero_row = lax.broadcasted_iota(jnp.int32, (32, width), 0) <= 16

    def count(step, carry):
        window = pl.ds(pl.multiple_of(step * width, width), width)
        numbers = numbers_ref[:, window]
        plane = (numbers[1:2, :] + kmax) * kmax + numbers[0:1, :] - 1
        in_plane = jnp.where(plane_ids == plane, 1.0, 0.0).astype(bf16)
        in_third = jnp.where((third_ids == numbers[2:3, :]) & zero_row, 1.0, 0.0).astype(bf16)
        acc[...] += dot_nt(in_plane, in_third)
        acc0[...] += dot_nt(in_third[16:32, :], in_plane)
        return carry

    lax.fori_loop(0, numbers_ref.shape[1] // width, count, 0)

    lane = lax.broadcasted_iota(jnp.int32, (grid_rows, 128), 1)
    row = lax.broadcasted_iota(jnp.int32, (grid_rows, 128), 0)
    m0 = (row % 8 + 1).astype(f32)
    m1 = (row // 8 - kmax).astype(f32)
    m2 = (lane % 8 + 1).astype(f32)
    weight = wave_weight(m0, m1, m2, cell_ref)
    from_ids = lax.broadcasted_iota(jnp.int32, (32, 128), 0)
    lane_ids = lax.broadcasted_iota(jnp.int32, (32, 128), 1) % 8
    expand_up = jnp.where(from_ids == lane_ids, 1.0, 0.0)
    expand_down = jnp.where(from_ids == lane_ids + 8, 1.0, 0.0)
    counts = acc[...]
    up = weight * jnp.dot(counts, expand_up, precision=highest, preferred_element_type=f32)
    down = weight * jnp.dot(counts, expand_down, precision=highest, preferred_element_type=f32)
    block = lane // 32
    first, second, third = block == 0, block == 1, block == 2
    factor_ref[0] = jnp.where(first, up, jnp.where(second, down, jnp.where(third, -up, -down)))
    factor_ref[1] = jnp.where(first, down, jnp.where(second, -up, jnp.where(third, -down, up)))
    factor_ref[2] = m2 * jnp.where(first, up, jnp.where(second, -down, jnp.where(third, -up, down)))
    factor_ref[3] = m2 * jnp.where(first, -down, jnp.where(second, -up, jnp.where(third, down, up)))
    lane0 = lax.broadcasted_iota(jnp.int32, (8, grid_rows), 1)
    n0 = (lane0 % 8 + 1).astype(f32)
    n1 = (lane0 // 8 - kmax).astype(f32)
    flat_ref[...] = wave_weight(n0, n1, 0.0 * n0, cell_ref) * acc0[0:1, :]


def force_kernel(
    scale,
    sums_ref,
    charges_ref,
    lattice_ref,
    real_ref,
    imag_ref,
    third_ref,
    factor_ref,
    flat_ref,
    cell_ref,
    count_ref,
    forces_ref,
    born_ref,
    energy_ref,
    flat_sums,
):
    atoms = real_ref.shape[1]
    sums = sums_ref[0:grid_rows, :]
    swapped = pltpu.roll(sums, 64, 1)
    plus = pltpu.roll(sums + swapped, 32, 1)
    minus = pltpu.roll(sums - swapped, 32, 1)
    f0 = factor_ref[0]
    f1 = factor_ref[1]
    even = f0 * plus + f1 * minus
    odd = factor_ref[2] * plus + factor_ref[3] * minus
    row = lax.broadcasted_iota(jnp.int32, (grid_rows, 128), 0)
    m0 = (row % 8 + 1).astype(f32)
    m1 = (row // 8 - kmax).astype(f32)
    flat_sums[:, 0:128] = sums_ref[grid_rows : grid_rows + 8, :]
    flat_sums[:, 128:grid_rows] = sums_ref[grid_rows + 8 : grid_rows + 16, 0:8]
    flat_re = flat_sums[0:4, :]
    flat_im = flat_sums[4:8, :]
    flat_weight = flat_ref[0:4, :]
    part = jnp.sum(jnp.abs(f0) * plus * plus + jnp.abs(f1) * minus * minus, axis=0, keepdims=True)
    flat_part = jnp.sum(
        flat_weight * (flat_re * flat_re + flat_im * flat_im), axis=0, keepdims=True
    )
    energy_ref[...] = (0.5 * scale) * (
        0.5 * jnp.sum(part, axis=1, keepdims=True) + jnp.sum(flat_part, axis=1, keepdims=True)
    )

    lane0 = lax.broadcasted_iota(jnp.int32, (4, grid_rows), 1)
    n0 = (lane0 % 8 + 1).astype(f32)
    n1 = (lane0 // 8 - kmax).astype(f32)
    up = flat_weight * flat_im
    down = -flat_weight * flat_re
    flat_up = jnp.concatenate([up * n0, up * n1], axis=0).astype(bf16)
    flat_down = jnp.concatenate([down * n0, down * n1], axis=0).astype(bf16)
    real = real_ref[...]
    imag = imag_ref[...]
    tables = [jnp.transpose(t) for t in (even * m0, even * m1, odd)]
    with_real = jnp.concatenate([t[0:64] for t in tables], axis=0).astype(bf16)
    with_imag = jnp.concatenate([t[64:128] for t in tables], axis=0).astype(bf16)
    from_real = dot_nn(with_real, real)
    from_imag = dot_nn(with_imag, imag)
    flat = dot_nn(flat_up, real) + dot_nn(flat_down, imag)
    with_cos = lattice_ref[0:32, :]
    with_sin = lattice_ref[32:64, :]
    charges = charges_ref[...]
    alive = lax.broadcasted_iota(jnp.int32, (1, atoms), 1) < count_ref[0]
    total = jnp.sum(charges[0:4], axis=0, keepdims=True)
    for axis in range(3):
        base = 64 * axis
        terms = with_cos * (from_real[base : base + 32] + from_imag[base + 32 : base + 64])
        terms = terms + with_sin * (from_real[base + 32 : base + 64] + from_imag[base : base + 32])
        gradient = jnp.sum(terms, axis=0, keepdims=True)
        if axis < 2:
            gradient = gradient + jnp.sum(
                charges[0:4] * flat[4 * axis : 4 * axis + 4], axis=0, keepdims=True
            )
        forces_ref[axis : axis + 1, :] = jnp.where(
            alive, -(two_pi * scale / cell_ref[axis]) * gradient, 0.0
        )
        born_ref[axis : axis + 1, :] = jnp.where(
            alive, total * third_ref[16 + axis : 17 + axis, :], 0.0
        )


def call(kernel, outs, *args, smem=(), scratch=(), cost=None):
    specs = [
        pl.BlockSpec(memory_space=pltpu.SMEM if i in smem else pltpu.VMEM)
        for i in range(len(args))
    ]
    return pl.pallas_call(
        kernel,
        out_shape=[jax.ShapeDtypeStruct(shape, dtype) for shape, dtype in outs],
        in_specs=specs,
        out_specs=[pl.BlockSpec(memory_space=pltpu.VMEM)] * len(outs),
        scratch_shapes=list(scratch),
        compiler_params=params,
        cost_estimate=cost,
    )(*args)


def shifted(block, axis, step):
    count = lax.axis_size(axis)
    return lax.ppermute(block, axis, [(i, (i + step) % count) for i in range(count)])


def exchange(picked):
    lower_narrow = shifted(picked[3], "narrow", 1)
    upper_narrow = shifted(picked[2], "narrow", -1)
    lower_wide = shifted(picked[1], "wide", 1)
    upper_wide = shifted(picked[0], "wide", -1)
    return lower_wide, upper_wide, lower_narrow, upper_narrow


def summed(block):
    for axis in ("wide", "narrow"):
        count = lax.axis_size(axis)
        step = 1
        while step < count:
            block = block + lax.ppermute(block, axis, [(i, i ^ step) for i in range(count)])
            step *= 2
    return block


def per_device(
    fractions,
    cell_lengths,
    features,
    atom_counts,
    send_index,
    senders,
    radial,
    self_weight,
    message_weight,
    charge_weight,
    wave_numbers,
):
    atoms, width = features.shape
    ghosts = send_index.shape[1]
    rows = atoms + 4 * ghosts
    total_atoms = atoms * lax.axis_size("wide") * lax.axis_size("narrow")
    scale = 4.0 / math.sqrt(total_atoms * wave_numbers.shape[1])
    picked_outs = [((width, ghosts), f32)] * 4
    hidden_out = [((width, atoms), bf16)]
    readout = jnp.pad(charge_weight, ((0, 0), (0, 8 - charge_weight.shape[1])))

    hidden, *picked = call(first_kernel, hidden_out + picked_outs, features, send_index)
    received = exchange(picked)
    (edges,) = call(
        edge_kernel,
        [((rows, atoms), bf16)],
        senders,
        radial,
        cost=pl.CostEstimate(flops=10**9, bytes_accessed=20 * 2**20, transcendentals=0),
    )
    layers = self_weight.shape[0]
    for layer in range(layers - 1):
        hidden, *picked = call(
            layer_kernel,
            hidden_out + picked_outs,
            hidden,
            *received,
            edges,
            self_weight[layer],
            message_weight[layer],
            send_index,
        )
        received = exchange(picked)
    real, imag, third, factor, flat = call(
        table_kernel,
        [
            ((grid_rows, atoms), bf16),
            ((grid_rows, atoms), bf16),
            ((24, atoms), f32),
            ((4, grid_rows, 128), f32),
            ((8, grid_rows), f32),
        ],
        fractions,
        cell_lengths,
        wave_numbers,
        smem=(1,),
        scratch=[pltpu.VMEM((grid_rows, 32), f32), pltpu.VMEM((16, grid_rows), f32)],
        cost=pl.CostEstimate(flops=10**9, bytes_accessed=20 * 2**20, transcendentals=0),
    )
    sums, charges, lattice = call(
        last_kernel,
        [((grid_rows + 16, 128), f32), ((8, atoms), f32), ((64, atoms), f32)],
        hidden,
        *received,
        edges,
        self_weight[layers - 1],
        message_weight[layers - 1],
        readout,
        atom_counts,
        real,
        imag,
        third,
        smem=(9,),
    )
    sums = summed(sums)
    forces, born_charges, energy = call(
        functools.partial(force_kernel, scale),
        [((3, atoms), f32), ((3, atoms), f32), ((1, 1), f32)],
        sums,
        charges,
        lattice,
        real,
        imag,
        third,
        factor,
        flat,
        cell_lengths,
        atom_counts,
        smem=(8, 9),
        scratch=[pltpu.VMEM((8, grid_rows), f32)],
    )
    return (forces, born_charges, energy[0, 0])


def solution(mesh):
    return jax.shard_map(
        per_device,
        mesh=mesh,
        in_specs=(
            P(None, ("wide", "narrow")),
            P(),
            P(("wide", "narrow"), None),
            P(("wide", "narrow")),
            P(("wide", "narrow"), None),
            P(None, ("wide", "narrow")),
            P(None, ("wide", "narrow")),
            P(),
            P(),
            P(),
            P(),
        ),
        out_specs=(P(None, ("wide", "narrow")), P(None, ("wide", "narrow")), P()),
        check_vma=False,
    )
```

```python
import functools
import math

import jax
import jax.numpy as jnp
from jax import lax
from jax.experimental import pallas as pl
from jax.experimental.pallas import tpu as pltpu
from jax.sharding import PartitionSpec as P

smearing = 0.5
two_pi = 2.0 * math.pi
kmax = 8
grid_rows = (2 * kmax + 1) * kmax
half_rows = 80
f32 = jnp.float32
bf16 = jnp.bfloat16
highest = lax.Precision.HIGHEST
params = pltpu.CompilerParams(vmem_limit_bytes=48 * 1024 * 1024)


def dot_nn(a, b):
    return lax.dot_general(a, b, (((1,), (0,)), ((), ())), preferred_element_type=f32)


def dot_tn(a, b):
    return lax.dot_general(a, b, (((0,), (0,)), ((), ())), preferred_element_type=f32)


def dot_nt(a, b, precision=None):
    return lax.dot_general(
        a, b, (((1,), (1,)), ((), ())), precision=precision, preferred_element_type=f32
    )


def pick_matrix(index_ref, block, atoms):
    row_ids = lax.broadcasted_iota(jnp.int32, (atoms, index_ref.shape[1]), 0)
    return jnp.where(row_ids == index_ref[block : block + 1, :], 1.0, 0.0).astype(bf16)


def first_kernel(features_ref, index_ref, hidden_ref, p2, p3):
    hidden = jnp.transpose(features_ref[...].astype(f32)).astype(bf16)
    hidden_ref[...] = hidden
    for block, picked_ref in ((2, p2), (3, p3)):
        picked_ref[...] = dot_nn(hidden, pick_matrix(index_ref, block, hidden.shape[1]))


def wide_kernel(hidden_ref, index_ref, p0, p1):
    hidden = hidden_ref[...]
    for block, picked_ref in ((0, p0), (1, p1)):
        picked_ref[...] = dot_nn(hidden, pick_matrix(index_ref, block, hidden.shape[1]))


def edge_tiles(senders_ref, radial_ref, edges_ref, skip_from, skip):
    slots, atoms = senders_ref.shape
    rows = 128
    lanes = 128
    row_ids = lax.broadcasted_iota(jnp.int32, (rows, lanes), 0).astype(f32).astype(bf16)

    def one_tile(tile, carry):
        first = pl.multiple_of(tile * rows, rows)
        sender = jnp.where(first >= skip_from, first + skip, first)
        for part in range(atoms // lanes):
            window = pl.ds(part * lanes, lanes)
            local = jnp.clip(senders_ref[:, window] - sender, -1, rows)
            local = local.astype(f32).astype(bf16)
            weight = radial_ref[:, window].astype(bf16)
            total = jnp.zeros((rows, lanes), bf16)
            for slot in range(slots):
                total = total + jnp.where(
                    row_ids == local[slot : slot + 1, :],
                    weight[slot : slot + 1, :],
                    jnp.zeros((), bf16),
                )
            edges_ref[pl.ds(first, rows), window] = total
        return carry

    lax.fori_loop(0, edges_ref.shape[0] // rows, one_tile, 0)


def far_edge_kernel(senders_ref, radial_ref, index_ref, hidden_ref, edges_ref, pick_ref, p0, p1):
    for block in (2, 3):
        pick_ref[block - 2] = pick_matrix(index_ref, block, senders_ref.shape[1])
    wide_kernel(hidden_ref, index_ref, p0, p1)
    edge_tiles(senders_ref, radial_ref, edges_ref, 0, senders_ref.shape[1])


def near_edge_kernel(senders_ref, radial_ref, edges_ref):
    atoms = senders_ref.shape[1]
    edge_tiles(senders_ref, radial_ref, edges_ref, atoms, edges_ref.shape[0] - atoms)


def near_kernel(layer, hidden_ref, g2, g3, edges_ref, self_ref, own_ref, gathered_ref):
    hidden = hidden_ref[...]
    atoms = hidden.shape[1]
    ghosts = g2.shape[1]
    own_ref[...] = dot_tn(self_ref[layer], hidden)
    gathered = dot_nn(hidden, edges_ref[0:atoms, :])
    gathered = gathered + dot_nn(g2[...].astype(bf16), edges_ref[atoms : atoms + ghosts, :])
    gathered_ref[...] = gathered + dot_nn(
        g3[...].astype(bf16), edges_ref[atoms + ghosts : atoms + 2 * ghosts, :]
    )


def interact(layer, hidden_ref, own_ref, gathered_ref, g0, g1, edges_ref, message_ref):
    hidden = hidden_ref[...]
    ghosts = g0.shape[1]
    gathered = gathered_ref[...]
    gathered = gathered + dot_nn(g0[...].astype(bf16), edges_ref[0:ghosts, :])
    gathered = gathered + dot_nn(g1[...].astype(bf16), edges_ref[ghosts : 2 * ghosts, :])
    high = gathered.astype(bf16)
    low = (gathered - high.astype(f32)).astype(bf16)
    message = message_ref[layer]
    total = own_ref[...] + dot_tn(message, high) + dot_tn(message, low)
    return (hidden.astype(f32) + total * (1.0 / (1.0 + jnp.exp(-total)))).astype(bf16)


def layer_kernel(
    layer, hidden_ref, own_ref, gathered_ref, g0, g1, edges_ref, message_ref, pick_ref, out_ref, p2, p3
):
    hidden = interact(layer, hidden_ref, own_ref, gathered_ref, g0, g1, edges_ref, message_ref)
    out_ref[...] = hidden
    p2[...] = dot_nn(hidden, pick_ref[0])
    p3[...] = dot_nn(hidden, pick_ref[1])


def half_windows(core):
    own = pl.ds(pl.multiple_of(core * half_rows, half_rows), half_rows)
    other = pl.ds(pl.multiple_of((1 - core) * half_rows, half_rows), half_rows)
    return own, other


def last_kernel(
    layer,
    hidden_ref,
    own_ref,
    gathered_ref,
    g0,
    g1,
    edges_ref,
    message_ref,
    readout_ref,
    count_ref,
    core_ref,
    real_ref,
    imag_ref,
    third_ref,
    send_ref,
    keep_ref,
    charges_ref,
    lattice_ref,
    sums_ref,
):
    hidden = interact(layer, hidden_ref, own_ref, gathered_ref, g0, g1, edges_ref, message_ref)
    atoms = hidden.shape[1]
    slot_ids = lax.broadcasted_iota(jnp.int32, (8, atoms), 1)
    charges = jnp.where(slot_ids < count_ref[0], dot_tn(readout_ref[...], hidden), 0.0)
    charges_ref[...] = charges
    cosine = third_ref[0:8, :]
    sine = third_ref[8:16, :]
    for c in range(4):
        lattice_ref[8 * c : 8 * c + 8, :] = charges[c : c + 1, :] * cosine
        lattice_ref[32 + 8 * c : 40 + 8 * c, :] = charges[c : c + 1, :] * sine
    with_cos = lattice_ref[0:32, :].astype(bf16)
    with_sin = lattice_ref[32:64, :].astype(bf16)
    none = jnp.zeros((64, atoms), bf16)
    real = real_ref[...]
    imag = imag_ref[...]
    sums_ref[0:grid_rows, :] = dot_nt(real, jnp.concatenate([with_cos, with_sin, none])) + dot_nt(
        imag, jnp.concatenate([none, with_sin, with_cos])
    )
    flat = charges.astype(bf16)
    flat_real = dot_nt(flat, real)
    flat_imag = dot_nt(flat, imag)
    sums_ref[grid_rows : grid_rows + 4, :] = flat_real[0:4, 0:128]
    sums_ref[grid_rows + 4 : grid_rows + 8, :] = flat_imag[0:4, 0:128]
    sums_ref[grid_rows + 8 :, :] = jnp.zeros((sums_ref.shape[0] - grid_rows - 8, 128), f32)
    sums_ref[grid_rows + 8 : grid_rows + 12, 0:8] = flat_real[0:4, 128:grid_rows]
    sums_ref[grid_rows + 12 : grid_rows + 16, 0:8] = flat_imag[0:4, 128:grid_rows]
    own, other = half_windows(core_ref[0])
    keep_ref[...] = sums_ref[own, :]
    send_ref[...] = sums_ref[other, :]


def wave_weight(m0, m1, m2, cell_ref):
    w0 = two_pi * m0 / cell_ref[0]
    w1 = two_pi * m1 / cell_ref[1]
    w2 = two_pi * m2 / cell_ref[2]
    squared = w0 * w0 + w1 * w1 + w2 * w2
    return jnp.exp(-0.5 * smearing * smearing * squared) / squared


def phase_kernel(fractions_ref, hidden_ref, index_ref, real_ref, imag_ref, third_ref, p0, p1):
    wide_kernel(hidden_ref, index_ref, p0, p1)
    atoms = fractions_ref.shape[1]
    orders = lax.broadcasted_iota(jnp.int32, (8, atoms), 0).astype(f32) + 1.0
    cosines, sines = [], []
    for axis in range(3):
        turns = orders * fractions_ref[axis : axis + 1, :]
        angle = two_pi * (turns - jnp.round(turns))
        cosines.append(jnp.cos(angle))
        sines.append(jnp.sin(angle))
    third_ref[0:8, :] = cosines[2]
    third_ref[8:16, :] = sines[2]
    for axis in range(3):
        third_ref[16 + axis : 17 + axis, :] = cosines[axis][0:1, :]
    c0, s0 = cosines[0], sines[0]
    for m in range(-kmax, kmax + 1):
        window = pl.ds((m + kmax) * kmax, kmax)
        if m == 0:
            re, im = c0, s0
        else:
            row = abs(m) - 1
            c1 = cosines[1][row : row + 1, :]
            s1 = sines[1][row : row + 1, :]
            if m < 0:
                s1 = -s1
            re, im = c0 * c1 - s0 * s1, s0 * c1 + c0 * s1
        real_ref[window, :] = re.astype(bf16)
        imag_ref[window, :] = im.astype(bf16)


def weight_kernel(cell_ref, numbers_ref, after_ref, factor_ref, flat_ref, acc, acc0):
    acc[...] = jnp.zeros_like(acc)
    acc0[...] = jnp.zeros_like(acc0)
    width = math.gcd(numbers_ref.shape[1], 1024)
    plane_ids = lax.broadcasted_iota(jnp.int32, (grid_rows, width), 0)
    third_ids = lax.broadcasted_iota(jnp.int32, (32, width), 0)
    third_ids = jnp.where(third_ids < 8, third_ids + 1, jnp.where(third_ids < 16, 7 - third_ids, 0))
    zero_row = lax.broadcasted_iota(jnp.int32, (32, width), 0) <= 16

    def count(step, carry):
        window = pl.ds(pl.multiple_of(step * width, width), width)
        numbers = numbers_ref[:, window]
        plane = (numbers[1:2, :] + kmax) * kmax + numbers[0:1, :] - 1
        in_plane = jnp.where(plane_ids == plane, 1.0, 0.0).astype(bf16)
        in_third = jnp.where((third_ids == numbers[2:3, :]) & zero_row, 1.0, 0.0).astype(bf16)
        acc[...] += dot_nt(in_plane, in_third)
        acc0[...] += dot_nt(in_third[16:32, :], in_plane)
        return carry

    lax.fori_loop(0, numbers_ref.shape[1] // width, count, 0)

    lane = lax.broadcasted_iota(jnp.int32, (grid_rows, 128), 1)
    row = lax.broadcasted_iota(jnp.int32, (grid_rows, 128), 0)
    m0 = (row % 8 + 1).astype(f32)
    m1 = (row // 8 - kmax).astype(f32)
    m2 = (lane % 8 + 1).astype(f32)
    weight = wave_weight(m0, m1, m2, cell_ref)
    from_ids = lax.broadcasted_iota(jnp.int32, (32, 128), 0)
    lane_ids = lax.broadcasted_iota(jnp.int32, (32, 128), 1) % 8
    expand_up = jnp.where(from_ids == lane_ids, 1.0, 0.0)
    expand_down = jnp.where(from_ids == lane_ids + 8, 1.0, 0.0)
    counts = acc[...]
    up = weight * jnp.dot(counts, expand_up, precision=highest, preferred_element_type=f32)
    down = weight * jnp.dot(counts, expand_down, precision=highest, preferred_element_type=f32)
    block = lane // 32
    first, second, third = block == 0, block == 1, block == 2
    factor_ref[0] = jnp.where(first, up, jnp.where(second, down, jnp.where(third, -up, -down)))
    factor_ref[1] = jnp.where(first, down, jnp.where(second, -up, jnp.where(third, -down, up)))
    factor_ref[2] = m2 * jnp.where(first, up, jnp.where(second, -down, jnp.where(third, -up, down)))
    factor_ref[3] = m2 * jnp.where(first, -down, jnp.where(second, -up, jnp.where(third, down, up)))
    lane0 = lax.broadcasted_iota(jnp.int32, (8, grid_rows), 1)
    n0 = (lane0 % 8 + 1).astype(f32)
    n1 = (lane0 // 8 - kmax).astype(f32)
    flat_ref[...] = wave_weight(n0, n1, 0.0 * n0, cell_ref) * acc0[0:1, :]


def force_kernel(
    scale,
    half_ref,
    other_ref,
    core_ref,
    charges_ref,
    lattice_ref,
    real_ref,
    imag_ref,
    third_ref,
    factor_ref,
    flat_ref,
    cell_ref,
    count_ref,
    forces_ref,
    born_ref,
    energy_ref,
    sums_ref,
    flat_sums,
):
    atoms = real_ref.shape[1]
    own, other = half_windows(core_ref[0])
    sums_ref[own, :] = half_ref[...]
    sums_ref[other, :] = other_ref[...]
    sums = sums_ref[0:grid_rows, :]
    swapped = pltpu.roll(sums, 64, 1)
    plus = pltpu.roll(sums + swapped, 32, 1)
    minus = pltpu.roll(sums - swapped, 32, 1)
    f0 = factor_ref[0]
    f1 = factor_ref[1]
    even = f0 * plus + f1 * minus
    odd = factor_ref[2] * plus + factor_ref[3] * minus
    row = lax.broadcasted_iota(jnp.int32, (grid_rows, 128), 0)
    m0 = (row % 8 + 1).astype(f32)
    m1 = (row // 8 - kmax).astype(f32)
    flat_sums[:, 0:128] = sums_ref[grid_rows : grid_rows + 8, :]
    flat_sums[:, 128:grid_rows] = sums_ref[grid_rows + 8 : grid_rows + 16, 0:8]
    flat_re = flat_sums[0:4, :]
    flat_im = flat_sums[4:8, :]
    flat_weight = flat_ref[0:4, :]
    part = jnp.sum(jnp.abs(f0) * plus * plus + jnp.abs(f1) * minus * minus, axis=0, keepdims=True)
    flat_part = jnp.sum(
        flat_weight * (flat_re * flat_re + flat_im * flat_im), axis=0, keepdims=True
    )
    energy_ref[...] = (0.5 * scale) * (
        0.5 * jnp.sum(part, axis=1, keepdims=True) + jnp.sum(flat_part, axis=1, keepdims=True)
    )

    lane0 = lax.broadcasted_iota(jnp.int32, (4, grid_rows), 1)
    n0 = (lane0 % 8 + 1).astype(f32)
    n1 = (lane0 // 8 - kmax).astype(f32)
    up = flat_weight * flat_im
    down = -flat_weight * flat_re
    flat_up = jnp.concatenate([up * n0, up * n1], axis=0).astype(bf16)
    flat_down = jnp.concatenate([down * n0, down * n1], axis=0).astype(bf16)
    real = real_ref[...]
    imag = imag_ref[...]
    tables = [jnp.transpose(t) for t in (even * m0, even * m1, odd)]
    with_real = jnp.concatenate([t[0:64] for t in tables], axis=0).astype(bf16)
    with_imag = jnp.concatenate([t[64:128] for t in tables], axis=0).astype(bf16)
    from_real = dot_nn(with_real, real)
    from_imag = dot_nn(with_imag, imag)
    flat = dot_nn(flat_up, real) + dot_nn(flat_down, imag)
    with_cos = lattice_ref[0:32, :]
    with_sin = lattice_ref[32:64, :]
    charges = charges_ref[...]
    alive = lax.broadcasted_iota(jnp.int32, (1, atoms), 1) < count_ref[0]
    total = jnp.sum(charges[0:4], axis=0, keepdims=True)
    for axis in range(3):
        base = 64 * axis
        terms = with_cos * (from_real[base : base + 32] + from_imag[base + 32 : base + 64])
        terms = terms + with_sin * (from_real[base + 32 : base + 64] + from_imag[base : base + 32])
        gradient = jnp.sum(terms, axis=0, keepdims=True)
        if axis < 2:
            gradient = gradient + jnp.sum(
                charges[0:4] * flat[4 * axis : 4 * axis + 4], axis=0, keepdims=True
            )
        forces_ref[axis : axis + 1, :] = jnp.where(
            alive, -(two_pi * scale / cell_ref[axis]) * gradient, 0.0
        )
        born_ref[axis : axis + 1, :] = jnp.where(
            alive, total * third_ref[16 + axis : 17 + axis, :], 0.0
        )


def call(kernel, outs, *args, smem=(), scratch=(), cost=None):
    specs = [
        pl.BlockSpec(memory_space=pltpu.SMEM if i in smem else pltpu.VMEM)
        for i in range(len(args))
    ]
    return pl.pallas_call(
        kernel,
        out_shape=[jax.ShapeDtypeStruct(shape, dtype) for shape, dtype in outs],
        in_specs=specs,
        out_specs=[pl.BlockSpec(memory_space=pltpu.VMEM)] * len(outs),
        scratch_shapes=list(scratch),
        compiler_params=params,
        cost_estimate=cost,
    )(*args)


def shifted(block, axis, step):
    count = lax.axis_size(axis)
    return lax.ppermute(block, axis, [(i, (i + step) % count) for i in range(count)])


def exchange_narrow(p2, p3):
    return shifted(p3, "narrow", 1), shifted(p2, "narrow", -1)


def exchange_wide(p0, p1):
    return shifted(p1, "wide", 1), shifted(p0, "wide", -1)


def flipped(block, axis, step):
    return lax.ppermute(block, axis, [(i, i ^ step) for i in range(lax.axis_size(axis))])


def summed(send, keep, beside):
    block = keep + flipped(send, "wide", 1)
    for axis, step in (("wide", 2), ("narrow", 1)):
        while step < lax.axis_size(axis):
            if axis == "narrow" and 2 * step >= lax.axis_size(axis):
                block, beside = lax.optimization_barrier((block, beside))
            block = block + flipped(block, axis, step)
            step *= 2
    return block, flipped(block, "wide", 1), beside


def per_device(
    fractions,
    cell_lengths,
    features,
    atom_counts,
    send_index,
    senders,
    radial,
    self_weight,
    message_weight,
    charge_weight,
    wave_numbers,
):
    atoms, width = features.shape
    ghosts = send_index.shape[1]
    rows = atoms + 4 * ghosts
    total_atoms = atoms * lax.axis_size("wide") * lax.axis_size("narrow")
    scale = 4.0 / math.sqrt(total_atoms * wave_numbers.shape[1])
    picked_outs = [((width, ghosts), f32)] * 2
    hidden_out = [((width, atoms), bf16)]
    sum_out = [((width, atoms), f32)]
    busy = pl.CostEstimate(flops=10**9, bytes_accessed=20 * 2**20, transcendentals=0)
    readout = jnp.pad(charge_weight, ((0, 0), (0, 8 - charge_weight.shape[1])))
    core = jnp.reshape(lax.axis_index("wide") % 2, (1,)).astype(jnp.int32)

    hidden, p2, p3 = call(
        first_kernel,
        hidden_out + picked_outs,
        features,
        send_index,
        cost=busy,
    )
    g2, g3 = exchange_narrow(p2, p3)
    far_edges, picks, p0, p1 = call(
        far_edge_kernel,
        [((2 * ghosts, atoms), bf16), ((2, atoms, ghosts), bf16)] + picked_outs,
        senders,
        radial,
        send_index,
        hidden,
        cost=busy,
    )
    g0, g1 = exchange_wide(p0, p1)
    (near_edges,) = call(
        near_edge_kernel, [((rows - 2 * ghosts, atoms), bf16)], senders, radial, cost=busy
    )
    layers = self_weight.shape[0]
    for layer in range(layers):
        own, gathered = call(
            functools.partial(near_kernel, layer), sum_out * 2, hidden, g2, g3, near_edges, self_weight
        )
        if layer == layers - 1:
            break
        hidden, p2, p3 = call(
            functools.partial(layer_kernel, layer),
            hidden_out + picked_outs,
            hidden,
            own,
            gathered,
            g0,
            g1,
            far_edges,
            message_weight,
            picks,
        )
        g2, g3 = exchange_narrow(p2, p3)
        real, imag, third, p0, p1 = call(
            phase_kernel,
            [((grid_rows, atoms), bf16), ((grid_rows, atoms), bf16), ((24, atoms), f32)]
            + picked_outs,
            fractions,
            hidden,
            send_index,
            cost=busy,
        )
        g0, g1 = exchange_wide(p0, p1)
    send, keep, charges, lattice = call(
        functools.partial(last_kernel, layers - 1),
        [((half_rows, 128), f32)] * 2 + [((8, atoms), f32), ((64, atoms), f32)],
        hidden,
        own,
        gathered,
        g0,
        g1,
        far_edges,
        message_weight,
        readout,
        atom_counts,
        core,
        real,
        imag,
        third,
        smem=(8, 9),
        scratch=[pltpu.VMEM((2 * half_rows, 128), f32)],
    )
    factor, flat = call(
        weight_kernel,
        [((4, grid_rows, 128), f32), ((8, grid_rows), f32)],
        cell_lengths,
        wave_numbers,
        send,
        smem=(0,),
        scratch=[pltpu.VMEM((grid_rows, 32), f32), pltpu.VMEM((16, grid_rows), f32)],
        cost=busy,
    )
    half, other, (factor, flat) = summed(send, keep, (factor, flat))
    forces, born_charges, energy = call(
        functools.partial(force_kernel, scale),
        [((3, atoms), f32), ((3, atoms), f32), ((1, 1), f32)],
        half,
        other,
        core,
        charges,
        lattice,
        real,
        imag,
        third,
        factor,
        flat,
        cell_lengths,
        atom_counts,
        smem=(2, 10, 11),
        scratch=[pltpu.VMEM((2 * half_rows, 128), f32), pltpu.VMEM((8, grid_rows), f32)],
    )
    return (forces, born_charges, energy[0, 0])


def solution(mesh):
    return jax.shard_map(
        per_device,
        mesh=mesh,
        in_specs=(
            P(None, ("wide", "narrow")),
            P(),
            P(("wide", "narrow"), None),
            P(("wide", "narrow")),
            P(("wide", "narrow"), None),
            P(None, ("wide", "narrow")),
            P(None, ("wide", "narrow")),
            P(),
            P(),
            P(),
            P(),
        ),
        out_specs=(P(None, ("wide", "narrow")), P(None, ("wide", "narrow")), P()),
        check_vma=False,
    )
```

```python
import functools
import math

import jax
import jax.numpy as jnp
from jax import lax
from jax.experimental import pallas as pl
from jax.experimental.pallas import tpu as pltpu
from jax.sharding import PartitionSpec as P

smearing = 0.5
two_pi = 2.0 * math.pi
kmax = 8
grid_rows = (2 * kmax + 1) * kmax
half_rows = 80
f32 = jnp.float32
bf16 = jnp.bfloat16
params = pltpu.CompilerParams(vmem_limit_bytes=48 * 1024 * 1024)


def dot_nn(a, b):
    return lax.dot_general(a, b, (((1,), (0,)), ((), ())), preferred_element_type=f32)


def dot_nt(a, b):
    return lax.dot_general(a, b, (((1,), (1,)), ((), ())), preferred_element_type=f32)


def pick_matrix(index_ref, block, atoms):
    row_ids = lax.broadcasted_iota(jnp.int32, (atoms, index_ref.shape[1]), 0)
    return jnp.where(row_ids == index_ref[block : block + 1, :], 1.0, 0.0).astype(bf16)


def first_kernel(features_ref, index_ref, hidden_ref, p2, p3):
    hidden = jnp.transpose(features_ref[...].astype(f32)).astype(bf16)
    hidden_ref[...] = hidden
    for block, picked_ref in ((2, p2), (3, p3)):
        picked_ref[...] = dot_nn(hidden, pick_matrix(index_ref, block, hidden.shape[1]))


def wide_kernel(hidden_ref, index_ref, p0, p1):
    hidden = hidden_ref[...]
    for block, picked_ref in ((0, p0), (1, p1)):
        picked_ref[...] = dot_nn(hidden, pick_matrix(index_ref, block, hidden.shape[1]))


def edge_tiles(senders_ref, radial_ref, edges_ref, skip_from, skip):
    slots, atoms = senders_ref.shape
    rows = 128
    lanes = 128
    row_ids = lax.broadcasted_iota(jnp.int32, (rows, lanes), 0).astype(f32).astype(bf16)

    def one_tile(tile, carry):
        first = pl.multiple_of(tile * rows, rows)
        sender = jnp.where(first >= skip_from, first + skip, first)
        for part in range(atoms // lanes):
            window = pl.ds(part * lanes, lanes)
            local = jnp.clip(senders_ref[:, window] - sender, -1, rows)
            local = local.astype(f32).astype(bf16)
            weight = radial_ref[:, window].astype(bf16)
            total = jnp.zeros((rows, lanes), bf16)
            for slot in range(slots):
                total = total + jnp.where(
                    row_ids == local[slot : slot + 1, :],
                    weight[slot : slot + 1, :],
                    jnp.zeros((), bf16),
                )
            edges_ref[pl.ds(first, rows), window] = total
        return carry

    lax.fori_loop(0, edges_ref.shape[0] // rows, one_tile, 0)


def far_edge_kernel(senders_ref, radial_ref, index_ref, hidden_ref, edges_ref, pick_ref, p0, p1):
    ghosts = index_ref.shape[1]
    for block in (2, 3):
        window = pl.ds((block - 2) * ghosts, ghosts)
        pick_ref[:, window] = pick_matrix(index_ref, block, senders_ref.shape[1])
    wide_kernel(hidden_ref, index_ref, p0, p1)
    edge_tiles(senders_ref, radial_ref, edges_ref, 0, senders_ref.shape[1])


def near_edge_kernel(
    senders_ref, radial_ref, self_ref, message_ref, edges_ref, self_rows_ref, message_rows_ref
):
    atoms = senders_ref.shape[1]
    edge_tiles(senders_ref, radial_ref, edges_ref, atoms, edges_ref.shape[0] - atoms)
    for layer in range(self_ref.shape[0]):
        self_rows_ref[layer] = jnp.transpose(self_ref[layer].astype(f32)).astype(bf16)
        message = jnp.transpose(message_ref[layer].astype(f32)).astype(bf16)
        message_rows_ref[layer] = jnp.concatenate([message, message], axis=1)


def near_kernel(layer, hidden_ref, g2, g3, edges_ref, self_rows_ref, own_ref, gathered_ref):
    hidden = hidden_ref[...]
    own_ref[...] = dot_nn(self_rows_ref[layer], hidden)
    known = jnp.concatenate([hidden, g2[...].astype(bf16), g3[...].astype(bf16)], axis=1)
    gathered_ref[...] = dot_nn(known, edges_ref[...])


def interact(layer, hidden_ref, own_ref, gathered_ref, g0, g1, edges_ref, message_rows_ref):
    received = jnp.concatenate([g0[...].astype(bf16), g1[...].astype(bf16)], axis=1)
    gathered = gathered_ref[...] + dot_nn(received, edges_ref[...])
    high = gathered.astype(bf16)
    low = (gathered - high.astype(f32)).astype(bf16)
    total = own_ref[...] + dot_nn(message_rows_ref[layer], jnp.concatenate([high, low], axis=0))
    gate = 0.5 * total * (1.0 + jnp.tanh(0.5 * total))
    return (hidden_ref[...].astype(f32) + gate).astype(bf16)


def layer_kernel(
    layer, hidden_ref, own_ref, gathered_ref, g0, g1, edges_ref, message_rows_ref, pick_ref, out_ref, p2, p3
):
    hidden = interact(layer, hidden_ref, own_ref, gathered_ref, g0, g1, edges_ref, message_rows_ref)
    out_ref[...] = hidden
    picked = dot_nn(hidden, pick_ref[...])
    ghosts = p2.shape[1]
    p2[...] = picked[:, 0:ghosts]
    p3[...] = picked[:, ghosts:]


def last_kernel(
    layer,
    hidden_ref,
    own_ref,
    gathered_ref,
    g0,
    g1,
    edges_ref,
    message_rows_ref,
    readout_ref,
    count_ref,
    phase_ref,
    third_ref,
    send_ref,
    keep_ref,
    lattice_ref,
):
    hidden = interact(layer, hidden_ref, own_ref, gathered_ref, g0, g1, edges_ref, message_rows_ref)
    atoms = hidden.shape[1]
    slot_ids = lax.broadcasted_iota(jnp.int32, (8, atoms), 1)
    readout = readout_ref[...].astype(f32)
    readout = jnp.concatenate([readout, jnp.zeros_like(readout)], axis=0).astype(bf16)
    charges = jnp.where(slot_ids < count_ref[...], dot_nn(readout, hidden), 0.0)
    cosine = third_ref[0:8, :]
    sine = third_ref[8:16, :]
    rows = [charges[c : c + 1, :] * cosine for c in range(4)]
    rows = rows + [charges[c : c + 1, :] * sine for c in range(4)]
    lattice = jnp.concatenate(rows + [charges], axis=0)
    lattice_ref[...] = lattice
    lattice = lattice.astype(bf16)
    core = lax.rem(lax.axis_index("wide"), 2)
    for out_ref, part in ((keep_ref, core), (send_ref, 1 - core)):
        phases = phase_ref[part]
        out_ref[0:72, :] = dot_nt(lattice, phases[0:128, :])
        out_ref[72:80, 0:72] = dot_nt(phases[128:grid_rows, :], lattice)
        out_ref[72:80, 72:128] = jnp.zeros((8, 56), f32)


def wave_weight(m0, m1, m2, cell_ref):
    w0 = two_pi * m0 / cell_ref[0]
    w1 = two_pi * m1 / cell_ref[1]
    w2 = two_pi * m2 / cell_ref[2]
    squared = w0 * w0 + w1 * w1 + w2 * w2
    return jnp.exp(-0.5 * smearing * smearing * squared) / squared


def phase_kernel(fractions_ref, hidden_ref, index_ref, phase_ref, third_ref, p0, p1):
    wide_kernel(hidden_ref, index_ref, p0, p1)
    atoms = fractions_ref.shape[1]
    orders = lax.broadcasted_iota(jnp.int32, (8, atoms), 0).astype(f32) + 1.0
    cosines, sines = [], []
    for axis in range(3):
        turns = orders * fractions_ref[axis : axis + 1, :]
        angle = two_pi * (turns - jnp.round(turns))
        cosines.append(jnp.cos(angle))
        sines.append(jnp.sin(angle))
    third_ref[0:8, :] = cosines[2]
    third_ref[8:16, :] = sines[2]
    for axis in range(3):
        third_ref[16 + axis : 17 + axis, :] = cosines[axis][0:1, :]
    c0, s0 = cosines[0], sines[0]
    for m in range(-kmax, kmax + 1):
        window = pl.ds((m + kmax) * kmax, kmax)
        if m == 0:
            re, im = c0, s0
        else:
            row = abs(m) - 1
            c1 = cosines[1][row : row + 1, :]
            s1 = sines[1][row : row + 1, :]
            if m < 0:
                s1 = -s1
            re, im = c0 * c1 - s0 * s1, s0 * c1 + c0 * s1
        phase_ref[0, window, :] = re.astype(bf16)
        phase_ref[1, window, :] = im.astype(bf16)


def weight_kernel(cell_ref, numbers_ref, lattice_ref, third_ref, weight_ref, born_ref, acc):
    total = jnp.sum(lattice_ref[64:68, :], axis=0, keepdims=True)
    born_ref[...] = total * third_ref[16:19, :]
    acc[...] = jnp.zeros_like(acc)
    width = math.gcd(numbers_ref.shape[1], 1024)
    plane_ids = lax.broadcasted_iota(jnp.int32, (grid_rows, width), 0)
    third_ids = lax.broadcasted_iota(jnp.int32, (32, width), 0)
    third_ids = jnp.where(
        third_ids < 8, third_ids + 1, jnp.where(third_ids < 16, 7 - third_ids, (third_ids - 16) * 64)
    )

    def count(step, carry):
        window = pl.ds(pl.multiple_of(step * width, width), width)
        numbers = numbers_ref[:, window]
        plane = (numbers[1:2, :] + kmax) * kmax + numbers[0:1, :] - 1
        in_plane = jnp.where(plane_ids == plane, 1.0, 0.0).astype(bf16)
        in_third = jnp.where(third_ids == numbers[2:3, :], 1.0, 0.0).astype(bf16)
        acc[...] += dot_nt(in_third, in_plane)
        return carry

    lax.fori_loop(0, numbers_ref.shape[1] // width, count, 0)
    lane = lax.broadcasted_iota(jnp.int32, (8, grid_rows), 1)
    m0 = (lane % 8 + 1).astype(f32)
    m1 = (lane // 8 - kmax).astype(f32)
    m2 = lax.broadcasted_iota(jnp.int32, (8, grid_rows), 0).astype(f32) + 1.0
    weight = wave_weight(m0, m1, m2, cell_ref)
    up = weight * acc[0:8, :]
    down = weight * acc[8:16, :]
    flat = wave_weight(m0, m1, 0.0 * m0, cell_ref) * acc[16:17, :]
    for c in range(4):
        weight_ref[8 * c : 8 * c + 8, :] = up
        weight_ref[32 + 8 * c : 40 + 8 * c, :] = down
    weight_ref[64:72, :] = flat


def force_kernel(
    scale,
    half_ref,
    other_ref,
    lattice_ref,
    phase_ref,
    weight_ref,
    cell_ref,
    count_ref,
    forces_ref,
    energy_ref,
    sums_ref,
):
    atoms = lattice_ref.shape[1]
    core = lax.rem(lax.axis_index("wide"), 2)
    for part_ref, part in ((half_ref, core), (other_ref, 1 - core)):
        sums_ref[part, :, 0:128] = part_ref[0:72, :]
        sums_ref[part, :, 128:grid_rows] = jnp.transpose(part_ref[72:80, :])[0:72, :]
    real = sums_ref[0]
    imag = sums_ref[1]
    real_cos, real_sin, real_flat = real[0:32], real[32:64], real[64:72]
    imag_cos, imag_sin, imag_flat = imag[0:32], imag[32:64], imag[64:72]
    weight_up = weight_ref[0:32, :]
    weight_down = weight_ref[32:64, :]
    weight_flat = weight_ref[64:72, :]
    up_re, up_im = real_cos - imag_sin, imag_cos + real_sin
    down_re, down_im = real_cos + imag_sin, imag_cos - real_sin
    up_im_w, up_re_w = weight_up * up_im, weight_up * up_re
    down_im_w, down_re_w = weight_down * down_im, weight_down * down_re
    flat_im_w, flat_re_w = weight_flat * imag_flat, weight_flat * real_flat
    power = up_im_w * up_im + up_re_w * up_re + down_im_w * down_im + down_re_w * down_re
    flat_power = flat_im_w * imag_flat + flat_re_w * real_flat
    power = jnp.sum(power, axis=0, keepdims=True) + jnp.sum(flat_power, axis=0, keepdims=True)
    energy_ref[...] = (0.5 * scale) * jnp.sum(power, axis=1, keepdims=True)

    im_sum, im_diff = up_im_w + down_im_w, up_im_w - down_im_w
    re_sum, re_diff = up_re_w + down_re_w, down_re_w - up_re_w
    even_real = jnp.concatenate([im_sum, re_diff, flat_im_w], axis=0)
    even_imag = jnp.concatenate([-re_sum, -im_diff, -flat_re_w], axis=0)
    m2 = (lax.broadcasted_iota(jnp.int32, (32, grid_rows), 0) % 8 + 1).astype(f32)
    odd_real = jnp.concatenate([m2 * im_diff, -m2 * re_sum], axis=0)
    odd_imag = jnp.concatenate([m2 * re_diff, -m2 * im_sum], axis=0)
    lane = lax.broadcasted_iota(jnp.int32, (72, grid_rows), 1)
    m0 = (lane % 8 + 1).astype(f32)
    m1 = (lane // 8 - kmax).astype(f32)
    with_real = jnp.concatenate([even_real * m0, even_real * m1, odd_real], axis=0).astype(bf16)
    with_imag = jnp.concatenate([even_imag * m0, even_imag * m1, odd_imag], axis=0).astype(bf16)
    back = dot_nn(with_real, phase_ref[0]) + dot_nn(with_imag, phase_ref[1])
    lattice = lattice_ref[...]
    alive = lax.broadcasted_iota(jnp.int32, (1, atoms), 1) < count_ref[...]
    for axis in range(3):
        rows = 64 if axis == 2 else 72
        terms = lattice[0:rows] * back[72 * axis : 72 * axis + rows]
        gradient = jnp.sum(terms, axis=0, keepdims=True)
        forces_ref[axis : axis + 1, :] = jnp.where(
            alive, -(two_pi * scale / cell_ref[axis]) * gradient, 0.0
        )


def call(kernel, outs, *args, smem=(), scratch=(), cost=None):
    specs = [
        pl.BlockSpec(memory_space=pltpu.SMEM if i in smem else pltpu.VMEM)
        for i in range(len(args))
    ]
    return pl.pallas_call(
        kernel,
        out_shape=[jax.ShapeDtypeStruct(shape, dtype) for shape, dtype in outs],
        in_specs=specs,
        out_specs=[pl.BlockSpec(memory_space=pltpu.VMEM)] * len(outs),
        scratch_shapes=list(scratch),
        compiler_params=params,
        cost_estimate=cost,
    )(*args)


def shifted(block, axis, step):
    count = lax.axis_size(axis)
    return lax.ppermute(block, axis, [(i, (i + step) % count) for i in range(count)])


def exchange_narrow(p2, p3):
    return shifted(p3, "narrow", 1), shifted(p2, "narrow", -1)


def exchange_wide(p0, p1):
    return shifted(p1, "wide", 1), shifted(p0, "wide", -1)


def flipped(block, axis, step):
    return lax.ppermute(block, axis, [(i, i ^ step) for i in range(lax.axis_size(axis))])


def summed(send, keep, beside):
    block = keep + flipped(send, "wide", 1)
    for axis, step in (("wide", 2), ("narrow", 1)):
        while step < lax.axis_size(axis):
            if axis == "narrow" and 2 * step >= lax.axis_size(axis):
                block, beside = lax.optimization_barrier((block, beside))
            block = block + flipped(block, axis, step)
            step *= 2
    return block, flipped(block, "wide", 1), beside


def per_device(
    fractions,
    cell_lengths,
    features,
    atom_counts,
    send_index,
    senders,
    radial,
    self_weight,
    message_weight,
    charge_weight,
    wave_numbers,
):
    atoms, width = features.shape
    ghosts = send_index.shape[1]
    rows = atoms + 4 * ghosts
    total_atoms = atoms * lax.axis_size("wide") * lax.axis_size("narrow")
    scale = 4.0 / math.sqrt(total_atoms * wave_numbers.shape[1])
    picked_outs = [((width, ghosts), f32)] * 2
    hidden_out = [((width, atoms), bf16)]
    sum_out = [((width, atoms), f32)]
    busy = pl.CostEstimate(flops=10**9, bytes_accessed=20 * 2**20, transcendentals=0)
    readout = charge_weight.T
    counts = atom_counts.reshape(1, 1)

    hidden, p2, p3 = call(
        first_kernel,
        hidden_out + picked_outs,
        features,
        send_index,
        cost=busy,
    )
    g2, g3 = exchange_narrow(p2, p3)
    far_edges, picks, p0, p1 = call(
        far_edge_kernel,
        [((2 * ghosts, atoms), bf16), ((atoms, 2 * ghosts), bf16)] + picked_outs,
        senders,
        radial,
        send_index,
        hidden,
        cost=busy,
    )
    g0, g1 = exchange_wide(p0, p1)
    layers = self_weight.shape[0]
    near_edges, self_rows, message_rows = call(
        near_edge_kernel,
        [
            ((rows - 2 * ghosts, atoms), bf16),
            ((layers, width, width), bf16),
            ((layers, width, 2 * width), bf16),
        ],
        senders,
        radial,
        self_weight,
        message_weight,
        cost=busy,
    )
    for layer in range(layers):
        own, gathered = call(
            functools.partial(near_kernel, layer), sum_out * 2, hidden, g2, g3, near_edges, self_rows
        )
        if layer == layers - 1:
            break
        hidden, p2, p3 = call(
            functools.partial(layer_kernel, layer),
            hidden_out + picked_outs,
            hidden,
            own,
            gathered,
            g0,
            g1,
            far_edges,
            message_rows,
            picks,
            cost=busy,
        )
        g2, g3 = exchange_narrow(p2, p3)
        phases, third, p0, p1 = call(
            phase_kernel,
            [((2, grid_rows, atoms), bf16), ((24, atoms), f32)] + picked_outs,
            fractions,
            hidden,
            send_index,
            cost=busy,
        )
        g0, g1 = exchange_wide(p0, p1)
    send, keep, lattice = call(
        functools.partial(last_kernel, layers - 1),
        [((half_rows, 128), f32)] * 2 + [((72, atoms), f32)],
        hidden,
        own,
        gathered,
        g0,
        g1,
        far_edges,
        message_rows,
        readout,
        counts,
        phases,
        third,
    )
    weights, born_charges = call(
        weight_kernel,
        [((72, grid_rows), f32), ((3, atoms), f32)],
        cell_lengths,
        wave_numbers,
        lattice,
        third,
        smem=(0,),
        scratch=[pltpu.VMEM((32, grid_rows), f32)],
        cost=busy,
    )
    half, other, weights = summed(send, keep, weights)
    forces, energy = call(
        functools.partial(force_kernel, scale),
        [((3, atoms), f32), ((1, 1), f32)],
        half,
        other,
        lattice,
        phases,
        weights,
        cell_lengths,
        counts,
        smem=(5,),
        scratch=[pltpu.VMEM((2, 72, grid_rows), f32)],
    )
    return (forces, born_charges, energy[0, 0])


def solution(mesh):
    return jax.shard_map(
        per_device,
        mesh=mesh,
        in_specs=(
            P(None, ("wide", "narrow")),
            P(),
            P(("wide", "narrow"), None),
            P(("wide", "narrow")),
            P(("wide", "narrow"), None),
            P(None, ("wide", "narrow")),
            P(None, ("wide", "narrow")),
            P(),
            P(),
            P(),
            P(),
        ),
        out_specs=(P(None, ("wide", "narrow")), P(None, ("wide", "narrow")), P()),
        check_vma=False,
    )
```

```python
import functools
import math

import jax
import jax.numpy as jnp
from jax import lax
from jax.experimental import pallas as pl
from jax.experimental.pallas import tpu as pltpu
from jax.sharding import PartitionSpec as P

smearing = 0.5
two_pi = 2.0 * math.pi
kmax = 8
grid_rows = (2 * kmax + 1) * kmax
half_rows = 80
f32 = jnp.float32
bf16 = jnp.bfloat16
params = pltpu.CompilerParams(vmem_limit_bytes=48 * 1024 * 1024)


def dot_nn(a, b):
    return lax.dot_general(a, b, (((1,), (0,)), ((), ())), preferred_element_type=f32)


def dot_nt(a, b):
    return lax.dot_general(a, b, (((1,), (1,)), ((), ())), preferred_element_type=f32)


def parity(axis):
    return lax.rem(lax.axis_index(axis), 2)


def block_order(axis):
    odd = parity(axis)
    first = 0 if axis == "wide" else 2
    return first + odd, first + 1 - odd


def pick_matrix(index_ref, block, atoms):
    row_ids = lax.broadcasted_iota(jnp.int32, (atoms, index_ref.shape[1]), 0)
    return jnp.where(row_ids == index_ref[pl.ds(block, 1), :], 1.0, 0.0).astype(bf16)


def opening_kernel(opened_ref):
    opened_ref[...] = jnp.zeros(opened_ref.shape, f32)


def first_kernel(opened_ref, features_ref, index_ref, hidden_ref, pa, pb):
    hidden = jnp.transpose(features_ref[...].astype(f32)).astype(bf16)
    hidden_ref[...] = hidden
    for block, picked_ref in zip(block_order("narrow"), (pa, pb)):
        picked_ref[...] = dot_nn(hidden, pick_matrix(index_ref, block, hidden.shape[1]))


def wide_kernel(hidden_ref, index_ref, pa, pb):
    hidden = hidden_ref[...]
    for block, picked_ref in zip(block_order("wide"), (pa, pb)):
        picked_ref[...] = dot_nn(hidden, pick_matrix(index_ref, block, hidden.shape[1]))


def edge_tiles(senders_ref, radial_ref, edges_ref, local, axis):
    slots, atoms = senders_ref.shape
    rows = 128
    lanes = 128
    row_ids = lax.broadcasted_iota(jnp.int32, (rows, lanes), 0).astype(f32).astype(bf16)
    ghosts = (edges_ref.shape[0] - local) // 2
    one, two = block_order(axis)
    skip_one = atoms + one * ghosts - local
    skip_two = atoms + two * ghosts - local - ghosts

    def one_tile(tile, carry):
        first = pl.multiple_of(tile * rows, rows)
        skip = jnp.where(first < local, 0, jnp.where(first < local + ghosts, skip_one, skip_two))
        sender = first + skip
        for part in range(atoms // lanes):
            window = pl.ds(part * lanes, lanes)
            local_row = jnp.clip(senders_ref[:, window] - sender, -1, rows)
            local_row = local_row.astype(f32).astype(bf16)
            weight = radial_ref[:, window].astype(bf16)
            total = jnp.zeros((rows, lanes), bf16)
            for slot in range(slots):
                total = total + jnp.where(
                    row_ids == local_row[slot : slot + 1, :],
                    weight[slot : slot + 1, :],
                    jnp.zeros((), bf16),
                )
            edges_ref[pl.ds(first, rows), window] = total
        return carry

    lax.fori_loop(0, edges_ref.shape[0] // rows, one_tile, 0)


def far_edge_kernel(senders_ref, radial_ref, index_ref, hidden_ref, edges_ref, pick_ref, pa, pb):
    wide_kernel(hidden_ref, index_ref, pa, pb)
    ghosts = index_ref.shape[1]
    for i, block in enumerate(block_order("narrow")):
        pick_ref[:, i * ghosts : (i + 1) * ghosts] = pick_matrix(
            index_ref, block, senders_ref.shape[1]
        )
    edge_tiles(senders_ref, radial_ref, edges_ref, 0, "wide")


def near_edge_kernel(
    senders_ref, radial_ref, self_ref, message_ref, edges_ref, self_rows_ref, message_rows_ref
):
    edge_tiles(senders_ref, radial_ref, edges_ref, senders_ref.shape[1], "narrow")
    for layer in range(self_ref.shape[0]):
        self_rows_ref[layer] = jnp.transpose(self_ref[layer].astype(f32)).astype(bf16)
        message = jnp.transpose(message_ref[layer].astype(f32)).astype(bf16)
        message_rows_ref[layer] = jnp.concatenate([message, message], axis=1)


def local_kernel(layer, hidden_ref, edges_ref, self_rows_ref, own_ref, gathered_ref):
    hidden = hidden_ref[...]
    own_ref[...] = dot_nn(self_rows_ref[layer], hidden)
    gathered_ref[...] = dot_nn(hidden, edges_ref[0 : hidden.shape[1], :])


def near_kernel(gathered_ref, g2, g3, edges_ref, sum_ref):
    received = jnp.concatenate([g2[...].astype(bf16), g3[...].astype(bf16)], axis=1)
    local = edges_ref.shape[0] - received.shape[1]
    sum_ref[...] = gathered_ref[...] + dot_nn(received, edges_ref[local:, :])


def interact(layer, hidden_ref, own_ref, gathered_ref, g0, g1, edges_ref, message_rows_ref):
    received = jnp.concatenate([g0[...].astype(bf16), g1[...].astype(bf16)], axis=1)
    gathered = gathered_ref[...] + dot_nn(received, edges_ref[...])
    high = gathered.astype(bf16)
    low = (gathered - high.astype(f32)).astype(bf16)
    total = own_ref[...] + dot_nn(message_rows_ref[layer], jnp.concatenate([high, low], axis=0))
    gate = 0.5 * total * (1.0 + jnp.tanh(0.5 * total))
    return (hidden_ref[...].astype(f32) + gate).astype(bf16)


def layer_kernel(
    layer, hidden_ref, own_ref, gathered_ref, g0, g1, edges_ref, message_rows_ref, pick_ref, out_ref, p2, p3
):
    hidden = interact(layer, hidden_ref, own_ref, gathered_ref, g0, g1, edges_ref, message_rows_ref)
    out_ref[...] = hidden
    picked = dot_nn(hidden, pick_ref[...])
    ghosts = p2.shape[1]
    p2[...] = picked[:, 0:ghosts]
    p3[...] = picked[:, ghosts:]


def last_kernel(
    layer,
    hidden_ref,
    own_ref,
    gathered_ref,
    g0,
    g1,
    edges_ref,
    message_rows_ref,
    readout_ref,
    count_ref,
    phase_ref,
    third_ref,
    send_ref,
    keep_ref,
    lattice_ref,
):
    hidden = interact(layer, hidden_ref, own_ref, gathered_ref, g0, g1, edges_ref, message_rows_ref)
    atoms = hidden.shape[1]
    slot_ids = lax.broadcasted_iota(jnp.int32, (8, atoms), 1)
    readout = readout_ref[...].astype(f32)
    readout = jnp.concatenate([readout, jnp.zeros_like(readout)], axis=0).astype(bf16)
    charges = jnp.where(slot_ids < count_ref[...], dot_nn(readout, hidden), 0.0)
    cosine = third_ref[0:8, :]
    sine = third_ref[8:16, :]
    rows = [charges[c : c + 1, :] * cosine for c in range(4)]
    rows = rows + [charges[c : c + 1, :] * sine for c in range(4)]
    lattice = jnp.concatenate(rows + [charges], axis=0)
    lattice_ref[...] = lattice
    lattice = lattice.astype(bf16)
    core = parity("wide")
    for out_ref, part in ((keep_ref, core), (send_ref, 1 - core)):
        phases = phase_ref[part]
        out_ref[0:72, :] = dot_nt(lattice, phases[0:128, :])
        out_ref[72:80, 0:72] = dot_nt(phases[128:grid_rows, :], lattice)
        out_ref[72:80, 72:128] = jnp.zeros((8, 56), f32)


def wave_weight(m0, m1, m2, cell_ref):
    w0 = two_pi * m0 / cell_ref[0]
    w1 = two_pi * m1 / cell_ref[1]
    w2 = two_pi * m2 / cell_ref[2]
    squared = w0 * w0 + w1 * w1 + w2 * w2
    return jnp.exp(-0.5 * smearing * smearing * squared) / squared


def phase_kernel(fractions_ref, hidden_ref, index_ref, phase_ref, third_ref, p0, p1):
    wide_kernel(hidden_ref, index_ref, p0, p1)
    atoms = fractions_ref.shape[1]
    orders = lax.broadcasted_iota(jnp.int32, (8, atoms), 0).astype(f32) + 1.0
    cosines, sines = [], []
    for axis in range(3):
        turns = orders * fractions_ref[axis : axis + 1, :]
        angle = two_pi * (turns - jnp.round(turns))
        cosines.append(jnp.cos(angle))
        sines.append(jnp.sin(angle))
    third_ref[0:8, :] = cosines[2]
    third_ref[8:16, :] = sines[2]
    for axis in range(3):
        third_ref[16 + axis : 17 + axis, :] = cosines[axis][0:1, :]
    c0, s0 = cosines[0], sines[0]
    for m in range(-kmax, kmax + 1):
        window = pl.ds((m + kmax) * kmax, kmax)
        if m == 0:
            re, im = c0, s0
        else:
            row = abs(m) - 1
            c1 = cosines[1][row : row + 1, :]
            s1 = sines[1][row : row + 1, :]
            if m < 0:
                s1 = -s1
            re, im = c0 * c1 - s0 * s1, s0 * c1 + c0 * s1
        phase_ref[0, window, :] = re.astype(bf16)
        phase_ref[1, window, :] = im.astype(bf16)


def weight_kernel(
    scale,
    cell_ref,
    numbers_ref,
    lattice_ref,
    third_ref,
    count_ref,
    weight_ref,
    factor_ref,
    born_ref,
    acc,
):
    alive = lax.broadcasted_iota(jnp.int32, (1, lattice_ref.shape[1]), 1) < count_ref[...]
    for axis in range(3):
        factor_ref[axis : axis + 1, :] = jnp.where(alive, -(two_pi * scale / cell_ref[axis]), 0.0)
    total = jnp.sum(lattice_ref[64:68, :], axis=0, keepdims=True)
    born_ref[...] = total * third_ref[16:19, :]
    acc[...] = jnp.zeros_like(acc)
    width = math.gcd(numbers_ref.shape[1], 1024)
    plane_ids = lax.broadcasted_iota(jnp.int32, (grid_rows, width), 0)
    third_ids = lax.broadcasted_iota(jnp.int32, (32, width), 0)
    third_ids = jnp.where(
        third_ids < 8, third_ids + 1, jnp.where(third_ids < 16, 7 - third_ids, (third_ids - 16) * 64)
    )

    def count(step, carry):
        window = pl.ds(pl.multiple_of(step * width, width), width)
        numbers = numbers_ref[:, window]
        plane = (numbers[1:2, :] + kmax) * kmax + numbers[0:1, :] - 1
        in_plane = jnp.where(plane_ids == plane, 1.0, 0.0).astype(bf16)
        in_third = jnp.where(third_ids == numbers[2:3, :], 1.0, 0.0).astype(bf16)
        acc[...] += dot_nt(in_third, in_plane)
        return carry

    lax.fori_loop(0, numbers_ref.shape[1] // width, count, 0)
    lane = lax.broadcasted_iota(jnp.int32, (8, grid_rows), 1)
    m0 = (lane % 8 + 1).astype(f32)
    m1 = (lane // 8 - kmax).astype(f32)
    m2 = lax.broadcasted_iota(jnp.int32, (8, grid_rows), 0).astype(f32) + 1.0
    weight = wave_weight(m0, m1, m2, cell_ref)
    up = weight * acc[0:8, :]
    down = weight * acc[8:16, :]
    flat = wave_weight(m0, m1, 0.0 * m0, cell_ref) * acc[16:17, :]
    for c in range(4):
        weight_ref[8 * c : 8 * c + 8, :] = up
        weight_ref[32 + 8 * c : 40 + 8 * c, :] = down
    weight_ref[64:72, :] = flat


def force_kernel(
    scale,
    half_ref,
    other_ref,
    lattice_ref,
    phase_ref,
    weight_ref,
    factor_ref,
    forces_ref,
    energy_ref,
    sums_ref,
):
    core = parity("wide")
    for part_ref, part in ((half_ref, core), (other_ref, 1 - core)):
        sums_ref[part, :, 0:128] = part_ref[0:72, :]
        sums_ref[part, :, 128:grid_rows] = jnp.transpose(part_ref[72:80, :])[0:72, :]
    real = sums_ref[0]
    imag = sums_ref[1]
    real_cos, real_sin, real_flat = real[0:32], real[32:64], real[64:72]
    imag_cos, imag_sin, imag_flat = imag[0:32], imag[32:64], imag[64:72]
    weight_up = weight_ref[0:32, :]
    weight_down = weight_ref[32:64, :]
    weight_flat = weight_ref[64:72, :]
    up_re, up_im = real_cos - imag_sin, imag_cos + real_sin
    down_re, down_im = real_cos + imag_sin, imag_cos - real_sin
    up_im_w, up_re_w = weight_up * up_im, weight_up * up_re
    down_im_w, down_re_w = weight_down * down_im, weight_down * down_re
    flat_im_w, flat_re_w = weight_flat * imag_flat, weight_flat * real_flat
    power = up_im_w * up_im + up_re_w * up_re + down_im_w * down_im + down_re_w * down_re
    flat_power = flat_im_w * imag_flat + flat_re_w * real_flat
    power = jnp.sum(power, axis=0, keepdims=True) + jnp.sum(flat_power, axis=0, keepdims=True)
    energy_ref[...] = (0.5 * scale) * jnp.sum(power, axis=1, keepdims=True)

    im_sum, im_diff = up_im_w + down_im_w, up_im_w - down_im_w
    re_sum, re_diff = up_re_w + down_re_w, down_re_w - up_re_w
    even_real = jnp.concatenate([im_sum, re_diff, flat_im_w], axis=0)
    even_imag = jnp.concatenate([-re_sum, -im_diff, -flat_re_w], axis=0)
    m2 = (lax.broadcasted_iota(jnp.int32, (32, grid_rows), 0) % 8 + 1).astype(f32)
    odd_real = jnp.concatenate([m2 * im_diff, -m2 * re_sum], axis=0)
    odd_imag = jnp.concatenate([m2 * re_diff, -m2 * im_sum], axis=0)
    lane = lax.broadcasted_iota(jnp.int32, (72, grid_rows), 1)
    m0 = (lane % 8 + 1).astype(f32)
    m1 = (lane // 8 - kmax).astype(f32)
    with_real = jnp.concatenate([even_real * m0, even_real * m1, odd_real], axis=0).astype(bf16)
    with_imag = jnp.concatenate([even_imag * m0, even_imag * m1, odd_imag], axis=0).astype(bf16)
    back = dot_nn(with_real, phase_ref[0]) + dot_nn(with_imag, phase_ref[1])
    lattice = lattice_ref[...]
    for axis in range(3):
        rows = 64 if axis == 2 else 72
        terms = lattice[0:rows] * back[72 * axis : 72 * axis + rows]
        gradient = jnp.sum(terms, axis=0, keepdims=True)
        forces_ref[axis : axis + 1, :] = factor_ref[axis : axis + 1, :] * gradient


def call(kernel, outs, *args, smem=(), scratch=(), cost=None):
    specs = [
        pl.BlockSpec(memory_space=pltpu.SMEM if i in smem else pltpu.VMEM)
        for i in range(len(args))
    ]
    return pl.pallas_call(
        kernel,
        out_shape=[jax.ShapeDtypeStruct(shape, dtype) for shape, dtype in outs],
        in_specs=specs,
        out_specs=[pl.BlockSpec(memory_space=pltpu.VMEM)] * len(outs),
        scratch_shapes=list(scratch),
        compiler_params=params,
        cost_estimate=cost,
    )(*args)


def matched(first, second, axis):
    count = lax.axis_size(axis)
    ways = (-1, 1)
    one = lax.ppermute(first, axis, [(i, (i + ways[i % 2]) % count) for i in range(count)])
    two = lax.ppermute(second, axis, [(i, (i - ways[i % 2]) % count) for i in range(count)])
    return one, two


def flipped(block, axis, step):
    return lax.ppermute(block, axis, [(i, i ^ step) for i in range(lax.axis_size(axis))])


def summed(send, keep, beside):
    block = keep + flipped(send, "wide", 1)
    for axis, step in (("wide", 2), ("narrow", 1)):
        while step < lax.axis_size(axis):
            if axis == "narrow" and 2 * step >= lax.axis_size(axis):
                block, beside = lax.optimization_barrier((block, beside))
            block = block + flipped(block, axis, step)
            step *= 2
    return block, flipped(block, "wide", 1), beside


def per_device(
    fractions,
    cell_lengths,
    features,
    atom_counts,
    send_index,
    senders,
    radial,
    self_weight,
    message_weight,
    charge_weight,
    wave_numbers,
):
    atoms, width = features.shape
    ghosts = send_index.shape[1]
    rows = atoms + 4 * ghosts
    total_atoms = atoms * lax.axis_size("wide") * lax.axis_size("narrow")
    scale = 4.0 / math.sqrt(total_atoms * wave_numbers.shape[1])
    picked_outs = [((width, ghosts), f32)] * 2
    hidden_out = [((width, atoms), bf16)]
    sum_out = [((width, atoms), f32)]
    busy = pl.CostEstimate(flops=10**9, bytes_accessed=20 * 2**20, transcendentals=0)
    readout = charge_weight.T
    counts = atom_counts.reshape(1, 1)

    (opened,) = call(opening_kernel, [((8, 128), f32)], cost=busy)
    hidden, p2, p3 = call(
        first_kernel,
        hidden_out + picked_outs,
        opened,
        features,
        send_index,
        cost=busy,
    )
    g2, g3 = matched(p2, p3, "narrow")
    far_edges, picks, p0, p1 = call(
        far_edge_kernel,
        [((2 * ghosts, atoms), bf16), ((atoms, 2 * ghosts), bf16)] + picked_outs,
        senders,
        radial,
        send_index,
        hidden,
        cost=busy,
    )
    g0, g1 = matched(p0, p1, "wide")
    layers = self_weight.shape[0]
    near_edges, self_rows, message_rows = call(
        near_edge_kernel,
        [
            ((rows - 2 * ghosts, atoms), bf16),
            ((layers, width, width), bf16),
            ((layers, width, 2 * width), bf16),
        ],
        senders,
        radial,
        self_weight,
        message_weight,
        cost=busy,
    )
    for layer in range(layers):
        own, gathered = call(
            functools.partial(local_kernel, layer), sum_out * 2, hidden, near_edges, self_rows, cost=busy
        )
        (gathered,) = call(near_kernel, sum_out, gathered, g2, g3, near_edges)
        if layer == layers - 1:
            break
        hidden, p2, p3 = call(
            functools.partial(layer_kernel, layer),
            hidden_out + picked_outs,
            hidden,
            own,
            gathered,
            g0,
            g1,
            far_edges,
            message_rows,
            picks,
            cost=busy,
        )
        g2, g3 = matched(p2, p3, "narrow")
        phases, third, p0, p1 = call(
            phase_kernel,
            [((2, grid_rows, atoms), bf16), ((24, atoms), f32)] + picked_outs,
            fractions,
            hidden,
            send_index,
            cost=busy,
        )
        g0, g1 = matched(p0, p1, "wide")
    send, keep, lattice = call(
        functools.partial(last_kernel, layers - 1),
        [((half_rows, 128), f32)] * 2 + [((72, atoms), f32)],
        hidden,
        own,
        gathered,
        g0,
        g1,
        far_edges,
        message_rows,
        readout,
        counts,
        phases,
        third,
    )
    weights, factor, born_charges = call(
        functools.partial(weight_kernel, scale),
        [((72, grid_rows), f32), ((8, atoms), f32), ((3, atoms), f32)],
        cell_lengths,
        wave_numbers,
        lattice,
        third,
        counts,
        smem=(0,),
        scratch=[pltpu.VMEM((32, grid_rows), f32)],
        cost=busy,
    )
    half, other, (weights, factor) = summed(send, keep, (weights, factor))
    forces, energy = call(
        functools.partial(force_kernel, scale),
        [((3, atoms), f32), ((1, 1), f32)],
        half,
        other,
        lattice,
        phases,
        weights,
        factor,
        scratch=[pltpu.VMEM((2, 72, grid_rows), f32)],
    )
    return (forces, born_charges, energy[0, 0])


def solution(mesh):
    return jax.shard_map(
        per_device,
        mesh=mesh,
        in_specs=(
            P(None, ("wide", "narrow")),
            P(),
            P(("wide", "narrow"), None),
            P(("wide", "narrow")),
            P(("wide", "narrow"), None),
            P(None, ("wide", "narrow")),
            P(None, ("wide", "narrow")),
            P(),
            P(),
            P(),
            P(),
        ),
        out_specs=(P(None, ("wide", "narrow")), P(None, ("wide", "narrow")), P()),
        check_vma=False,
    )
```

```python
import functools
import math

import jax
import jax.numpy as jnp
from jax import lax
from jax.experimental import pallas as pl
from jax.experimental.pallas import tpu as pltpu
from jax.sharding import PartitionSpec as P

smearing = 0.5
two_pi = 2.0 * math.pi
kmax = 8
grid_rows = (2 * kmax + 1) * kmax
half_rows = 80
f32 = jnp.float32
bf16 = jnp.bfloat16
params = pltpu.CompilerParams(vmem_limit_bytes=48 * 1024 * 1024)


def dot_nn(a, b):
    return lax.dot_general(a, b, (((1,), (0,)), ((), ())), preferred_element_type=f32)


def dot_nt(a, b):
    return lax.dot_general(a, b, (((1,), (1,)), ((), ())), preferred_element_type=f32)


def parity(axis):
    return lax.rem(lax.axis_index(axis), 2)


def block_order(axis):
    odd = parity(axis)
    first = 0 if axis == "wide" else 2
    return first + odd, first + 1 - odd


def pick_matrix(index_ref, block, atoms):
    row_ids = lax.broadcasted_iota(jnp.int32, (atoms, index_ref.shape[1]), 0)
    return jnp.where(row_ids == index_ref[pl.ds(block, 1), :], 1.0, 0.0).astype(bf16)


def opening_kernel(opened_ref):
    opened_ref[...] = jnp.zeros(opened_ref.shape, f32)


def first_kernel(opened_ref, features_ref, index_ref, hidden_ref, pa, pb):
    hidden = jnp.transpose(features_ref[...].astype(f32)).astype(bf16)
    hidden_ref[...] = hidden
    for block, picked_ref in zip(block_order("narrow"), (pa, pb)):
        picked_ref[...] = dot_nn(hidden, pick_matrix(index_ref, block, hidden.shape[1]))


def wide_kernel(hidden_ref, index_ref, pa, pb):
    hidden = hidden_ref[...]
    for block, picked_ref in zip(block_order("wide"), (pa, pb)):
        picked_ref[...] = dot_nn(hidden, pick_matrix(index_ref, block, hidden.shape[1]))


def edge_tiles(senders_ref, radial_ref, edges_ref, local, axis):
    slots, atoms = senders_ref.shape
    rows = 128
    lanes = 128
    row_ids = lax.broadcasted_iota(jnp.int32, (rows, lanes), 0).astype(f32).astype(bf16)
    ghosts = (edges_ref.shape[0] - local) // 2
    one, two = block_order(axis)
    skip_one = atoms + one * ghosts - local
    skip_two = atoms + two * ghosts - local - ghosts

    def one_tile(tile, carry):
        first = pl.multiple_of(tile * rows, rows)
        skip = jnp.where(first < local, 0, jnp.where(first < local + ghosts, skip_one, skip_two))
        sender = first + skip
        for part in range(atoms // lanes):
            window = pl.ds(part * lanes, lanes)
            local_row = jnp.clip(senders_ref[:, window] - sender, -1, rows)
            local_row = local_row.astype(f32).astype(bf16)
            weight = radial_ref[:, window].astype(bf16)
            total = jnp.zeros((rows, lanes), bf16)
            for slot in range(slots):
                total = total + jnp.where(
                    row_ids == local_row[slot : slot + 1, :],
                    weight[slot : slot + 1, :],
                    jnp.zeros((), bf16),
                )
            edges_ref[pl.ds(first, rows), window] = total
        return carry

    lax.fori_loop(0, edges_ref.shape[0] // rows, one_tile, 0)


def far_edge_kernel(senders_ref, radial_ref, index_ref, hidden_ref, edges_ref, pick_ref, pa, pb):
    wide_kernel(hidden_ref, index_ref, pa, pb)
    ghosts = index_ref.shape[1]
    for i, block in enumerate(block_order("narrow")):
        pick_ref[:, i * ghosts : (i + 1) * ghosts] = pick_matrix(
            index_ref, block, senders_ref.shape[1]
        )
    edge_tiles(senders_ref, radial_ref, edges_ref, 0, "wide")


def near_edge_kernel(
    senders_ref, radial_ref, self_ref, message_ref, edges_ref, self_rows_ref, message_rows_ref
):
    edge_tiles(senders_ref, radial_ref, edges_ref, senders_ref.shape[1], "narrow")
    for layer in range(self_ref.shape[0]):
        self_rows_ref[layer] = jnp.transpose(self_ref[layer].astype(f32)).astype(bf16)
        message = jnp.transpose(message_ref[layer].astype(f32)).astype(bf16)
        message_rows_ref[layer] = jnp.concatenate([message, message], axis=1)


def local_kernel(layer, hidden_ref, edges_ref, self_rows_ref, own_ref, gathered_ref):
    hidden = hidden_ref[...]
    own_ref[...] = dot_nn(self_rows_ref[layer], hidden)
    gathered_ref[...] = dot_nn(hidden, edges_ref[0 : hidden.shape[1], :])


def near_kernel(gathered_ref, g2, g3, edges_ref, sum_ref):
    received = jnp.concatenate([g2[...].astype(bf16), g3[...].astype(bf16)], axis=1)
    local = edges_ref.shape[0] - received.shape[1]
    sum_ref[...] = gathered_ref[...] + dot_nn(received, edges_ref[local:, :])


def interact(layer, hidden_ref, own_ref, gathered_ref, g0, g1, edges_ref, message_rows_ref):
    received = jnp.concatenate([g0[...].astype(bf16), g1[...].astype(bf16)], axis=1)
    gathered = gathered_ref[...] + dot_nn(received, edges_ref[...])
    high = gathered.astype(bf16)
    low = (gathered - high.astype(f32)).astype(bf16)
    total = own_ref[...] + dot_nn(message_rows_ref[layer], jnp.concatenate([high, low], axis=0))
    gate = 0.5 * total * (1.0 + jnp.tanh(0.5 * total))
    return (hidden_ref[...].astype(f32) + gate).astype(bf16)


def layer_kernel(
    layer, hidden_ref, own_ref, gathered_ref, g0, g1, edges_ref, message_rows_ref, pick_ref, out_ref, p2, p3
):
    hidden = interact(layer, hidden_ref, own_ref, gathered_ref, g0, g1, edges_ref, message_rows_ref)
    out_ref[...] = hidden
    picked = dot_nn(hidden, pick_ref[...])
    ghosts = p2.shape[1]
    p2[...] = picked[:, 0:ghosts]
    p3[...] = picked[:, ghosts:]


def structure_part(lattice, phase_ref, part, out_ref):
    phases = phase_ref[part]
    out_ref[0:72, :] = dot_nt(lattice, phases[0:128, :])
    out_ref[72:80, 0:72] = dot_nt(phases[128:grid_rows, :], lattice)
    out_ref[72:80, 72:128] = jnp.zeros((8, 56), f32)


def last_kernel(
    layer,
    hidden_ref,
    own_ref,
    gathered_ref,
    g0,
    g1,
    edges_ref,
    message_rows_ref,
    readout_ref,
    count_ref,
    phase_ref,
    third_ref,
    send_ref,
    lattice_ref,
):
    hidden = interact(layer, hidden_ref, own_ref, gathered_ref, g0, g1, edges_ref, message_rows_ref)
    atoms = hidden.shape[1]
    slot_ids = lax.broadcasted_iota(jnp.int32, (8, atoms), 1)
    readout = readout_ref[...].astype(f32)
    readout = jnp.concatenate([readout, jnp.zeros_like(readout)], axis=0).astype(bf16)
    charges = jnp.where(slot_ids < count_ref[...], dot_nn(readout, hidden), 0.0)
    cosine = third_ref[0:8, :]
    sine = third_ref[8:16, :]
    rows = [charges[c : c + 1, :] * cosine for c in range(4)]
    rows = rows + [charges[c : c + 1, :] * sine for c in range(4)]
    lattice = jnp.concatenate(rows + [charges], axis=0)
    lattice_ref[...] = lattice
    structure_part(lattice.astype(bf16), phase_ref, 1 - parity("wide"), send_ref)


def keep_kernel(lattice_ref, phase_ref, keep_ref):
    structure_part(lattice_ref[...].astype(bf16), phase_ref, parity("wide"), keep_ref)


def wave_weight(m0, m1, m2, cell_ref):
    w0 = two_pi * m0 / cell_ref[0]
    w1 = two_pi * m1 / cell_ref[1]
    w2 = two_pi * m2 / cell_ref[2]
    squared = w0 * w0 + w1 * w1 + w2 * w2
    return jnp.exp(-0.5 * smearing * smearing * squared) / squared


def phase_kernel(fractions_ref, hidden_ref, index_ref, phase_ref, third_ref, p0, p1):
    wide_kernel(hidden_ref, index_ref, p0, p1)
    atoms = fractions_ref.shape[1]
    orders = lax.broadcasted_iota(jnp.int32, (8, atoms), 0).astype(f32) + 1.0
    cosines, sines = [], []
    for axis in range(3):
        turns = orders * fractions_ref[axis : axis + 1, :]
        angle = two_pi * (turns - jnp.round(turns))
        cosines.append(jnp.cos(angle))
        sines.append(jnp.sin(angle))
    third_ref[0:8, :] = cosines[2]
    third_ref[8:16, :] = sines[2]
    for axis in range(3):
        third_ref[16 + axis : 17 + axis, :] = cosines[axis][0:1, :]
    c0, s0 = cosines[0], sines[0]
    for m in range(-kmax, kmax + 1):
        window = pl.ds((m + kmax) * kmax, kmax)
        if m == 0:
            re, im = c0, s0
        else:
            row = abs(m) - 1
            c1 = cosines[1][row : row + 1, :]
            s1 = sines[1][row : row + 1, :]
            if m < 0:
                s1 = -s1
            re, im = c0 * c1 - s0 * s1, s0 * c1 + c0 * s1
        phase_ref[0, window, :] = re.astype(bf16)
        phase_ref[1, window, :] = im.astype(bf16)


def weight_kernel(
    scale,
    cell_ref,
    numbers_ref,
    lattice_ref,
    third_ref,
    count_ref,
    weight_ref,
    factor_ref,
    born_ref,
    acc,
):
    alive = lax.broadcasted_iota(jnp.int32, (1, lattice_ref.shape[1]), 1) < count_ref[...]
    for axis in range(3):
        factor_ref[axis : axis + 1, :] = jnp.where(alive, -(two_pi * scale / cell_ref[axis]), 0.0)
    total = jnp.sum(lattice_ref[64:68, :], axis=0, keepdims=True)
    born_ref[...] = total * third_ref[16:19, :]
    acc[...] = jnp.zeros_like(acc)
    width = math.gcd(numbers_ref.shape[1], 1024)
    plane_ids = lax.broadcasted_iota(jnp.int32, (grid_rows, width), 0)
    third_ids = lax.broadcasted_iota(jnp.int32, (32, width), 0)
    third_ids = jnp.where(
        third_ids < 8, third_ids + 1, jnp.where(third_ids < 16, 7 - third_ids, (third_ids - 16) * 64)
    )

    def count(step, carry):
        window = pl.ds(pl.multiple_of(step * width, width), width)
        numbers = numbers_ref[:, window]
        plane = (numbers[1:2, :] + kmax) * kmax + numbers[0:1, :] - 1
        in_plane = jnp.where(plane_ids == plane, 1.0, 0.0).astype(bf16)
        in_third = jnp.where(third_ids == numbers[2:3, :], 1.0, 0.0).astype(bf16)
        acc[...] += dot_nt(in_third, in_plane)
        return carry

    lax.fori_loop(0, numbers_ref.shape[1] // width, count, 0)
    lane = lax.broadcasted_iota(jnp.int32, (8, grid_rows), 1)
    m0 = (lane % 8 + 1).astype(f32)
    m1 = (lane // 8 - kmax).astype(f32)
    m2 = lax.broadcasted_iota(jnp.int32, (8, grid_rows), 0).astype(f32) + 1.0
    weight = wave_weight(m0, m1, m2, cell_ref)
    up = weight * acc[0:8, :]
    down = weight * acc[8:16, :]
    flat = wave_weight(m0, m1, 0.0 * m0, cell_ref) * acc[16:17, :]
    for c in range(4):
        weight_ref[8 * c : 8 * c + 8, :] = up
        weight_ref[32 + 8 * c : 40 + 8 * c, :] = down
    weight_ref[64:72, :] = flat


def force_kernel(
    scale,
    half_ref,
    other_ref,
    lattice_ref,
    phase_ref,
    weight_ref,
    factor_ref,
    forces_ref,
    energy_ref,
    sums_ref,
):
    core = parity("wide")
    for part_ref, part in ((half_ref, core), (other_ref, 1 - core)):
        sums_ref[part, :, 0:128] = part_ref[0:72, :]
        sums_ref[part, :, 128:grid_rows] = jnp.transpose(part_ref[72:80, :])[0:72, :]
    real = sums_ref[0]
    imag = sums_ref[1]
    real_cos, real_sin, real_flat = real[0:32], real[32:64], real[64:72]
    imag_cos, imag_sin, imag_flat = imag[0:32], imag[32:64], imag[64:72]
    weight_up = weight_ref[0:32, :]
    weight_down = weight_ref[32:64, :]
    weight_flat = weight_ref[64:72, :]
    up_re, up_im = real_cos - imag_sin, imag_cos + real_sin
    down_re, down_im = real_cos + imag_sin, imag_cos - real_sin
    up_im_w, up_re_w = weight_up * up_im, weight_up * up_re
    down_im_w, down_re_w = weight_down * down_im, weight_down * down_re
    flat_im_w, flat_re_w = weight_flat * imag_flat, weight_flat * real_flat
    power = up_im_w * up_im + up_re_w * up_re + down_im_w * down_im + down_re_w * down_re
    flat_power = flat_im_w * imag_flat + flat_re_w * real_flat
    power = jnp.sum(power, axis=0, keepdims=True) + jnp.sum(flat_power, axis=0, keepdims=True)
    energy_ref[...] = (0.5 * scale) * jnp.sum(power, axis=1, keepdims=True)

    im_sum, im_diff = up_im_w + down_im_w, up_im_w - down_im_w
    re_sum, re_diff = up_re_w + down_re_w, down_re_w - up_re_w
    even_real = jnp.concatenate([im_sum, re_diff, flat_im_w], axis=0)
    even_imag = jnp.concatenate([-re_sum, -im_diff, -flat_re_w], axis=0)
    m2 = (lax.broadcasted_iota(jnp.int32, (32, grid_rows), 0) % 8 + 1).astype(f32)
    odd_real = jnp.concatenate([m2 * im_diff, -m2 * re_sum], axis=0)
    odd_imag = jnp.concatenate([m2 * re_diff, -m2 * im_sum], axis=0)
    lane = lax.broadcasted_iota(jnp.int32, (72, grid_rows), 1)
    m0 = (lane % 8 + 1).astype(f32)
    m1 = (lane // 8 - kmax).astype(f32)
    with_real = jnp.concatenate([even_real * m0, even_real * m1, odd_real], axis=0).astype(bf16)
    with_imag = jnp.concatenate([even_imag * m0, even_imag * m1, odd_imag], axis=0).astype(bf16)
    back = dot_nn(with_real, phase_ref[0]) + dot_nn(with_imag, phase_ref[1])
    lattice = lattice_ref[...]
    for axis in range(3):
        rows = 64 if axis == 2 else 72
        terms = lattice[0:rows] * back[72 * axis : 72 * axis + rows]
        gradient = jnp.sum(terms, axis=0, keepdims=True)
        forces_ref[axis : axis + 1, :] = factor_ref[axis : axis + 1, :] * gradient


def call(kernel, outs, *args, smem=(), scratch=(), cost=None):
    specs = [
        pl.BlockSpec(memory_space=pltpu.SMEM if i in smem else pltpu.VMEM)
        for i in range(len(args))
    ]
    return pl.pallas_call(
        kernel,
        out_shape=[jax.ShapeDtypeStruct(shape, dtype) for shape, dtype in outs],
        in_specs=specs,
        out_specs=[pl.BlockSpec(memory_space=pltpu.VMEM)] * len(outs),
        scratch_shapes=list(scratch),
        compiler_params=params,
        cost_estimate=cost,
    )(*args)


def matched(first, second, axis):
    count = lax.axis_size(axis)
    ways = (-1, 1)
    one = lax.ppermute(first, axis, [(i, (i + ways[i % 2]) % count) for i in range(count)])
    two = lax.ppermute(second, axis, [(i, (i - ways[i % 2]) % count) for i in range(count)])
    return one, two


def flipped(block, axis, step):
    return lax.ppermute(block, axis, [(i, i ^ step) for i in range(lax.axis_size(axis))])


def summed(send, keep, beside):
    block = keep + flipped(send, "wide", 1)
    for axis, step in (("wide", 2), ("narrow", 1)):
        while step < lax.axis_size(axis):
            if axis == "narrow" and 2 * step >= lax.axis_size(axis):
                block, beside = lax.optimization_barrier((block, beside))
            block = block + flipped(block, axis, step)
            step *= 2
    return block, flipped(block, "wide", 1), beside


def per_device(
    fractions,
    cell_lengths,
    features,
    atom_counts,
    send_index,
    senders,
    radial,
    self_weight,
    message_weight,
    charge_weight,
    wave_numbers,
):
    atoms, width = features.shape
    ghosts = send_index.shape[1]
    rows = atoms + 4 * ghosts
    total_atoms = atoms * lax.axis_size("wide") * lax.axis_size("narrow")
    scale = 4.0 / math.sqrt(total_atoms * wave_numbers.shape[1])
    picked_outs = [((width, ghosts), f32)] * 2
    hidden_out = [((width, atoms), bf16)]
    sum_out = [((width, atoms), f32)]
    busy = pl.CostEstimate(flops=10**9, bytes_accessed=20 * 2**20, transcendentals=0)
    readout = charge_weight.T
    counts = atom_counts.reshape(1, 1)

    (opened,) = call(opening_kernel, [((8, 128), f32)], cost=busy)
    hidden, p2, p3 = call(
        first_kernel,
        hidden_out + picked_outs,
        opened,
        features,
        send_index,
        cost=busy,
    )
    g2, g3 = matched(p2, p3, "narrow")
    far_edges, picks, p0, p1 = call(
        far_edge_kernel,
        [((2 * ghosts, atoms), bf16), ((atoms, 2 * ghosts), bf16)] + picked_outs,
        senders,
        radial,
        send_index,
        hidden,
        cost=busy,
    )
    g0, g1 = matched(p0, p1, "wide")
    layers = self_weight.shape[0]
    near_edges, self_rows, message_rows = call(
        near_edge_kernel,
        [
            ((rows - 2 * ghosts, atoms), bf16),
            ((layers, width, width), bf16),
            ((layers, width, 2 * width), bf16),
        ],
        senders,
        radial,
        self_weight,
        message_weight,
        cost=busy,
    )
    for layer in range(layers):
        own, gathered = call(
            functools.partial(local_kernel, layer), sum_out * 2, hidden, near_edges, self_rows, cost=busy
        )
        (gathered,) = call(near_kernel, sum_out, gathered, g2, g3, near_edges)
        if layer == layers - 1:
            break
        hidden, p2, p3 = call(
            functools.partial(layer_kernel, layer),
            hidden_out + picked_outs,
            hidden,
            own,
            gathered,
            g0,
            g1,
            far_edges,
            message_rows,
            picks,
            cost=busy,
        )
        g2, g3 = matched(p2, p3, "narrow")
        phases, third, p0, p1 = call(
            phase_kernel,
            [((2, grid_rows, atoms), bf16), ((24, atoms), f32)] + picked_outs,
            fractions,
            hidden,
            send_index,
            cost=busy,
        )
        g0, g1 = matched(p0, p1, "wide")
    send, lattice = call(
        functools.partial(last_kernel, layers - 1),
        [((half_rows, 128), f32), ((72, atoms), f32)],
        hidden,
        own,
        gathered,
        g0,
        g1,
        far_edges,
        message_rows,
        readout,
        counts,
        phases,
        third,
    )
    weights, factor, born_charges = call(
        functools.partial(weight_kernel, scale),
        [((72, grid_rows), f32), ((8, atoms), f32), ((3, atoms), f32)],
        cell_lengths,
        wave_numbers,
        lattice,
        third,
        counts,
        smem=(0,),
        scratch=[pltpu.VMEM((32, grid_rows), f32)],
        cost=busy,
    )
    (keep,) = call(keep_kernel, [((half_rows, 128), f32)], lattice, phases, cost=busy)
    half, other, (weights, factor) = summed(send, keep, (weights, factor))
    forces, energy = call(
        functools.partial(force_kernel, scale),
        [((3, atoms), f32), ((1, 1), f32)],
        half,
        other,
        lattice,
        phases,
        weights,
        factor,
        scratch=[pltpu.VMEM((2, 72, grid_rows), f32)],
    )
    return (forces, born_charges, energy[0, 0])


def solution(mesh):
    return jax.shard_map(
        per_device,
        mesh=mesh,
        in_specs=(
            P(None, ("wide", "narrow")),
            P(),
            P(("wide", "narrow"), None),
            P(("wide", "narrow")),
            P(("wide", "narrow"), None),
            P(None, ("wide", "narrow")),
            P(None, ("wide", "narrow")),
            P(),
            P(),
            P(),
            P(),
        ),
        out_specs=(P(None, ("wide", "narrow")), P(None, ("wide", "narrow")), P()),
        check_vma=False,
    )
```

```python
import functools
import math

import jax
import jax.numpy as jnp
from jax import lax
from jax.experimental import pallas as pl
from jax.experimental.pallas import tpu as pltpu
from jax.sharding import PartitionSpec as P

smearing = 0.5
two_pi = 2.0 * math.pi
kmax = 8
grid_rows = (2 * kmax + 1) * kmax
half_rows = 80
f32 = jnp.float32
bf16 = jnp.bfloat16
params = pltpu.CompilerParams(vmem_limit_bytes=48 * 1024 * 1024)


def dot_nn(a, b):
    return lax.dot_general(a, b, (((1,), (0,)), ((), ())), preferred_element_type=f32)


def dot_nt(a, b):
    return lax.dot_general(a, b, (((1,), (1,)), ((), ())), preferred_element_type=f32)


def parity(axis):
    return lax.rem(lax.axis_index(axis), 2)


def block_order(axis):
    odd = parity(axis)
    first = 0 if axis == "wide" else 2
    return first + odd, first + 1 - odd


def pick_matrix(index_ref, block, atoms):
    row_ids = lax.broadcasted_iota(jnp.int32, (atoms, index_ref.shape[1]), 0)
    return jnp.where(row_ids == index_ref[pl.ds(block, 1), :], 1.0, 0.0).astype(bf16)


def opening_kernel(opened_ref):
    opened_ref[...] = jnp.zeros(opened_ref.shape, f32)


def first_kernel(opened_ref, features_ref, index_ref, hidden_ref, pa, pb):
    hidden = jnp.transpose(features_ref[...].astype(f32)).astype(bf16)
    hidden_ref[...] = hidden
    for block, picked_ref in zip(block_order("narrow"), (pa, pb)):
        picked_ref[...] = dot_nn(hidden, pick_matrix(index_ref, block, hidden.shape[1]))


def wide_kernel(hidden_ref, index_ref, pa, pb):
    hidden = hidden_ref[...]
    for block, picked_ref in zip(block_order("wide"), (pa, pb)):
        picked_ref[...] = dot_nn(hidden, pick_matrix(index_ref, block, hidden.shape[1]))


def edge_tiles(senders_ref, radial_ref, edges_ref, local, axis):
    slots, atoms = senders_ref.shape
    rows = 128
    lanes = 128
    row_ids = lax.broadcasted_iota(jnp.int32, (rows, lanes), 0).astype(f32).astype(bf16)
    ghosts = (edges_ref.shape[0] - local) // 2
    one, two = block_order(axis)
    skip_one = atoms + one * ghosts - local
    skip_two = atoms + two * ghosts - local - ghosts

    def one_tile(tile, carry):
        first = pl.multiple_of(tile * rows, rows)
        skip = jnp.where(first < local, 0, jnp.where(first < local + ghosts, skip_one, skip_two))
        sender = first + skip
        for part in range(atoms // lanes):
            window = pl.ds(part * lanes, lanes)
            local_row = jnp.clip(senders_ref[:, window] - sender, -1, rows)
            local_row = local_row.astype(f32).astype(bf16)
            weight = radial_ref[:, window].astype(bf16)
            total = jnp.zeros((rows, lanes), bf16)
            for slot in range(slots):
                total = total + jnp.where(
                    row_ids == local_row[slot : slot + 1, :],
                    weight[slot : slot + 1, :],
                    jnp.zeros((), bf16),
                )
            edges_ref[pl.ds(first, rows), window] = total
        return carry

    lax.fori_loop(0, edges_ref.shape[0] // rows, one_tile, 0)


def pick_kernel(index_ref, hidden_ref, pick_ref, pa, pb):
    wide_kernel(hidden_ref, index_ref, pa, pb)
    ghosts = index_ref.shape[1]
    for i, block in enumerate(block_order("narrow")):
        pick_ref[:, i * ghosts : (i + 1) * ghosts] = pick_matrix(
            index_ref, block, hidden_ref.shape[1]
        )


def edge_kernel(
    senders_ref, radial_ref, self_ref, message_ref, near_ref, far_ref, self_rows_ref, message_rows_ref
):
    edge_tiles(senders_ref, radial_ref, near_ref, senders_ref.shape[1], "narrow")
    edge_tiles(senders_ref, radial_ref, far_ref, 0, "wide")
    for layer in range(self_ref.shape[0]):
        self_rows_ref[layer] = jnp.transpose(self_ref[layer].astype(f32)).astype(bf16)
        message = jnp.transpose(message_ref[layer].astype(f32)).astype(bf16)
        message_rows_ref[layer] = jnp.concatenate([message, message], axis=1)


def local_kernel(layer, hidden_ref, edges_ref, self_rows_ref, own_ref, gathered_ref):
    hidden = hidden_ref[...]
    own_ref[...] = dot_nn(self_rows_ref[layer], hidden)
    gathered_ref[...] = dot_nn(hidden, edges_ref[0 : hidden.shape[1], :])


def near_kernel(gathered_ref, g2, g3, edges_ref, sum_ref):
    received = jnp.concatenate([g2[...].astype(bf16), g3[...].astype(bf16)], axis=1)
    local = edges_ref.shape[0] - received.shape[1]
    sum_ref[...] = gathered_ref[...] + dot_nn(received, edges_ref[local:, :])


def interact(layer, hidden_ref, own_ref, gathered_ref, g0, g1, edges_ref, message_rows_ref):
    received = jnp.concatenate([g0[...].astype(bf16), g1[...].astype(bf16)], axis=1)
    gathered = gathered_ref[...] + dot_nn(received, edges_ref[...])
    high = gathered.astype(bf16)
    low = (gathered - high.astype(f32)).astype(bf16)
    total = own_ref[...] + dot_nn(message_rows_ref[layer], jnp.concatenate([high, low], axis=0))
    gate = 0.5 * total * (1.0 + jnp.tanh(0.5 * total))
    return (hidden_ref[...].astype(f32) + gate).astype(bf16)


def layer_kernel(
    layer, hidden_ref, own_ref, gathered_ref, g0, g1, edges_ref, message_rows_ref, pick_ref, out_ref, p2, p3
):
    hidden = interact(layer, hidden_ref, own_ref, gathered_ref, g0, g1, edges_ref, message_rows_ref)
    out_ref[...] = hidden
    picked = dot_nn(hidden, pick_ref[...])
    ghosts = p2.shape[1]
    p2[...] = picked[:, 0:ghosts]
    p3[...] = picked[:, ghosts:]


def structure_part(lattice, phase_ref, part, out_ref):
    phases = phase_ref[part]
    out_ref[0:72, :] = dot_nt(lattice, phases[0:128, :])
    out_ref[72:80, 0:72] = dot_nt(phases[128:grid_rows, :], lattice)
    out_ref[72:80, 72:128] = jnp.zeros((8, 56), f32)


def last_kernel(
    layer,
    hidden_ref,
    own_ref,
    gathered_ref,
    g0,
    g1,
    edges_ref,
    message_rows_ref,
    readout_ref,
    count_ref,
    phase_ref,
    third_ref,
    send_ref,
    lattice_ref,
):
    hidden = interact(layer, hidden_ref, own_ref, gathered_ref, g0, g1, edges_ref, message_rows_ref)
    atoms = hidden.shape[1]
    slot_ids = lax.broadcasted_iota(jnp.int32, (8, atoms), 1)
    readout = readout_ref[...].astype(f32)
    readout = jnp.concatenate([readout, jnp.zeros_like(readout)], axis=0).astype(bf16)
    charges = jnp.where(slot_ids < count_ref[...], dot_nn(readout, hidden), 0.0)
    cosine = third_ref[0:8, :]
    sine = third_ref[8:16, :]
    rows = [charges[c : c + 1, :] * cosine for c in range(4)]
    rows = rows + [charges[c : c + 1, :] * sine for c in range(4)]
    lattice = jnp.concatenate(rows + [charges], axis=0)
    lattice_ref[...] = lattice
    structure_part(lattice.astype(bf16), phase_ref, 1 - parity("wide"), send_ref)


def keep_kernel(lattice_ref, phase_ref, keep_ref):
    structure_part(lattice_ref[...].astype(bf16), phase_ref, parity("wide"), keep_ref)


def wave_weight(m0, m1, m2, cell_ref):
    w0 = two_pi * m0 / cell_ref[0]
    w1 = two_pi * m1 / cell_ref[1]
    w2 = two_pi * m2 / cell_ref[2]
    squared = w0 * w0 + w1 * w1 + w2 * w2
    return jnp.exp(-0.5 * smearing * smearing * squared) / squared


def phase_kernel(fractions_ref, hidden_ref, index_ref, phase_ref, third_ref, p0, p1):
    wide_kernel(hidden_ref, index_ref, p0, p1)
    atoms = fractions_ref.shape[1]
    orders = lax.broadcasted_iota(jnp.int32, (8, atoms), 0).astype(f32) + 1.0
    cosines, sines = [], []
    for axis in range(3):
        turns = orders * fractions_ref[axis : axis + 1, :]
        angle = two_pi * (turns - jnp.round(turns))
        cosines.append(jnp.cos(angle))
        sines.append(jnp.sin(angle))
    third_ref[0:8, :] = cosines[2]
    third_ref[8:16, :] = sines[2]
    for axis in range(3):
        third_ref[16 + axis : 17 + axis, :] = cosines[axis][0:1, :]
    c0, s0 = cosines[0], sines[0]
    for m in range(-kmax, kmax + 1):
        window = pl.ds((m + kmax) * kmax, kmax)
        if m == 0:
            re, im = c0, s0
        else:
            row = abs(m) - 1
            c1 = cosines[1][row : row + 1, :]
            s1 = sines[1][row : row + 1, :]
            if m < 0:
                s1 = -s1
            re, im = c0 * c1 - s0 * s1, s0 * c1 + c0 * s1
        phase_ref[0, window, :] = re.astype(bf16)
        phase_ref[1, window, :] = im.astype(bf16)


def weight_kernel(
    scale,
    cell_ref,
    numbers_ref,
    lattice_ref,
    third_ref,
    count_ref,
    weight_ref,
    factor_ref,
    born_ref,
    acc,
):
    alive = lax.broadcasted_iota(jnp.int32, (1, lattice_ref.shape[1]), 1) < count_ref[...]
    for axis in range(3):
        factor_ref[axis : axis + 1, :] = jnp.where(alive, -(two_pi * scale / cell_ref[axis]), 0.0)
    total = jnp.sum(lattice_ref[64:68, :], axis=0, keepdims=True)
    born_ref[...] = total * third_ref[16:19, :]
    acc[...] = jnp.zeros_like(acc)
    width = math.gcd(numbers_ref.shape[1], 1024)
    plane_ids = lax.broadcasted_iota(jnp.int32, (grid_rows, width), 0)
    third_ids = lax.broadcasted_iota(jnp.int32, (32, width), 0)
    third_ids = jnp.where(
        third_ids < 8, third_ids + 1, jnp.where(third_ids < 16, 7 - third_ids, (third_ids - 16) * 64)
    )

    def count(step, carry):
        window = pl.ds(pl.multiple_of(step * width, width), width)
        numbers = numbers_ref[:, window]
        plane = (numbers[1:2, :] + kmax) * kmax + numbers[0:1, :] - 1
        in_plane = jnp.where(plane_ids == plane, 1.0, 0.0).astype(bf16)
        in_third = jnp.where(third_ids == numbers[2:3, :], 1.0, 0.0).astype(bf16)
        acc[...] += dot_nt(in_third, in_plane)
        return carry

    lax.fori_loop(0, numbers_ref.shape[1] // width, count, 0)
    lane = lax.broadcasted_iota(jnp.int32, (8, grid_rows), 1)
    m0 = (lane % 8 + 1).astype(f32)
    m1 = (lane // 8 - kmax).astype(f32)
    m2 = lax.broadcasted_iota(jnp.int32, (8, grid_rows), 0).astype(f32) + 1.0
    weight = wave_weight(m0, m1, m2, cell_ref)
    up = weight * acc[0:8, :]
    down = weight * acc[8:16, :]
    flat = wave_weight(m0, m1, 0.0 * m0, cell_ref) * acc[16:17, :]
    for c in range(4):
        weight_ref[8 * c : 8 * c + 8, :] = up
        weight_ref[32 + 8 * c : 40 + 8 * c, :] = down
    weight_ref[64:72, :] = flat


def force_kernel(
    scale,
    half_ref,
    other_ref,
    lattice_ref,
    phase_ref,
    weight_ref,
    factor_ref,
    forces_ref,
    energy_ref,
    sums_ref,
):
    core = parity("wide")
    for part_ref, part in ((half_ref, core), (other_ref, 1 - core)):
        sums_ref[part, :, 0:128] = part_ref[0:72, :]
        sums_ref[part, :, 128:grid_rows] = jnp.transpose(part_ref[72:80, :])[0:72, :]
    real = sums_ref[0]
    imag = sums_ref[1]
    real_cos, real_sin, real_flat = real[0:32], real[32:64], real[64:72]
    imag_cos, imag_sin, imag_flat = imag[0:32], imag[32:64], imag[64:72]
    weight_up = weight_ref[0:32, :]
    weight_down = weight_ref[32:64, :]
    weight_flat = weight_ref[64:72, :]
    up_re, up_im = real_cos - imag_sin, imag_cos + real_sin
    down_re, down_im = real_cos + imag_sin, imag_cos - real_sin
    up_im_w, up_re_w = weight_up * up_im, weight_up * up_re
    down_im_w, down_re_w = weight_down * down_im, weight_down * down_re
    flat_im_w, flat_re_w = weight_flat * imag_flat, weight_flat * real_flat
    power = up_im_w * up_im + up_re_w * up_re + down_im_w * down_im + down_re_w * down_re
    flat_power = flat_im_w * imag_flat + flat_re_w * real_flat
    power = jnp.sum(power, axis=0, keepdims=True) + jnp.sum(flat_power, axis=0, keepdims=True)
    energy_ref[...] = (0.5 * scale) * jnp.sum(power, axis=1, keepdims=True)

    im_sum, im_diff = up_im_w + down_im_w, up_im_w - down_im_w
    re_sum, re_diff = up_re_w + down_re_w, down_re_w - up_re_w
    even_real = jnp.concatenate([im_sum, re_diff, flat_im_w], axis=0)
    even_imag = jnp.concatenate([-re_sum, -im_diff, -flat_re_w], axis=0)
    m2 = (lax.broadcasted_iota(jnp.int32, (32, grid_rows), 0) % 8 + 1).astype(f32)
    odd_real = jnp.concatenate([m2 * im_diff, -m2 * re_sum], axis=0)
    odd_imag = jnp.concatenate([m2 * re_diff, -m2 * im_sum], axis=0)
    lane = lax.broadcasted_iota(jnp.int32, (72, grid_rows), 1)
    m0 = (lane % 8 + 1).astype(f32)
    m1 = (lane // 8 - kmax).astype(f32)
    with_real = jnp.concatenate([even_real * m0, even_real * m1, odd_real], axis=0).astype(bf16)
    with_imag = jnp.concatenate([even_imag * m0, even_imag * m1, odd_imag], axis=0).astype(bf16)
    back = dot_nn(with_real, phase_ref[0]) + dot_nn(with_imag, phase_ref[1])
    lattice = lattice_ref[...]
    for axis in range(3):
        rows = 64 if axis == 2 else 72
        terms = lattice[0:rows] * back[72 * axis : 72 * axis + rows]
        gradient = jnp.sum(terms, axis=0, keepdims=True)
        forces_ref[axis : axis + 1, :] = factor_ref[axis : axis + 1, :] * gradient


def call(kernel, outs, *args, smem=(), scratch=(), cost=None):
    specs = [
        pl.BlockSpec(memory_space=pltpu.SMEM if i in smem else pltpu.VMEM)
        for i in range(len(args))
    ]
    return pl.pallas_call(
        kernel,
        out_shape=[jax.ShapeDtypeStruct(shape, dtype) for shape, dtype in outs],
        in_specs=specs,
        out_specs=[pl.BlockSpec(memory_space=pltpu.VMEM)] * len(outs),
        scratch_shapes=list(scratch),
        compiler_params=params,
        cost_estimate=cost,
    )(*args)


def matched(first, second, axis):
    count = lax.axis_size(axis)
    ways = (-1, 1)
    one = lax.ppermute(first, axis, [(i, (i + ways[i % 2]) % count) for i in range(count)])
    two = lax.ppermute(second, axis, [(i, (i - ways[i % 2]) % count) for i in range(count)])
    return one, two


def flipped(block, wide_step, narrow_step):
    wide, narrow = lax.axis_size("wide"), lax.axis_size("narrow")
    pairs = [
        (w * narrow + z, (w ^ wide_step) * narrow + (z ^ narrow_step))
        for w in range(wide)
        for z in range(narrow)
    ]
    return lax.ppermute(block, ("wide", "narrow"), pairs)


def summed(send, keep, beside):
    wide_steps = [2**i for i in range(1, (lax.axis_size("wide") - 1).bit_length())]
    narrow_steps = [2**i for i in range((lax.axis_size("narrow") - 1).bit_length())]
    count = max(len(wide_steps), len(narrow_steps))
    block = keep + flipped(send, 1, 0)
    for i in range(count):
        if i == count - 1:
            block, beside = lax.optimization_barrier((block, beside))
        wide_step = wide_steps[i] if i < len(wide_steps) else 0
        narrow_step = narrow_steps[i] if i < len(narrow_steps) else 0
        if wide_step and narrow_step:
            one, two, three = [flipped(block, *steps) for steps in [(0, narrow_step), (wide_step, narrow_step), (wide_step, 0)]]
            block = block + ((one + two) + three)
        else:
            block = block + flipped(block, wide_step, narrow_step)
    return block, flipped(block, 1, 0), beside


def per_device(
    fractions,
    cell_lengths,
    features,
    atom_counts,
    send_index,
    senders,
    radial,
    self_weight,
    message_weight,
    charge_weight,
    wave_numbers,
):
    atoms, width = features.shape
    ghosts = send_index.shape[1]
    rows = atoms + 4 * ghosts
    total_atoms = atoms * lax.axis_size("wide") * lax.axis_size("narrow")
    scale = 4.0 / math.sqrt(total_atoms * wave_numbers.shape[1])
    picked_outs = [((width, ghosts), f32)] * 2
    hidden_out = [((width, atoms), bf16)]
    sum_out = [((width, atoms), f32)]
    busy = pl.CostEstimate(flops=10**9, bytes_accessed=20 * 2**20, transcendentals=0)
    readout = charge_weight.T
    counts = atom_counts.reshape(1, 1)

    (opened,) = call(opening_kernel, [((8, 128), f32)], cost=busy)
    hidden, p2, p3 = call(
        first_kernel,
        hidden_out + picked_outs,
        opened,
        features,
        send_index,
        cost=busy,
    )
    g2, g3 = matched(p2, p3, "narrow")
    picks, p0, p1 = call(
        pick_kernel, [((atoms, 2 * ghosts), bf16)] + picked_outs, send_index, hidden, cost=busy
    )
    g0, g1 = matched(p0, p1, "wide")
    layers = self_weight.shape[0]
    near_edges, far_edges, self_rows, message_rows = call(
        edge_kernel,
        [
            ((rows - 2 * ghosts, atoms), bf16),
            ((2 * ghosts, atoms), bf16),
            ((layers, width, width), bf16),
            ((layers, width, 2 * width), bf16),
        ],
        senders,
        radial,
        self_weight,
        message_weight,
        cost=busy,
    )
    for layer in range(layers):
        own, gathered = call(
            functools.partial(local_kernel, layer), sum_out * 2, hidden, near_edges, self_rows, cost=busy
        )
        (gathered,) = call(near_kernel, sum_out, gathered, g2, g3, near_edges)
        if layer == layers - 1:
            break
        hidden, p2, p3 = call(
            functools.partial(layer_kernel, layer),
            hidden_out + picked_outs,
            hidden,
            own,
            gathered,
            g0,
            g1,
            far_edges,
            message_rows,
            picks,
            cost=busy,
        )
        g2, g3 = matched(p2, p3, "narrow")
        phases, third, p0, p1 = call(
            phase_kernel,
            [((2, grid_rows, atoms), bf16), ((24, atoms), f32)] + picked_outs,
            fractions,
            hidden,
            send_index,
            cost=busy,
        )
        g0, g1 = matched(p0, p1, "wide")
    send, lattice = call(
        functools.partial(last_kernel, layers - 1),
        [((half_rows, 128), f32), ((72, atoms), f32)],
        hidden,
        own,
        gathered,
        g0,
        g1,
        far_edges,
        message_rows,
        readout,
        counts,
        phases,
        third,
    )
    weights, factor, born_charges = call(
        functools.partial(weight_kernel, scale),
        [((72, grid_rows), f32), ((8, atoms), f32), ((3, atoms), f32)],
        cell_lengths,
        wave_numbers,
        lattice,
        third,
        counts,
        smem=(0,),
        scratch=[pltpu.VMEM((32, grid_rows), f32)],
        cost=busy,
    )
    (keep,) = call(keep_kernel, [((half_rows, 128), f32)], lattice, phases, cost=busy)
    half, other, (weights, factor) = summed(send, keep, (weights, factor))
    forces, energy = call(
        functools.partial(force_kernel, scale),
        [((3, atoms), f32), ((1, 1), f32)],
        half,
        other,
        lattice,
        phases,
        weights,
        factor,
        scratch=[pltpu.VMEM((2, 72, grid_rows), f32)],
    )
    return (forces, born_charges, energy[0, 0])


def solution(mesh):
    return jax.shard_map(
        per_device,
        mesh=mesh,
        in_specs=(
            P(None, ("wide", "narrow")),
            P(),
            P(("wide", "narrow"), None),
            P(("wide", "narrow")),
            P(("wide", "narrow"), None),
            P(None, ("wide", "narrow")),
            P(None, ("wide", "narrow")),
            P(),
            P(),
            P(),
            P(),
        ),
        out_specs=(P(None, ("wide", "narrow")), P(None, ("wide", "narrow")), P()),
        check_vma=False,
    )
```

```python
import functools
import math

import jax
import jax.numpy as jnp
from jax import lax
from jax.experimental import pallas as pl
from jax.experimental.pallas import tpu as pltpu
from jax.sharding import PartitionSpec as P

smearing = 0.5
two_pi = 2.0 * math.pi
kmax = 8
grid_rows = (2 * kmax + 1) * kmax
half_rows = 80
f32 = jnp.float32
bf16 = jnp.bfloat16
params = pltpu.CompilerParams(vmem_limit_bytes=48 * 1024 * 1024)


def dot_nn(a, b):
    return lax.dot_general(a, b, (((1,), (0,)), ((), ())), preferred_element_type=f32)


def dot_nt(a, b):
    return lax.dot_general(a, b, (((1,), (1,)), ((), ())), preferred_element_type=f32)


def parity(axis):
    return lax.rem(lax.axis_index(axis), 2)


def block_order(axis):
    odd = parity(axis) if axis == "wide" else 1 - parity(axis)
    first = 0 if axis == "wide" else 2
    return first + odd, first + 1 - odd


def pick_matrix(index_ref, block, atoms):
    row_ids = lax.broadcasted_iota(jnp.int32, (atoms, index_ref.shape[1]), 0)
    return jnp.where(row_ids == index_ref[pl.ds(block, 1), :], 1.0, 0.0).astype(bf16)


def opening_kernel(opened_ref):
    opened_ref[...] = jnp.zeros(opened_ref.shape, f32)


def first_kernel(opened_ref, features_ref, index_ref, hidden_ref, pa, pb):
    hidden = jnp.transpose(features_ref[...].astype(f32)).astype(bf16)
    hidden_ref[...] = hidden
    for block, picked_ref in zip(block_order("narrow"), (pa, pb)):
        picked_ref[...] = dot_nn(hidden, pick_matrix(index_ref, block, hidden.shape[1]))


def wide_kernel(hidden_ref, index_ref, pa, pb):
    hidden = hidden_ref[...]
    for block, picked_ref in zip(block_order("wide"), (pa, pb)):
        picked_ref[...] = dot_nn(hidden, pick_matrix(index_ref, block, hidden.shape[1]))


def edge_tiles(senders_ref, radial_ref, edges_ref, local, axis):
    slots, atoms = senders_ref.shape
    rows = 128
    lanes = 128
    row_ids = lax.broadcasted_iota(jnp.int32, (rows, lanes), 0).astype(f32).astype(bf16)
    ghosts = (edges_ref.shape[0] - local) // 2
    one, two = block_order(axis)
    skip_one = atoms + one * ghosts - local
    skip_two = atoms + two * ghosts - local - ghosts

    def one_tile(tile, carry):
        first = pl.multiple_of(tile * rows, rows)
        skip = jnp.where(first < local, 0, jnp.where(first < local + ghosts, skip_one, skip_two))
        sender = first + skip
        for part in range(atoms // lanes):
            window = pl.ds(part * lanes, lanes)
            local_row = jnp.clip(senders_ref[:, window] - sender, -1, rows)
            local_row = local_row.astype(f32).astype(bf16)
            weight = radial_ref[:, window].astype(bf16)
            total = jnp.zeros((rows, lanes), bf16)
            for slot in range(slots):
                total = total + jnp.where(
                    row_ids == local_row[slot : slot + 1, :],
                    weight[slot : slot + 1, :],
                    jnp.zeros((), bf16),
                )
            edges_ref[pl.ds(first, rows), window] = total
        return carry

    lax.fori_loop(0, edges_ref.shape[0] // rows, one_tile, 0)


def pick_kernel(index_ref, hidden_ref, pick_ref, pa, pb):
    wide_kernel(hidden_ref, index_ref, pa, pb)
    ghosts = index_ref.shape[1]
    for i, block in enumerate(block_order("narrow")):
        pick_ref[:, i * ghosts : (i + 1) * ghosts] = pick_matrix(
            index_ref, block, hidden_ref.shape[1]
        )


def edge_kernel(
    senders_ref, radial_ref, self_ref, message_ref, near_ref, far_ref, self_rows_ref, message_rows_ref
):
    edge_tiles(senders_ref, radial_ref, near_ref, senders_ref.shape[1], "narrow")
    edge_tiles(senders_ref, radial_ref, far_ref, 0, "wide")
    for layer in range(self_ref.shape[0]):
        self_rows_ref[layer] = jnp.transpose(self_ref[layer].astype(f32)).astype(bf16)
        message = jnp.transpose(message_ref[layer].astype(f32)).astype(bf16)
        message_rows_ref[layer] = jnp.concatenate([message, message], axis=1)


def local_kernel(layer, hidden_ref, edges_ref, self_rows_ref, own_ref, gathered_ref):
    hidden = hidden_ref[...]
    own_ref[...] = dot_nn(self_rows_ref[layer], hidden)
    gathered_ref[...] = dot_nn(hidden, edges_ref[0 : hidden.shape[1], :])


def near_kernel(gathered_ref, g2, g3, edges_ref, sum_ref):
    received = jnp.concatenate([g2[...].astype(bf16), g3[...].astype(bf16)], axis=1)
    local = edges_ref.shape[0] - received.shape[1]
    sum_ref[...] = gathered_ref[...] + dot_nn(received, edges_ref[local:, :])


def interact(layer, hidden_ref, own_ref, gathered_ref, g0, g1, edges_ref, message_rows_ref):
    received = jnp.concatenate([g0[...].astype(bf16), g1[...].astype(bf16)], axis=1)
    gathered = gathered_ref[...] + dot_nn(received, edges_ref[...])
    high = gathered.astype(bf16)
    low = (gathered - high.astype(f32)).astype(bf16)
    total = own_ref[...] + dot_nn(message_rows_ref[layer], jnp.concatenate([high, low], axis=0))
    gate = 0.5 * total * (1.0 + jnp.tanh(0.5 * total))
    return (hidden_ref[...].astype(f32) + gate).astype(bf16)


def layer_kernel(
    layer, hidden_ref, own_ref, gathered_ref, g0, g1, edges_ref, message_rows_ref, pick_ref, out_ref, p2, p3
):
    hidden = interact(layer, hidden_ref, own_ref, gathered_ref, g0, g1, edges_ref, message_rows_ref)
    out_ref[...] = hidden
    picked = dot_nn(hidden, pick_ref[...])
    ghosts = p2.shape[1]
    p2[...] = picked[:, 0:ghosts]
    p3[...] = picked[:, ghosts:]


def structure_part(lattice, phase_ref, part, out_ref):
    phases = phase_ref[part]
    out_ref[0:72, :] = dot_nt(lattice, phases[0:128, :])
    out_ref[72:80, 0:72] = dot_nt(phases[128:grid_rows, :], lattice)
    out_ref[72:80, 72:128] = jnp.zeros((8, 56), f32)


def last_kernel(
    layer,
    hidden_ref,
    own_ref,
    gathered_ref,
    g0,
    g1,
    edges_ref,
    message_rows_ref,
    readout_ref,
    count_ref,
    phase_ref,
    third_ref,
    send_ref,
    lattice_ref,
):
    hidden = interact(layer, hidden_ref, own_ref, gathered_ref, g0, g1, edges_ref, message_rows_ref)
    atoms = hidden.shape[1]
    slot_ids = lax.broadcasted_iota(jnp.int32, (8, atoms), 1)
    readout = readout_ref[...].astype(f32)
    readout = jnp.concatenate([readout, jnp.zeros_like(readout)], axis=0).astype(bf16)
    charges = jnp.where(slot_ids < count_ref[...], dot_nn(readout, hidden), 0.0)
    cosine = third_ref[0:8, :]
    sine = third_ref[8:16, :]
    rows = [charges[c : c + 1, :] * cosine for c in range(4)]
    rows = rows + [charges[c : c + 1, :] * sine for c in range(4)]
    lattice = jnp.concatenate(rows + [charges], axis=0)
    lattice_ref[...] = lattice
    structure_part(lattice.astype(bf16), phase_ref, 1 - parity("wide"), send_ref)


def keep_kernel(lattice_ref, phase_ref, keep_ref):
    structure_part(lattice_ref[...].astype(bf16), phase_ref, parity("wide"), keep_ref)


def wave_weight(m0, m1, m2, cell_ref):
    w0 = two_pi * m0 / cell_ref[0]
    w1 = two_pi * m1 / cell_ref[1]
    w2 = two_pi * m2 / cell_ref[2]
    squared = w0 * w0 + w1 * w1 + w2 * w2
    return jnp.exp(-0.5 * smearing * smearing * squared) / squared


def phase_kernel(fractions_ref, hidden_ref, index_ref, phase_ref, third_ref, p0, p1):
    wide_kernel(hidden_ref, index_ref, p0, p1)
    atoms = fractions_ref.shape[1]
    orders = lax.broadcasted_iota(jnp.int32, (8, atoms), 0).astype(f32) + 1.0
    cosines, sines = [], []
    for axis in range(3):
        turns = orders * fractions_ref[axis : axis + 1, :]
        angle = two_pi * (turns - jnp.round(turns))
        cosines.append(jnp.cos(angle))
        sines.append(jnp.sin(angle))
    third_ref[0:8, :] = cosines[2]
    third_ref[8:16, :] = sines[2]
    for axis in range(3):
        third_ref[16 + axis : 17 + axis, :] = cosines[axis][0:1, :]
    c0, s0 = cosines[0], sines[0]
    for m in range(-kmax, kmax + 1):
        window = pl.ds((m + kmax) * kmax, kmax)
        if m == 0:
            re, im = c0, s0
        else:
            row = abs(m) - 1
            c1 = cosines[1][row : row + 1, :]
            s1 = sines[1][row : row + 1, :]
            if m < 0:
                s1 = -s1
            re, im = c0 * c1 - s0 * s1, s0 * c1 + c0 * s1
        phase_ref[0, window, :] = re.astype(bf16)
        phase_ref[1, window, :] = im.astype(bf16)


def weight_kernel(
    scale,
    cell_ref,
    numbers_ref,
    lattice_ref,
    third_ref,
    count_ref,
    weight_ref,
    factor_ref,
    born_ref,
    acc,
):
    alive = lax.broadcasted_iota(jnp.int32, (1, lattice_ref.shape[1]), 1) < count_ref[...]
    for axis in range(3):
        factor_ref[axis : axis + 1, :] = jnp.where(alive, -(two_pi * scale / cell_ref[axis]), 0.0)
    total = jnp.sum(lattice_ref[64:68, :], axis=0, keepdims=True)
    born_ref[...] = total * third_ref[16:19, :]
    acc[...] = jnp.zeros_like(acc)
    width = math.gcd(numbers_ref.shape[1], 1024)
    plane_ids = lax.broadcasted_iota(jnp.int32, (grid_rows, width), 0)
    third_ids = lax.broadcasted_iota(jnp.int32, (32, width), 0)
    third_ids = jnp.where(
        third_ids < 8, third_ids + 1, jnp.where(third_ids < 16, 7 - third_ids, (third_ids - 16) * 64)
    )

    def count(step, carry):
        window = pl.ds(pl.multiple_of(step * width, width), width)
        numbers = numbers_ref[:, window]
        plane = (numbers[1:2, :] + kmax) * kmax + numbers[0:1, :] - 1
        in_plane = jnp.where(plane_ids == plane, 1.0, 0.0).astype(bf16)
        in_third = jnp.where(third_ids == numbers[2:3, :], 1.0, 0.0).astype(bf16)
        acc[...] += dot_nt(in_third, in_plane)
        return carry

    lax.fori_loop(0, numbers_ref.shape[1] // width, count, 0)
    lane = lax.broadcasted_iota(jnp.int32, (8, grid_rows), 1)
    m0 = (lane % 8 + 1).astype(f32)
    m1 = (lane // 8 - kmax).astype(f32)
    m2 = lax.broadcasted_iota(jnp.int32, (8, grid_rows), 0).astype(f32) + 1.0
    weight = wave_weight(m0, m1, m2, cell_ref)
    up = weight * acc[0:8, :]
    down = weight * acc[8:16, :]
    flat = wave_weight(m0, m1, 0.0 * m0, cell_ref) * acc[16:17, :]
    for c in range(4):
        weight_ref[8 * c : 8 * c + 8, :] = up
        weight_ref[32 + 8 * c : 40 + 8 * c, :] = down
    weight_ref[64:72, :] = flat


def force_kernel(
    scale,
    half_ref,
    other_ref,
    lattice_ref,
    phase_ref,
    weight_ref,
    factor_ref,
    forces_ref,
    energy_ref,
    sums_ref,
):
    core = parity("wide")
    for part_ref, part in ((half_ref, core), (other_ref, 1 - core)):
        sums_ref[part, :, 0:128] = part_ref[0:72, :]
        sums_ref[part, :, 128:grid_rows] = jnp.transpose(part_ref[72:80, :])[0:72, :]
    real = sums_ref[0]
    imag = sums_ref[1]
    real_cos, real_sin, real_flat = real[0:32], real[32:64], real[64:72]
    imag_cos, imag_sin, imag_flat = imag[0:32], imag[32:64], imag[64:72]
    weight_up = weight_ref[0:32, :]
    weight_down = weight_ref[32:64, :]
    weight_flat = weight_ref[64:72, :]
    up_re, up_im = real_cos - imag_sin, imag_cos + real_sin
    down_re, down_im = real_cos + imag_sin, imag_cos - real_sin
    up_im_w, up_re_w = weight_up * up_im, weight_up * up_re
    down_im_w, down_re_w = weight_down * down_im, weight_down * down_re
    flat_im_w, flat_re_w = weight_flat * imag_flat, weight_flat * real_flat
    power = up_im_w * up_im + up_re_w * up_re + down_im_w * down_im + down_re_w * down_re
    flat_power = flat_im_w * imag_flat + flat_re_w * real_flat
    power = jnp.sum(power, axis=0, keepdims=True) + jnp.sum(flat_power, axis=0, keepdims=True)
    energy_ref[...] = (0.5 * scale) * jnp.sum(power, axis=1, keepdims=True)

    im_sum, im_diff = up_im_w + down_im_w, up_im_w - down_im_w
    re_sum, re_diff = up_re_w + down_re_w, down_re_w - up_re_w
    even_real = jnp.concatenate([im_sum, re_diff, flat_im_w], axis=0)
    even_imag = jnp.concatenate([-re_sum, -im_diff, -flat_re_w], axis=0)
    m2 = (lax.broadcasted_iota(jnp.int32, (32, grid_rows), 0) % 8 + 1).astype(f32)
    odd_real = jnp.concatenate([m2 * im_diff, -m2 * re_sum], axis=0)
    odd_imag = jnp.concatenate([m2 * re_diff, -m2 * im_sum], axis=0)
    lane = lax.broadcasted_iota(jnp.int32, (72, grid_rows), 1)
    m0 = (lane % 8 + 1).astype(f32)
    m1 = (lane // 8 - kmax).astype(f32)
    with_real = jnp.concatenate([even_real * m0, even_real * m1, odd_real], axis=0).astype(bf16)
    with_imag = jnp.concatenate([even_imag * m0, even_imag * m1, odd_imag], axis=0).astype(bf16)
    back = dot_nn(with_real, phase_ref[0]) + dot_nn(with_imag, phase_ref[1])
    lattice = lattice_ref[...]
    for axis in range(3):
        rows = 64 if axis == 2 else 72
        terms = lattice[0:rows] * back[72 * axis : 72 * axis + rows]
        gradient = jnp.sum(terms, axis=0, keepdims=True)
        forces_ref[axis : axis + 1, :] = factor_ref[axis : axis + 1, :] * gradient


def call(kernel, outs, *args, smem=(), scratch=(), cost=None):
    specs = [
        pl.BlockSpec(memory_space=pltpu.SMEM if i in smem else pltpu.VMEM)
        for i in range(len(args))
    ]
    return pl.pallas_call(
        kernel,
        out_shape=[jax.ShapeDtypeStruct(shape, dtype) for shape, dtype in outs],
        in_specs=specs,
        out_specs=[pl.BlockSpec(memory_space=pltpu.VMEM)] * len(outs),
        scratch_shapes=list(scratch),
        compiler_params=params,
        cost_estimate=cost,
    )(*args)


def matched(first, second, axis):
    count = lax.axis_size(axis)
    ways = (-1, 1) if axis == "wide" else (1, -1)
    one = lax.ppermute(first, axis, [(i, (i + ways[i % 2]) % count) for i in range(count)])
    two = lax.ppermute(second, axis, [(i, (i - ways[i % 2]) % count) for i in range(count)])
    return one, two


def flipped(block, wide_step, narrow_step):
    wide, narrow = lax.axis_size("wide"), lax.axis_size("narrow")
    pairs = [
        (w * narrow + z, (w ^ wide_step) * narrow + (z ^ narrow_step))
        for w in range(wide)
        for z in range(narrow)
    ]
    return lax.ppermute(block, ("wide", "narrow"), pairs)


def summed(send, keep, beside):
    wide_steps = [2**i for i in range(1, (lax.axis_size("wide") - 1).bit_length())]
    narrow_steps = [2**i for i in range((lax.axis_size("narrow") - 1).bit_length())]
    count = max(len(wide_steps), len(narrow_steps))
    block = keep + flipped(send, 1, 0)
    for i in range(count):
        last = i == count - 1
        if last:
            block, beside = lax.optimization_barrier((block, beside))
        wide_step = wide_steps[i] if i < len(wide_steps) else 0
        narrow_step = narrow_steps[i] if i < len(narrow_steps) else 0
        if wide_step and narrow_step:
            steps = [(0, narrow_step), (wide_step, narrow_step), (wide_step, 0)]
            if last:
                steps = [steps[1], steps[0], steps[2]]
            one, two, three = [flipped(block, *step) for step in steps]
            block = block + ((one + two) + three)
        else:
            block = block + flipped(block, wide_step, narrow_step)
    return block, flipped(block, 1, 0), beside


def per_device(
    fractions,
    cell_lengths,
    features,
    atom_counts,
    send_index,
    senders,
    radial,
    self_weight,
    message_weight,
    charge_weight,
    wave_numbers,
):
    atoms, width = features.shape
    ghosts = send_index.shape[1]
    rows = atoms + 4 * ghosts
    total_atoms = atoms * lax.axis_size("wide") * lax.axis_size("narrow")
    scale = 4.0 / math.sqrt(total_atoms * wave_numbers.shape[1])
    picked_outs = [((width, ghosts), f32)] * 2
    hidden_out = [((width, atoms), bf16)]
    sum_out = [((width, atoms), f32)]
    busy = pl.CostEstimate(flops=10**9, bytes_accessed=20 * 2**20, transcendentals=0)
    readout = charge_weight.T
    counts = atom_counts.reshape(1, 1)

    (opened,) = call(opening_kernel, [((8, 128), f32)], cost=busy)
    hidden, p2, p3 = call(
        first_kernel,
        hidden_out + picked_outs,
        opened,
        features,
        send_index,
        cost=busy,
    )
    g2, g3 = matched(p2, p3, "narrow")
    picks, p0, p1 = call(
        pick_kernel, [((atoms, 2 * ghosts), bf16)] + picked_outs, send_index, hidden, cost=busy
    )
    g0, g1 = matched(p0, p1, "wide")
    layers = self_weight.shape[0]
    near_edges, far_edges, self_rows, message_rows = call(
        edge_kernel,
        [
            ((rows - 2 * ghosts, atoms), bf16),
            ((2 * ghosts, atoms), bf16),
            ((layers, width, width), bf16),
            ((layers, width, 2 * width), bf16),
        ],
        senders,
        radial,
        self_weight,
        message_weight,
        cost=busy,
    )
    for layer in range(layers):
        own, gathered = call(
            functools.partial(local_kernel, layer), sum_out * 2, hidden, near_edges, self_rows, cost=busy
        )
        (gathered,) = call(near_kernel, sum_out, gathered, g2, g3, near_edges)
        if layer == layers - 1:
            break
        hidden, p2, p3 = call(
            functools.partial(layer_kernel, layer),
            hidden_out + picked_outs,
            hidden,
            own,
            gathered,
            g0,
            g1,
            far_edges,
            message_rows,
            picks,
            cost=busy,
        )
        g2, g3 = matched(p2, p3, "narrow")
        phases, third, p0, p1 = call(
            phase_kernel,
            [((2, grid_rows, atoms), bf16), ((24, atoms), f32)] + picked_outs,
            fractions,
            hidden,
            send_index,
            cost=busy,
        )
        g0, g1 = matched(p0, p1, "wide")
    send, lattice = call(
        functools.partial(last_kernel, layers - 1),
        [((half_rows, 128), f32), ((72, atoms), f32)],
        hidden,
        own,
        gathered,
        g0,
        g1,
        far_edges,
        message_rows,
        readout,
        counts,
        phases,
        third,
    )
    weights, factor, born_charges = call(
        functools.partial(weight_kernel, scale),
        [((72, grid_rows), f32), ((8, atoms), f32), ((3, atoms), f32)],
        cell_lengths,
        wave_numbers,
        lattice,
        third,
        counts,
        smem=(0,),
        scratch=[pltpu.VMEM((32, grid_rows), f32)],
        cost=busy,
    )
    (keep,) = call(keep_kernel, [((half_rows, 128), f32)], lattice, phases, cost=busy)
    half, other, (weights, factor) = summed(send, keep, (weights, factor))
    forces, energy = call(
        functools.partial(force_kernel, scale),
        [((3, atoms), f32), ((1, 1), f32)],
        half,
        other,
        lattice,
        phases,
        weights,
        factor,
        scratch=[pltpu.VMEM((2, 72, grid_rows), f32)],
    )
    return (forces, born_charges, energy[0, 0])


def solution(mesh):
    return jax.shard_map(
        per_device,
        mesh=mesh,
        in_specs=(
            P(None, ("wide", "narrow")),
            P(),
            P(("wide", "narrow"), None),
            P(("wide", "narrow")),
            P(("wide", "narrow"), None),
            P(None, ("wide", "narrow")),
            P(None, ("wide", "narrow")),
            P(),
            P(),
            P(),
            P(),
        ),
        out_specs=(P(None, ("wide", "narrow")), P(None, ("wide", "narrow")), P()),
        check_vma=False,
    )
```

```python
import functools
import math

import jax
import jax.numpy as jnp
from jax import lax
from jax.experimental import pallas as pl
from jax.experimental.pallas import tpu as pltpu
from jax.sharding import PartitionSpec as P

smearing = 0.5
two_pi = 2.0 * math.pi
kmax = 8
grid_rows = (2 * kmax + 1) * kmax
half_rows = 80
f32 = jnp.float32
bf16 = jnp.bfloat16
params = pltpu.CompilerParams(vmem_limit_bytes=48 * 1024 * 1024)


def dot_nn(a, b):
    return lax.dot_general(a, b, (((1,), (0,)), ((), ())), preferred_element_type=f32)


def dot_nt(a, b):
    return lax.dot_general(a, b, (((1,), (1,)), ((), ())), preferred_element_type=f32)


def parity(axis):
    return lax.rem(lax.axis_index(axis), 2)


def block_order(axis):
    odd = parity(axis) if axis == "wide" else 1 - parity(axis)
    first = 0 if axis == "wide" else 2
    return first + odd, first + 1 - odd


def pick_matrix(index_ref, block, atoms):
    row_ids = lax.broadcasted_iota(jnp.int32, (atoms, index_ref.shape[1]), 0)
    return jnp.where(row_ids == index_ref[pl.ds(block, 1), :], 1.0, 0.0).astype(bf16)


def opening_kernel(opened_ref):
    opened_ref[...] = jnp.zeros(opened_ref.shape, f32)


def first_kernel(opened_ref, features_ref, index_ref, hidden_ref, pa, pb):
    hidden = jnp.transpose(features_ref[...].astype(f32)).astype(bf16)
    hidden_ref[...] = hidden
    for block, picked_ref in zip(block_order("narrow"), (pa, pb)):
        picked_ref[...] = dot_nn(hidden, pick_matrix(index_ref, block, hidden.shape[1]))


def wide_kernel(hidden_ref, index_ref, pa, pb):
    hidden = hidden_ref[...]
    for block, picked_ref in zip(block_order("wide"), (pa, pb)):
        picked_ref[...] = dot_nn(hidden, pick_matrix(index_ref, block, hidden.shape[1]))


def edge_tiles(senders_ref, radial_ref, edges_ref, local, axis):
    slots, atoms = senders_ref.shape
    rows = 128
    lanes = 128
    row_ids = lax.broadcasted_iota(jnp.int32, (rows, lanes), 0).astype(f32).astype(bf16)
    ghosts = (edges_ref.shape[0] - local) // 2
    one, two = block_order(axis)
    skip_one = atoms + one * ghosts - local
    skip_two = atoms + two * ghosts - local - ghosts

    def one_tile(tile, carry):
        first = pl.multiple_of(tile * rows, rows)
        skip = jnp.where(first < local, 0, jnp.where(first < local + ghosts, skip_one, skip_two))
        sender = first + skip
        for part in range(atoms // lanes):
            window = pl.ds(part * lanes, lanes)
            local_row = jnp.clip(senders_ref[:, window] - sender, -1, rows)
            local_row = local_row.astype(f32).astype(bf16)
            weight = radial_ref[:, window].astype(bf16)
            total = jnp.zeros((rows, lanes), bf16)
            for slot in range(slots):
                total = total + jnp.where(
                    row_ids == local_row[slot : slot + 1, :],
                    weight[slot : slot + 1, :],
                    jnp.zeros((), bf16),
                )
            edges_ref[pl.ds(first, rows), window] = total
        return carry

    lax.fori_loop(0, edges_ref.shape[0] // rows, one_tile, 0)


def pick_kernel(index_ref, hidden_ref, pick_ref, pa, pb):
    wide_kernel(hidden_ref, index_ref, pa, pb)
    ghosts = index_ref.shape[1]
    for i, block in enumerate(block_order("narrow")):
        pick_ref[:, i * ghosts : (i + 1) * ghosts] = pick_matrix(
            index_ref, block, hidden_ref.shape[1]
        )


def edge_kernel(
    senders_ref, radial_ref, self_ref, message_ref, near_ref, far_ref, self_rows_ref, message_rows_ref
):
    edge_tiles(senders_ref, radial_ref, near_ref, senders_ref.shape[1], "narrow")
    edge_tiles(senders_ref, radial_ref, far_ref, 0, "wide")
    for layer in range(self_ref.shape[0]):
        self_rows_ref[layer] = jnp.transpose(self_ref[layer].astype(f32)).astype(bf16)
        message = jnp.transpose(message_ref[layer].astype(f32)).astype(bf16)
        message_rows_ref[layer] = jnp.concatenate([message, message], axis=1)


def local_kernel(layer, hidden_ref, edges_ref, self_rows_ref, own_ref, gathered_ref):
    hidden = hidden_ref[...]
    own_ref[...] = dot_nn(self_rows_ref[layer], hidden)
    gathered_ref[...] = dot_nn(hidden, edges_ref[0 : hidden.shape[1], :])


def near_kernel(gathered_ref, g2, g3, edges_ref, sum_ref):
    received = jnp.concatenate([g2[...].astype(bf16), g3[...].astype(bf16)], axis=1)
    local = edges_ref.shape[0] - received.shape[1]
    sum_ref[...] = gathered_ref[...] + dot_nn(received, edges_ref[local:, :])


def interact(layer, hidden_ref, own_ref, gathered_ref, g0, g1, edges_ref, message_rows_ref):
    received = jnp.concatenate([g0[...].astype(bf16), g1[...].astype(bf16)], axis=1)
    gathered = gathered_ref[...] + dot_nn(received, edges_ref[...])
    high = gathered.astype(bf16)
    low = (gathered - high.astype(f32)).astype(bf16)
    total = own_ref[...] + dot_nn(message_rows_ref[layer], jnp.concatenate([high, low], axis=0))
    gate = 0.5 * total * (1.0 + jnp.tanh(0.5 * total))
    return (hidden_ref[...].astype(f32) + gate).astype(bf16)


def layer_kernel(
    layer, hidden_ref, own_ref, gathered_ref, g0, g1, edges_ref, message_rows_ref, pick_ref, out_ref, p2, p3
):
    hidden = interact(layer, hidden_ref, own_ref, gathered_ref, g0, g1, edges_ref, message_rows_ref)
    out_ref[...] = hidden
    picked = dot_nn(hidden, pick_ref[...])
    ghosts = p2.shape[1]
    p2[...] = picked[:, 0:ghosts]
    p3[...] = picked[:, ghosts:]


def structure_part(lattice, phase_ref, part, out_ref):
    phases = phase_ref[part]
    out_ref[0:72, :] = dot_nt(lattice, phases[0:128, :])
    out_ref[72:80, 0:72] = dot_nt(phases[128:grid_rows, :], lattice)
    out_ref[72:80, 72:128] = jnp.zeros((8, 56), f32)


def last_kernel(
    layer,
    hidden_ref,
    own_ref,
    gathered_ref,
    g0,
    g1,
    edges_ref,
    message_rows_ref,
    readout_ref,
    count_ref,
    phase_ref,
    third_ref,
    send_ref,
    lattice_ref,
):
    hidden = interact(layer, hidden_ref, own_ref, gathered_ref, g0, g1, edges_ref, message_rows_ref)
    atoms = hidden.shape[1]
    slot_ids = lax.broadcasted_iota(jnp.int32, (8, atoms), 1)
    readout = readout_ref[...].astype(f32)
    readout = jnp.concatenate([readout, jnp.zeros_like(readout)], axis=0).astype(bf16)
    charges = jnp.where(slot_ids < count_ref[...], dot_nn(readout, hidden), 0.0)
    cosine = third_ref[0:8, :]
    sine = third_ref[8:16, :]
    rows = [charges[c : c + 1, :] * cosine for c in range(4)]
    rows = rows + [charges[c : c + 1, :] * sine for c in range(4)]
    lattice = jnp.concatenate(rows + [charges], axis=0)
    lattice_ref[...] = lattice
    structure_part(lattice.astype(bf16), phase_ref, 1 - parity("wide"), send_ref)


def keep_kernel(lattice_ref, phase_ref, keep_ref):
    structure_part(lattice_ref[...].astype(bf16), phase_ref, parity("wide"), keep_ref)


def wave_weight(m0, m1, m2, cell_ref):
    w0 = two_pi * m0 / cell_ref[0]
    w1 = two_pi * m1 / cell_ref[1]
    w2 = two_pi * m2 / cell_ref[2]
    squared = w0 * w0 + w1 * w1 + w2 * w2
    return jnp.exp(-0.5 * smearing * smearing * squared) / squared


def phase_kernel(fractions_ref, hidden_ref, index_ref, phase_ref, third_ref, p0, p1):
    wide_kernel(hidden_ref, index_ref, p0, p1)
    atoms = fractions_ref.shape[1]
    orders = lax.broadcasted_iota(jnp.int32, (8, atoms), 0).astype(f32) + 1.0
    cosines, sines = [], []
    for axis in range(3):
        turns = orders * fractions_ref[axis : axis + 1, :]
        angle = two_pi * (turns - jnp.round(turns))
        cosines.append(jnp.cos(angle))
        sines.append(jnp.sin(angle))
    third_ref[0:8, :] = cosines[2]
    third_ref[8:16, :] = sines[2]
    for axis in range(3):
        third_ref[16 + axis : 17 + axis, :] = cosines[axis][0:1, :]
    c0, s0 = cosines[0], sines[0]
    for m in range(-kmax, kmax + 1):
        window = pl.ds((m + kmax) * kmax, kmax)
        if m == 0:
            re, im = c0, s0
        else:
            row = abs(m) - 1
            c1 = cosines[1][row : row + 1, :]
            s1 = sines[1][row : row + 1, :]
            if m < 0:
                s1 = -s1
            re, im = c0 * c1 - s0 * s1, s0 * c1 + c0 * s1
        phase_ref[0, window, :] = re.astype(bf16)
        phase_ref[1, window, :] = im.astype(bf16)


def weight_kernel(
    scale,
    cell_ref,
    numbers_ref,
    lattice_ref,
    third_ref,
    count_ref,
    weight_ref,
    factor_ref,
    born_ref,
    acc,
):
    alive = lax.broadcasted_iota(jnp.int32, (1, lattice_ref.shape[1]), 1) < count_ref[...]
    for axis in range(3):
        factor_ref[axis : axis + 1, :] = jnp.where(alive, -(two_pi * scale / cell_ref[axis]), 0.0)
    total = jnp.sum(lattice_ref[64:68, :], axis=0, keepdims=True)
    born_ref[...] = total * third_ref[16:19, :]
    acc[...] = jnp.zeros_like(acc)
    width = math.gcd(numbers_ref.shape[1], 1024)
    plane_ids = lax.broadcasted_iota(jnp.int32, (grid_rows, width), 0)
    third_ids = lax.broadcasted_iota(jnp.int32, (32, width), 0)
    third_ids = jnp.where(
        third_ids < 8, third_ids + 1, jnp.where(third_ids < 16, 7 - third_ids, (third_ids - 16) * 64)
    )

    def count(step, carry):
        window = pl.ds(pl.multiple_of(step * width, width), width)
        numbers = numbers_ref[:, window]
        plane = (numbers[1:2, :] + kmax) * kmax + numbers[0:1, :] - 1
        in_plane = jnp.where(plane_ids == plane, 1.0, 0.0).astype(bf16)
        in_third = jnp.where(third_ids == numbers[2:3, :], 1.0, 0.0).astype(bf16)
        acc[...] += dot_nt(in_third, in_plane)
        return carry

    lax.fori_loop(0, numbers_ref.shape[1] // width, count, 0)
    lane = lax.broadcasted_iota(jnp.int32, (8, grid_rows), 1)
    m0 = (lane % 8 + 1).astype(f32)
    m1 = (lane // 8 - kmax).astype(f32)
    m2 = lax.broadcasted_iota(jnp.int32, (8, grid_rows), 0).astype(f32) + 1.0
    weight = wave_weight(m0, m1, m2, cell_ref)
    up = weight * acc[0:8, :]
    down = weight * acc[8:16, :]
    flat = wave_weight(m0, m1, 0.0 * m0, cell_ref) * acc[16:17, :]
    for c in range(4):
        weight_ref[8 * c : 8 * c + 8, :] = up
        weight_ref[32 + 8 * c : 40 + 8 * c, :] = down
    weight_ref[64:72, :] = flat


def force_kernel(
    scale,
    half_ref,
    other_ref,
    lattice_ref,
    phase_ref,
    weight_ref,
    factor_ref,
    forces_ref,
    energy_ref,
    sums_ref,
):
    core = parity("wide")
    for part_ref, part in ((half_ref, core), (other_ref, 1 - core)):
        sums_ref[part, :, 0:128] = part_ref[0:72, :]
        sums_ref[part, :, 128:grid_rows] = jnp.transpose(part_ref[72:80, :])[0:72, :]
    real = sums_ref[0]
    imag = sums_ref[1]
    real_cos, real_sin, real_flat = real[0:32], real[32:64], real[64:72]
    imag_cos, imag_sin, imag_flat = imag[0:32], imag[32:64], imag[64:72]
    weight_up = weight_ref[0:32, :]
    weight_down = weight_ref[32:64, :]
    weight_flat = weight_ref[64:72, :]
    up_re, up_im = real_cos - imag_sin, imag_cos + real_sin
    down_re, down_im = real_cos + imag_sin, imag_cos - real_sin
    up_im_w, up_re_w = weight_up * up_im, weight_up * up_re
    down_im_w, down_re_w = weight_down * down_im, weight_down * down_re
    flat_im_w, flat_re_w = weight_flat * imag_flat, weight_flat * real_flat
    power = up_im_w * up_im + up_re_w * up_re + down_im_w * down_im + down_re_w * down_re
    flat_power = flat_im_w * imag_flat + flat_re_w * real_flat
    power = jnp.sum(power, axis=0, keepdims=True) + jnp.sum(flat_power, axis=0, keepdims=True)
    energy_ref[...] = (0.5 * scale) * jnp.sum(power, axis=1, keepdims=True)

    im_sum, im_diff = up_im_w + down_im_w, up_im_w - down_im_w
    re_sum, re_diff = up_re_w + down_re_w, down_re_w - up_re_w
    even_real = jnp.concatenate([im_sum, re_diff, flat_im_w], axis=0)
    even_imag = jnp.concatenate([-re_sum, -im_diff, -flat_re_w], axis=0)
    m2 = (lax.broadcasted_iota(jnp.int32, (32, grid_rows), 0) % 8 + 1).astype(f32)
    odd_real = jnp.concatenate([m2 * im_diff, -m2 * re_sum], axis=0)
    odd_imag = jnp.concatenate([m2 * re_diff, -m2 * im_sum], axis=0)
    lane = lax.broadcasted_iota(jnp.int32, (72, grid_rows), 1)
    m0 = (lane % 8 + 1).astype(f32)
    m1 = (lane // 8 - kmax).astype(f32)
    with_real = jnp.concatenate([even_real * m0, even_real * m1, odd_real], axis=0).astype(bf16)
    with_imag = jnp.concatenate([even_imag * m0, even_imag * m1, odd_imag], axis=0).astype(bf16)
    back = dot_nn(with_real, phase_ref[0]) + dot_nn(with_imag, phase_ref[1])
    lattice = lattice_ref[...]
    for axis in range(3):
        rows = 64 if axis == 2 else 72
        terms = lattice[0:rows] * back[72 * axis : 72 * axis + rows]
        gradient = jnp.sum(terms, axis=0, keepdims=True)
        forces_ref[axis : axis + 1, :] = factor_ref[axis : axis + 1, :] * gradient


def call(kernel, outs, *args, smem=(), scratch=(), cost=None):
    specs = [
        pl.BlockSpec(memory_space=pltpu.SMEM if i in smem else pltpu.VMEM)
        for i in range(len(args))
    ]
    return pl.pallas_call(
        kernel,
        out_shape=[jax.ShapeDtypeStruct(shape, dtype) for shape, dtype in outs],
        in_specs=specs,
        out_specs=[pl.BlockSpec(memory_space=pltpu.VMEM)] * len(outs),
        scratch_shapes=list(scratch),
        compiler_params=params,
        cost_estimate=cost,
    )(*args)


def matched(first, second, axis):
    count = lax.axis_size(axis)
    ways = (-1, 1) if axis == "wide" else (1, -1)
    one = lax.ppermute(first, axis, [(i, (i + ways[i % 2]) % count) for i in range(count)])
    two = lax.ppermute(second, axis, [(i, (i - ways[i % 2]) % count) for i in range(count)])
    return one, two


def flipped(block, wide_step, narrow_step):
    wide, narrow = lax.axis_size("wide"), lax.axis_size("narrow")
    pairs = [
        (w * narrow + z, (w ^ wide_step) * narrow + (z ^ narrow_step))
        for w in range(wide)
        for z in range(narrow)
    ]
    return lax.ppermute(block, ("wide", "narrow"), pairs)


def summed(send, keep, beside):
    stages = []
    for axis, step in (("wide", 2), ("narrow", 1)):
        while step < lax.axis_size(axis):
            if 2 * step < lax.axis_size(axis):
                stage = (2 * step, 3 * step, step) if axis == "wide" else (3 * step, 2 * step, step)
            else:
                stage = (step,)
            stages.append([(bits, 0) if axis == "wide" else (0, bits) for bits in stage])
            step *= 4
    block = keep + flipped(send, 1, 0)
    for i, stage in enumerate(stages):
        if i == len(stages) - 1:
            block, beside = lax.optimization_barrier((block, beside))
        received = [flipped(block, *steps) for steps in stage]
        block = block + functools.reduce(jnp.add, received)
    return block, flipped(block, 1, 0), beside


def per_device(
    fractions,
    cell_lengths,
    features,
    atom_counts,
    send_index,
    senders,
    radial,
    self_weight,
    message_weight,
    charge_weight,
    wave_numbers,
):
    atoms, width = features.shape
    ghosts = send_index.shape[1]
    rows = atoms + 4 * ghosts
    total_atoms = atoms * lax.axis_size("wide") * lax.axis_size("narrow")
    scale = 4.0 / math.sqrt(total_atoms * wave_numbers.shape[1])
    picked_outs = [((width, ghosts), f32)] * 2
    hidden_out = [((width, atoms), bf16)]
    sum_out = [((width, atoms), f32)]
    busy = pl.CostEstimate(flops=10**9, bytes_accessed=20 * 2**20, transcendentals=0)
    readout = charge_weight.T
    counts = atom_counts.reshape(1, 1)

    (opened,) = call(opening_kernel, [((8, 128), f32)], cost=busy)
    hidden, p2, p3 = call(
        first_kernel,
        hidden_out + picked_outs,
        opened,
        features,
        send_index,
        cost=busy,
    )
    g2, g3 = matched(p2, p3, "narrow")
    picks, p0, p1 = call(
        pick_kernel, [((atoms, 2 * ghosts), bf16)] + picked_outs, send_index, hidden, cost=busy
    )
    g0, g1 = matched(p0, p1, "wide")
    layers = self_weight.shape[0]
    near_edges, far_edges, self_rows, message_rows = call(
        edge_kernel,
        [
            ((rows - 2 * ghosts, atoms), bf16),
            ((2 * ghosts, atoms), bf16),
            ((layers, width, width), bf16),
            ((layers, width, 2 * width), bf16),
        ],
        senders,
        radial,
        self_weight,
        message_weight,
        cost=busy,
    )
    for layer in range(layers):
        own, gathered = call(
            functools.partial(local_kernel, layer), sum_out * 2, hidden, near_edges, self_rows, cost=busy
        )
        (gathered,) = call(near_kernel, sum_out, gathered, g2, g3, near_edges)
        if layer == layers - 1:
            break
        hidden, p2, p3 = call(
            functools.partial(layer_kernel, layer),
            hidden_out + picked_outs,
            hidden,
            own,
            gathered,
            g0,
            g1,
            far_edges,
            message_rows,
            picks,
            cost=busy,
        )
        g2, g3 = matched(p2, p3, "narrow")
        phases, third, p0, p1 = call(
            phase_kernel,
            [((2, grid_rows, atoms), bf16), ((24, atoms), f32)] + picked_outs,
            fractions,
            hidden,
            send_index,
            cost=busy,
        )
        g0, g1 = matched(p0, p1, "wide")
    send, lattice = call(
        functools.partial(last_kernel, layers - 1),
        [((half_rows, 128), f32), ((72, atoms), f32)],
        hidden,
        own,
        gathered,
        g0,
        g1,
        far_edges,
        message_rows,
        readout,
        counts,
        phases,
        third,
    )
    weights, factor, born_charges = call(
        functools.partial(weight_kernel, scale),
        [((72, grid_rows), f32), ((8, atoms), f32), ((3, atoms), f32)],
        cell_lengths,
        wave_numbers,
        lattice,
        third,
        counts,
        smem=(0,),
        scratch=[pltpu.VMEM((32, grid_rows), f32)],
        cost=busy,
    )
    (keep,) = call(keep_kernel, [((half_rows, 128), f32)], lattice, phases, cost=busy)
    half, other, (weights, factor) = summed(send, keep, (weights, factor))
    forces, energy = call(
        functools.partial(force_kernel, scale),
        [((3, atoms), f32), ((1, 1), f32)],
        half,
        other,
        lattice,
        phases,
        weights,
        factor,
        scratch=[pltpu.VMEM((2, 72, grid_rows), f32)],
    )
    return (forces, born_charges, energy[0, 0])


def solution(mesh):
    return jax.shard_map(
        per_device,
        mesh=mesh,
        in_specs=(
            P(None, ("wide", "narrow")),
            P(),
            P(("wide", "narrow"), None),
            P(("wide", "narrow")),
            P(("wide", "narrow"), None),
            P(None, ("wide", "narrow")),
            P(None, ("wide", "narrow")),
            P(),
            P(),
            P(),
            P(),
        ),
        out_specs=(P(None, ("wide", "narrow")), P(None, ("wide", "narrow")), P()),
        check_vma=False,
    )
```

```python
import functools
import math

import jax
import jax.numpy as jnp
from jax import lax
from jax.experimental import pallas as pl
from jax.experimental.pallas import tpu as pltpu
from jax.sharding import PartitionSpec as P

smearing = 0.5
two_pi = 2.0 * math.pi
kmax = 8
grid_rows = (2 * kmax + 1) * kmax
half_rows = 80
f32 = jnp.float32
bf16 = jnp.bfloat16
params = pltpu.CompilerParams(vmem_limit_bytes=48 * 1024 * 1024)


def dot_nn(a, b):
    return lax.dot_general(a, b, (((1,), (0,)), ((), ())), preferred_element_type=f32)


def dot_nt(a, b):
    return lax.dot_general(a, b, (((1,), (1,)), ((), ())), preferred_element_type=f32)


def parity(axis):
    return lax.rem(lax.axis_index(axis), 2)


def block_order(axis):
    odd = parity(axis) if axis == "wide" else 1 - parity(axis)
    first = 0 if axis == "wide" else 2
    return first + odd, first + 1 - odd


def pick_matrix(index_ref, block, atoms):
    row_ids = lax.broadcasted_iota(jnp.int32, (atoms, index_ref.shape[1]), 0)
    return jnp.where(row_ids == index_ref[pl.ds(block, 1), :], 1.0, 0.0).astype(bf16)


def opening_kernel(opened_ref):
    opened_ref[...] = jnp.zeros(opened_ref.shape, f32)


def first_kernel(opened_ref, features_ref, index_ref, hidden_ref, pa, pb):
    hidden = jnp.transpose(features_ref[...].astype(f32)).astype(bf16)
    hidden_ref[...] = hidden
    for block, picked_ref in zip(block_order("narrow"), (pa, pb)):
        picked_ref[...] = dot_nn(hidden, pick_matrix(index_ref, block, hidden.shape[1]))


def wide_kernel(hidden_ref, index_ref, pa, pb):
    hidden = hidden_ref[...]
    for block, picked_ref in zip(block_order("wide"), (pa, pb)):
        picked_ref[...] = dot_nn(hidden, pick_matrix(index_ref, block, hidden.shape[1]))


def edge_tiles(senders_ref, radial_ref, edges_ref, local, axis):
    slots, atoms = senders_ref.shape
    rows = 128
    lanes = 128
    row_ids = lax.broadcasted_iota(jnp.int32, (rows, lanes), 0).astype(f32).astype(bf16)
    ghosts = (edges_ref.shape[0] - local) // 2
    one, two = block_order(axis)
    skip_one = atoms + one * ghosts - local
    skip_two = atoms + two * ghosts - local - ghosts

    def one_tile(tile, carry):
        first = pl.multiple_of(tile * rows, rows)
        skip = jnp.where(first < local, 0, jnp.where(first < local + ghosts, skip_one, skip_two))
        sender = first + skip
        for part in range(atoms // lanes):
            window = pl.ds(part * lanes, lanes)
            local_row = jnp.clip(senders_ref[:, window] - sender, -1, rows)
            local_row = local_row.astype(f32).astype(bf16)
            weight = radial_ref[:, window].astype(bf16)
            total = jnp.zeros((rows, lanes), bf16)
            for slot in range(slots):
                total = total + jnp.where(
                    row_ids == local_row[slot : slot + 1, :],
                    weight[slot : slot + 1, :],
                    jnp.zeros((), bf16),
                )
            edges_ref[pl.ds(first, rows), window] = total
        return carry

    lax.fori_loop(0, edges_ref.shape[0] // rows, one_tile, 0)


def edge_kernel(
    senders_ref,
    radial_ref,
    self_ref,
    message_ref,
    index_ref,
    near_ref,
    far_ref,
    self_rows_ref,
    message_rows_ref,
    pick_ref,
):
    ghosts = index_ref.shape[1]
    for i, block in enumerate(block_order("narrow")):
        pick_ref[:, i * ghosts : (i + 1) * ghosts] = pick_matrix(
            index_ref, block, senders_ref.shape[1]
        )
    edge_tiles(senders_ref, radial_ref, near_ref, senders_ref.shape[1], "narrow")
    edge_tiles(senders_ref, radial_ref, far_ref, 0, "wide")
    for layer in range(self_ref.shape[0]):
        self_rows_ref[layer] = jnp.transpose(self_ref[layer].astype(f32)).astype(bf16)
        message = jnp.transpose(message_ref[layer].astype(f32)).astype(bf16)
        message_rows_ref[layer] = jnp.concatenate([message, message], axis=1)


def local_kernel(layer, hidden_ref, edges_ref, self_rows_ref, own_ref, gathered_ref):
    hidden = hidden_ref[...]
    own_ref[...] = dot_nn(self_rows_ref[layer], hidden)
    gathered_ref[...] = dot_nn(hidden, edges_ref[0 : hidden.shape[1], :])


def near_kernel(gathered_ref, g2, g3, edges_ref, sum_ref):
    received = jnp.concatenate([g2[...].astype(bf16), g3[...].astype(bf16)], axis=1)
    local = edges_ref.shape[0] - received.shape[1]
    sum_ref[...] = gathered_ref[...] + dot_nn(received, edges_ref[local:, :])


def interact(layer, hidden_ref, own_ref, gathered_ref, g0, g1, edges_ref, message_rows_ref):
    received = jnp.concatenate([g0[...].astype(bf16), g1[...].astype(bf16)], axis=1)
    gathered = gathered_ref[...] + dot_nn(received, edges_ref[...])
    high = gathered.astype(bf16)
    low = (gathered - high.astype(f32)).astype(bf16)
    total = own_ref[...] + dot_nn(message_rows_ref[layer], jnp.concatenate([high, low], axis=0))
    gate = 0.5 * total * (1.0 + jnp.tanh(0.5 * total))
    return (hidden_ref[...].astype(f32) + gate).astype(bf16)


def layer_kernel(
    layer, hidden_ref, own_ref, gathered_ref, g0, g1, edges_ref, message_rows_ref, pick_ref, out_ref, p2, p3
):
    hidden = interact(layer, hidden_ref, own_ref, gathered_ref, g0, g1, edges_ref, message_rows_ref)
    out_ref[...] = hidden
    picked = dot_nn(hidden, pick_ref[...])
    ghosts = p2.shape[1]
    p2[...] = picked[:, 0:ghosts]
    p3[...] = picked[:, ghosts:]


def structure_part(lattice, phase_ref, part, out_ref):
    phases = phase_ref[part]
    out_ref[0:72, :] = dot_nt(lattice, phases[0:128, :])
    out_ref[72:80, 0:72] = dot_nt(phases[128:grid_rows, :], lattice)
    out_ref[72:80, 72:128] = jnp.zeros((8, 56), f32)


def last_kernel(
    layer,
    hidden_ref,
    own_ref,
    gathered_ref,
    g0,
    g1,
    edges_ref,
    message_rows_ref,
    readout_ref,
    count_ref,
    phase_ref,
    third_ref,
    send_ref,
    lattice_ref,
):
    hidden = interact(layer, hidden_ref, own_ref, gathered_ref, g0, g1, edges_ref, message_rows_ref)
    atoms = hidden.shape[1]
    slot_ids = lax.broadcasted_iota(jnp.int32, (8, atoms), 1)
    readout = readout_ref[...].astype(f32)
    readout = jnp.concatenate([readout, jnp.zeros_like(readout)], axis=0).astype(bf16)
    charges = jnp.where(slot_ids < count_ref[...], dot_nn(readout, hidden), 0.0)
    cosine = third_ref[0:8, :]
    sine = third_ref[8:16, :]
    rows = [charges[c : c + 1, :] * cosine for c in range(4)]
    rows = rows + [charges[c : c + 1, :] * sine for c in range(4)]
    lattice = jnp.concatenate(rows + [charges], axis=0)
    lattice_ref[...] = lattice
    structure_part(lattice.astype(bf16), phase_ref, 1 - parity("wide"), send_ref)


def keep_kernel(lattice_ref, phase_ref, keep_ref):
    structure_part(lattice_ref[...].astype(bf16), phase_ref, parity("wide"), keep_ref)


def wave_weight(m0, m1, m2, cell_ref):
    w0 = two_pi * m0 / cell_ref[0]
    w1 = two_pi * m1 / cell_ref[1]
    w2 = two_pi * m2 / cell_ref[2]
    squared = w0 * w0 + w1 * w1 + w2 * w2
    return jnp.exp(-0.5 * smearing * smearing * squared) / squared


def phase_kernel(fractions_ref, after_ref, phase_ref, third_ref):
    atoms = fractions_ref.shape[1]
    orders = lax.broadcasted_iota(jnp.int32, (8, atoms), 0).astype(f32) + 1.0
    cosines, sines = [], []
    for axis in range(3):
        turns = orders * fractions_ref[axis : axis + 1, :]
        angle = two_pi * (turns - jnp.round(turns))
        cosines.append(jnp.cos(angle))
        sines.append(jnp.sin(angle))
    third_ref[0:8, :] = cosines[2]
    third_ref[8:16, :] = sines[2]
    for axis in range(3):
        third_ref[16 + axis : 17 + axis, :] = cosines[axis][0:1, :]
    c0, s0 = cosines[0], sines[0]
    for m in range(-kmax, kmax + 1):
        window = pl.ds((m + kmax) * kmax, kmax)
        if m == 0:
            re, im = c0, s0
        else:
            row = abs(m) - 1
            c1 = cosines[1][row : row + 1, :]
            s1 = sines[1][row : row + 1, :]
            if m < 0:
                s1 = -s1
            re, im = c0 * c1 - s0 * s1, s0 * c1 + c0 * s1
        phase_ref[0, window, :] = re.astype(bf16)
        phase_ref[1, window, :] = im.astype(bf16)


def weight_kernel(
    scale,
    cell_ref,
    numbers_ref,
    lattice_ref,
    third_ref,
    count_ref,
    weight_ref,
    factor_ref,
    born_ref,
    acc,
):
    alive = lax.broadcasted_iota(jnp.int32, (1, lattice_ref.shape[1]), 1) < count_ref[...]
    for axis in range(3):
        factor_ref[axis : axis + 1, :] = jnp.where(alive, -(two_pi * scale / cell_ref[axis]), 0.0)
    total = jnp.sum(lattice_ref[64:68, :], axis=0, keepdims=True)
    born_ref[...] = total * third_ref[16:19, :]
    acc[...] = jnp.zeros_like(acc)
    width = math.gcd(numbers_ref.shape[1], 1024)
    plane_ids = lax.broadcasted_iota(jnp.int32, (grid_rows, width), 0)
    third_ids = lax.broadcasted_iota(jnp.int32, (32, width), 0)
    third_ids = jnp.where(
        third_ids < 8, third_ids + 1, jnp.where(third_ids < 16, 7 - third_ids, (third_ids - 16) * 64)
    )

    def count(step, carry):
        window = pl.ds(pl.multiple_of(step * width, width), width)
        numbers = numbers_ref[:, window]
        plane = (numbers[1:2, :] + kmax) * kmax + numbers[0:1, :] - 1
        in_plane = jnp.where(plane_ids == plane, 1.0, 0.0).astype(bf16)
        in_third = jnp.where(third_ids == numbers[2:3, :], 1.0, 0.0).astype(bf16)
        acc[...] += dot_nt(in_third, in_plane)
        return carry

    lax.fori_loop(0, numbers_ref.shape[1] // width, count, 0)
    lane = lax.broadcasted_iota(jnp.int32, (8, grid_rows), 1)
    m0 = (lane % 8 + 1).astype(f32)
    m1 = (lane // 8 - kmax).astype(f32)
    m2 = lax.broadcasted_iota(jnp.int32, (8, grid_rows), 0).astype(f32) + 1.0
    weight = wave_weight(m0, m1, m2, cell_ref)
    up = weight * acc[0:8, :]
    down = weight * acc[8:16, :]
    flat = wave_weight(m0, m1, 0.0 * m0, cell_ref) * acc[16:17, :]
    for c in range(4):
        weight_ref[8 * c : 8 * c + 8, :] = up
        weight_ref[32 + 8 * c : 40 + 8 * c, :] = down
    weight_ref[64:72, :] = flat


def force_kernel(
    scale,
    half_ref,
    other_ref,
    lattice_ref,
    phase_ref,
    weight_ref,
    factor_ref,
    forces_ref,
    energy_ref,
    sums_ref,
):
    core = parity("wide")
    for part_ref, part in ((half_ref, core), (other_ref, 1 - core)):
        sums_ref[part, :, 0:128] = part_ref[0:72, :]
        sums_ref[part, :, 128:grid_rows] = jnp.transpose(part_ref[72:80, :])[0:72, :]
    real = sums_ref[0]
    imag = sums_ref[1]
    real_cos, real_sin, real_flat = real[0:32], real[32:64], real[64:72]
    imag_cos, imag_sin, imag_flat = imag[0:32], imag[32:64], imag[64:72]
    weight_up = weight_ref[0:32, :]
    weight_down = weight_ref[32:64, :]
    weight_flat = weight_ref[64:72, :]
    up_re, up_im = real_cos - imag_sin, imag_cos + real_sin
    down_re, down_im = real_cos + imag_sin, imag_cos - real_sin
    up_im_w, up_re_w = weight_up * up_im, weight_up * up_re
    down_im_w, down_re_w = weight_down * down_im, weight_down * down_re
    flat_im_w, flat_re_w = weight_flat * imag_flat, weight_flat * real_flat
    power = up_im_w * up_im + up_re_w * up_re + down_im_w * down_im + down_re_w * down_re
    flat_power = flat_im_w * imag_flat + flat_re_w * real_flat
    power = jnp.sum(power, axis=0, keepdims=True) + jnp.sum(flat_power, axis=0, keepdims=True)
    energy_ref[...] = (0.5 * scale) * jnp.sum(power, axis=1, keepdims=True)

    im_sum, im_diff = up_im_w + down_im_w, up_im_w - down_im_w
    re_sum, re_diff = up_re_w + down_re_w, down_re_w - up_re_w
    even_real = jnp.concatenate([im_sum, re_diff, flat_im_w], axis=0)
    even_imag = jnp.concatenate([-re_sum, -im_diff, -flat_re_w], axis=0)
    m2 = (lax.broadcasted_iota(jnp.int32, (32, grid_rows), 0) % 8 + 1).astype(f32)
    odd_real = jnp.concatenate([m2 * im_diff, -m2 * re_sum], axis=0)
    odd_imag = jnp.concatenate([m2 * re_diff, -m2 * im_sum], axis=0)
    lane = lax.broadcasted_iota(jnp.int32, (72, grid_rows), 1)
    m0 = (lane % 8 + 1).astype(f32)
    m1 = (lane // 8 - kmax).astype(f32)
    with_real = jnp.concatenate([even_real * m0, even_real * m1, odd_real], axis=0).astype(bf16)
    with_imag = jnp.concatenate([even_imag * m0, even_imag * m1, odd_imag], axis=0).astype(bf16)
    back = dot_nn(with_real, phase_ref[0]) + dot_nn(with_imag, phase_ref[1])
    lattice = lattice_ref[...]
    for axis in range(3):
        rows = 64 if axis == 2 else 72
        terms = lattice[0:rows] * back[72 * axis : 72 * axis + rows]
        gradient = jnp.sum(terms, axis=0, keepdims=True)
        forces_ref[axis : axis + 1, :] = factor_ref[axis : axis + 1, :] * gradient


def call(kernel, outs, *args, smem=(), scratch=(), cost=None):
    specs = [
        pl.BlockSpec(memory_space=pltpu.SMEM if i in smem else pltpu.VMEM)
        for i in range(len(args))
    ]
    return pl.pallas_call(
        kernel,
        out_shape=[jax.ShapeDtypeStruct(shape, dtype) for shape, dtype in outs],
        in_specs=specs,
        out_specs=[pl.BlockSpec(memory_space=pltpu.VMEM)] * len(outs),
        scratch_shapes=list(scratch),
        compiler_params=params,
        cost_estimate=cost,
    )(*args)


def matched(first, second, axis):
    count = lax.axis_size(axis)
    ways = (-1, 1) if axis == "wide" else (1, -1)
    one = lax.ppermute(first, axis, [(i, (i + ways[i % 2]) % count) for i in range(count)])
    two = lax.ppermute(second, axis, [(i, (i - ways[i % 2]) % count) for i in range(count)])
    return one, two


def flipped(block, wide_step, narrow_step):
    wide, narrow = lax.axis_size("wide"), lax.axis_size("narrow")
    pairs = [
        (w * narrow + z, (w ^ wide_step) * narrow + (z ^ narrow_step))
        for w in range(wide)
        for z in range(narrow)
    ]
    return lax.ppermute(block, ("wide", "narrow"), pairs)


def summed(send, keep, beside):
    stages = []
    for axis, step in (("wide", 2), ("narrow", 1)):
        while step < lax.axis_size(axis):
            if 2 * step < lax.axis_size(axis):
                stage = (2 * step, 3 * step, step) if axis == "wide" else (3 * step, 2 * step, step)
            else:
                stage = (step,)
            stages.append([(bits, 0) if axis == "wide" else (0, bits) for bits in stage])
            step *= 4
    block = keep + flipped(send, 1, 0)
    for i, stage in enumerate(stages):
        if i == len(stages) - 1:
            block, beside = lax.optimization_barrier((block, beside))
        received = [flipped(block, *steps) for steps in stage]
        block = block + functools.reduce(jnp.add, received)
    return block, flipped(block, 1, 0), beside


def per_device(
    fractions,
    cell_lengths,
    features,
    atom_counts,
    send_index,
    senders,
    radial,
    self_weight,
    message_weight,
    charge_weight,
    wave_numbers,
):
    atoms, width = features.shape
    ghosts = send_index.shape[1]
    rows = atoms + 4 * ghosts
    total_atoms = atoms * lax.axis_size("wide") * lax.axis_size("narrow")
    scale = 4.0 / math.sqrt(total_atoms * wave_numbers.shape[1])
    picked_outs = [((width, ghosts), f32)] * 2
    hidden_out = [((width, atoms), bf16)]
    sum_out = [((width, atoms), f32)]
    busy = pl.CostEstimate(flops=10**9, bytes_accessed=20 * 2**20, transcendentals=0)
    readout = charge_weight.T
    counts = atom_counts.reshape(1, 1)

    (opened,) = call(opening_kernel, [((8, 128), f32)], cost=busy)
    hidden, p2, p3 = call(
        first_kernel,
        hidden_out + picked_outs,
        opened,
        features,
        send_index,
        cost=busy,
    )
    g2, g3 = matched(p2, p3, "narrow")
    p0, p1 = call(wide_kernel, picked_outs, hidden, send_index, cost=busy)
    g0, g1 = matched(p0, p1, "wide")
    layers = self_weight.shape[0]
    near_edges, far_edges, self_rows, message_rows, picks = call(
        edge_kernel,
        [
            ((rows - 2 * ghosts, atoms), bf16),
            ((2 * ghosts, atoms), bf16),
            ((layers, width, width), bf16),
            ((layers, width, 2 * width), bf16),
            ((atoms, 2 * ghosts), bf16),
        ],
        senders,
        radial,
        self_weight,
        message_weight,
        send_index,
        cost=busy,
    )
    for layer in range(layers):
        own, gathered = call(
            functools.partial(local_kernel, layer), sum_out * 2, hidden, near_edges, self_rows, cost=busy
        )
        (gathered,) = call(near_kernel, sum_out, gathered, g2, g3, near_edges)
        if layer == layers - 1:
            break
        hidden, p2, p3 = call(
            functools.partial(layer_kernel, layer),
            hidden_out + picked_outs,
            hidden,
            own,
            gathered,
            g0,
            g1,
            far_edges,
            message_rows,
            picks,
            cost=busy,
        )
        g2, g3 = matched(p2, p3, "narrow")
        p0, p1 = call(wide_kernel, picked_outs, hidden, send_index, cost=busy)
        g0, g1 = matched(p0, p1, "wide")
    phases, third = call(
        phase_kernel,
        [((2, grid_rows, atoms), bf16), ((24, atoms), f32)],
        fractions,
        hidden,
        cost=busy,
    )
    send, lattice = call(
        functools.partial(last_kernel, layers - 1),
        [((half_rows, 128), f32), ((72, atoms), f32)],
        hidden,
        own,
        gathered,
        g0,
        g1,
        far_edges,
        message_rows,
        readout,
        counts,
        phases,
        third,
    )
    weights, factor, born_charges = call(
        functools.partial(weight_kernel, scale),
        [((72, grid_rows), f32), ((8, atoms), f32), ((3, atoms), f32)],
        cell_lengths,
        wave_numbers,
        lattice,
        third,
        counts,
        smem=(0,),
        scratch=[pltpu.VMEM((32, grid_rows), f32)],
        cost=busy,
    )
    (keep,) = call(keep_kernel, [((half_rows, 128), f32)], lattice, phases, cost=busy)
    half, other, (weights, factor) = summed(send, keep, (weights, factor))
    forces, energy = call(
        functools.partial(force_kernel, scale),
        [((3, atoms), f32), ((1, 1), f32)],
        half,
        other,
        lattice,
        phases,
        weights,
        factor,
        scratch=[pltpu.VMEM((2, 72, grid_rows), f32)],
    )
    return (forces, born_charges, energy[0, 0])


def solution(mesh):
    return jax.shard_map(
        per_device,
        mesh=mesh,
        in_specs=(
            P(None, ("wide", "narrow")),
            P(),
            P(("wide", "narrow"), None),
            P(("wide", "narrow")),
            P(("wide", "narrow"), None),
            P(None, ("wide", "narrow")),
            P(None, ("wide", "narrow")),
            P(),
            P(),
            P(),
            P(),
        ),
        out_specs=(P(None, ("wide", "narrow")), P(None, ("wide", "narrow")), P()),
        check_vma=False,
    )
```

```python
import functools
import math

import jax
import jax.numpy as jnp
from jax import lax
from jax.experimental import pallas as pl
from jax.experimental.pallas import tpu as pltpu
from jax.sharding import PartitionSpec as P

smearing = 0.5
two_pi = 2.0 * math.pi
kmax = 8
grid_rows = (2 * kmax + 1) * kmax
half_rows = 80
f32 = jnp.float32
bf16 = jnp.bfloat16
params = pltpu.CompilerParams(vmem_limit_bytes=48 * 1024 * 1024)


def dot_nn(a, b):
    return lax.dot_general(a, b, (((1,), (0,)), ((), ())), preferred_element_type=f32)


def dot_nt(a, b):
    return lax.dot_general(a, b, (((1,), (1,)), ((), ())), preferred_element_type=f32)


def parity(axis):
    return lax.rem(lax.axis_index(axis), 2)


def block_order(axis):
    odd = parity(axis) if axis == "wide" else 1 - parity(axis)
    first = 0 if axis == "wide" else 2
    return first + odd, first + 1 - odd


def pick_matrix(index_ref, block, atoms):
    row_ids = lax.broadcasted_iota(jnp.int32, (atoms, index_ref.shape[1]), 0)
    return jnp.where(row_ids == index_ref[pl.ds(block, 1), :], 1.0, 0.0).astype(bf16)


def opening_kernel(opened_ref):
    opened_ref[...] = jnp.zeros(opened_ref.shape, f32)


def first_kernel(opened_ref, features_ref, index_ref, hidden_ref, pa, pb):
    hidden = jnp.transpose(features_ref[...].astype(f32)).astype(bf16)
    hidden_ref[...] = hidden
    for block, picked_ref in zip(block_order("narrow"), (pa, pb)):
        picked_ref[...] = dot_nn(hidden, pick_matrix(index_ref, block, hidden.shape[1]))


def wide_kernel(hidden_ref, index_ref, pa, pb):
    hidden = hidden_ref[...]
    for block, picked_ref in zip(block_order("wide"), (pa, pb)):
        picked_ref[...] = dot_nn(hidden, pick_matrix(index_ref, block, hidden.shape[1]))


def edge_tiles(senders_ref, radial_ref, edges_ref, local, axis):
    slots, atoms = senders_ref.shape
    rows = 128
    lanes = 128
    row_ids = lax.broadcasted_iota(jnp.int32, (rows, lanes), 0).astype(f32).astype(bf16)
    ghosts = (edges_ref.shape[0] - local) // 2
    one, two = block_order(axis)
    skip_one = atoms + one * ghosts - local
    skip_two = atoms + two * ghosts - local - ghosts

    def one_tile(tile, carry):
        first = pl.multiple_of(tile * rows, rows)
        skip = jnp.where(first < local, 0, jnp.where(first < local + ghosts, skip_one, skip_two))
        sender = first + skip
        for part in range(atoms // lanes):
            window = pl.ds(part * lanes, lanes)
            local_row = jnp.clip(senders_ref[:, window] - sender, -1, rows)
            local_row = local_row.astype(f32).astype(bf16)
            weight = radial_ref[:, window].astype(bf16)
            total = jnp.zeros((rows, lanes), bf16)
            for slot in range(slots):
                total = total + jnp.where(
                    row_ids == local_row[slot : slot + 1, :],
                    weight[slot : slot + 1, :],
                    jnp.zeros((), bf16),
                )
            edges_ref[pl.ds(first, rows), window] = total
        return carry

    lax.fori_loop(0, edges_ref.shape[0] // rows, one_tile, 0)


def edge_kernel(
    senders_ref,
    radial_ref,
    self_ref,
    message_ref,
    index_ref,
    near_ref,
    far_ref,
    self_rows_ref,
    message_rows_ref,
    pick_ref,
):
    ghosts = index_ref.shape[1]
    for i, block in enumerate(block_order("narrow")):
        pick_ref[:, i * ghosts : (i + 1) * ghosts] = pick_matrix(
            index_ref, block, senders_ref.shape[1]
        )
    edge_tiles(senders_ref, radial_ref, near_ref, senders_ref.shape[1], "narrow")
    edge_tiles(senders_ref, radial_ref, far_ref, 0, "wide")
    for layer in range(self_ref.shape[0]):
        self_rows_ref[layer] = jnp.transpose(self_ref[layer].astype(f32)).astype(bf16)
        message = jnp.transpose(message_ref[layer].astype(f32)).astype(bf16)
        message_rows_ref[layer] = jnp.concatenate([message, message], axis=1)


def local_kernel(layer, hidden_ref, edges_ref, self_rows_ref, own_ref, gathered_ref):
    hidden = hidden_ref[...]
    own_ref[...] = dot_nn(self_rows_ref[layer], hidden)
    gathered_ref[...] = dot_nn(hidden, edges_ref[0 : hidden.shape[1], :])


def near_kernel(gathered_ref, g2, g3, edges_ref, sum_ref):
    received = jnp.concatenate([g2[...].astype(bf16), g3[...].astype(bf16)], axis=1)
    local = edges_ref.shape[0] - received.shape[1]
    sum_ref[...] = gathered_ref[...] + dot_nn(received, edges_ref[local:, :])


def interact(layer, hidden_ref, own_ref, gathered_ref, g0, g1, edges_ref, message_rows_ref):
    received = jnp.concatenate([g0[...].astype(bf16), g1[...].astype(bf16)], axis=1)
    gathered = gathered_ref[...] + dot_nn(received, edges_ref[...])
    high = gathered.astype(bf16)
    low = (gathered - high.astype(f32)).astype(bf16)
    total = own_ref[...] + dot_nn(message_rows_ref[layer], jnp.concatenate([high, low], axis=0))
    gate = 0.5 * total * (1.0 + jnp.tanh(0.5 * total))
    return (hidden_ref[...].astype(f32) + gate).astype(bf16)


def layer_kernel(
    layer, hidden_ref, own_ref, gathered_ref, g0, g1, edges_ref, message_rows_ref, pick_ref, out_ref, p2, p3
):
    hidden = interact(layer, hidden_ref, own_ref, gathered_ref, g0, g1, edges_ref, message_rows_ref)
    out_ref[...] = hidden
    picked = dot_nn(hidden, pick_ref[...])
    ghosts = p2.shape[1]
    p2[...] = picked[:, 0:ghosts]
    p3[...] = picked[:, ghosts:]


def structure_part(lattice, phase_ref, part, out_ref):
    phases = phase_ref[part]
    out_ref[0:72, :] = dot_nt(lattice, phases[0:128, :])
    out_ref[72:80, 0:72] = dot_nt(phases[128:grid_rows, :], lattice)
    out_ref[72:80, 72:128] = jnp.zeros((8, 56), f32)


def last_kernel(
    layer,
    hidden_ref,
    own_ref,
    gathered_ref,
    g0,
    g1,
    edges_ref,
    message_rows_ref,
    readout_ref,
    count_ref,
    phase_ref,
    third_ref,
    after_ref,
    send_ref,
    lattice_ref,
):
    hidden = interact(layer, hidden_ref, own_ref, gathered_ref, g0, g1, edges_ref, message_rows_ref)
    atoms = hidden.shape[1]
    slot_ids = lax.broadcasted_iota(jnp.int32, (8, atoms), 1)
    readout = readout_ref[...].astype(f32)
    readout = jnp.concatenate([readout, jnp.zeros_like(readout)], axis=0).astype(bf16)
    charges = jnp.where(slot_ids < count_ref[...], dot_nn(readout, hidden), 0.0)
    cosine = third_ref[0:8, :]
    sine = third_ref[8:16, :]
    rows = [charges[c : c + 1, :] * cosine for c in range(4)]
    rows = rows + [charges[c : c + 1, :] * sine for c in range(4)]
    lattice = jnp.concatenate(rows + [charges], axis=0)
    lattice_ref[...] = lattice
    structure_part(lattice.astype(bf16), phase_ref, 1 - parity("wide"), send_ref)


def keep_kernel(lattice_ref, phase_ref, keep_ref):
    structure_part(lattice_ref[...].astype(bf16), phase_ref, parity("wide"), keep_ref)


def wave_weight(m0, m1, m2, cell_ref):
    w0 = two_pi * m0 / cell_ref[0]
    w1 = two_pi * m1 / cell_ref[1]
    w2 = two_pi * m2 / cell_ref[2]
    squared = w0 * w0 + w1 * w1 + w2 * w2
    return jnp.exp(-0.5 * smearing * smearing * squared) / squared


def phase_kernel(fractions_ref, after_ref, phase_ref, third_ref):
    atoms = fractions_ref.shape[1]
    orders = lax.broadcasted_iota(jnp.int32, (8, atoms), 0).astype(f32) + 1.0
    cosines, sines = [], []
    for axis in range(3):
        turns = orders * fractions_ref[axis : axis + 1, :]
        angle = two_pi * (turns - jnp.round(turns))
        cosines.append(jnp.cos(angle))
        sines.append(jnp.sin(angle))
    third_ref[0:8, :] = cosines[2]
    third_ref[8:16, :] = sines[2]
    for axis in range(3):
        third_ref[16 + axis : 17 + axis, :] = cosines[axis][0:1, :]
    c0, s0 = cosines[0], sines[0]
    for m in range(-kmax, kmax + 1):
        window = pl.ds((m + kmax) * kmax, kmax)
        if m == 0:
            re, im = c0, s0
        else:
            row = abs(m) - 1
            c1 = cosines[1][row : row + 1, :]
            s1 = sines[1][row : row + 1, :]
            if m < 0:
                s1 = -s1
            re, im = c0 * c1 - s0 * s1, s0 * c1 + c0 * s1
        phase_ref[0, window, :] = re.astype(bf16)
        phase_ref[1, window, :] = im.astype(bf16)


def weight_kernel(
    scale,
    cell_ref,
    numbers_ref,
    count_ref,
    after_ref,
    weight_ref,
    factor_ref,
    acc,
):
    alive = lax.broadcasted_iota(jnp.int32, (1, factor_ref.shape[1]), 1) < count_ref[...]
    for axis in range(3):
        factor_ref[axis : axis + 1, :] = jnp.where(alive, -(two_pi * scale / cell_ref[axis]), 0.0)
    acc[...] = jnp.zeros_like(acc)
    width = math.gcd(numbers_ref.shape[1], 1024)
    plane_ids = lax.broadcasted_iota(jnp.int32, (grid_rows, width), 0)
    third_ids = lax.broadcasted_iota(jnp.int32, (32, width), 0)
    third_ids = jnp.where(
        third_ids < 8, third_ids + 1, jnp.where(third_ids < 16, 7 - third_ids, (third_ids - 16) * 64)
    )

    def count(step, carry):
        window = pl.ds(pl.multiple_of(step * width, width), width)
        numbers = numbers_ref[:, window]
        plane = (numbers[1:2, :] + kmax) * kmax + numbers[0:1, :] - 1
        in_plane = jnp.where(plane_ids == plane, 1.0, 0.0).astype(bf16)
        in_third = jnp.where(third_ids == numbers[2:3, :], 1.0, 0.0).astype(bf16)
        acc[...] += dot_nt(in_third, in_plane)
        return carry

    lax.fori_loop(0, numbers_ref.shape[1] // width, count, 0)
    lane = lax.broadcasted_iota(jnp.int32, (8, grid_rows), 1)
    m0 = (lane % 8 + 1).astype(f32)
    m1 = (lane // 8 - kmax).astype(f32)
    m2 = lax.broadcasted_iota(jnp.int32, (8, grid_rows), 0).astype(f32) + 1.0
    weight = wave_weight(m0, m1, m2, cell_ref)
    up = weight * acc[0:8, :]
    down = weight * acc[8:16, :]
    flat = wave_weight(m0, m1, 0.0 * m0, cell_ref) * acc[16:17, :]
    for c in range(4):
        weight_ref[8 * c : 8 * c + 8, :] = up
        weight_ref[32 + 8 * c : 40 + 8 * c, :] = down
    weight_ref[64:72, :] = flat


def born_kernel(lattice_ref, third_ref, born_ref, done_ref):
    total = jnp.sum(lattice_ref[64:68, :], axis=0, keepdims=True)
    born_ref[...] = total * third_ref[16:19, :]
    done_ref[...] = jnp.zeros(done_ref.shape, f32)


def force_kernel(
    scale,
    half_ref,
    other_ref,
    lattice_ref,
    phase_ref,
    weight_ref,
    factor_ref,
    forces_ref,
    energy_ref,
    sums_ref,
):
    core = parity("wide")
    for part_ref, part in ((half_ref, core), (other_ref, 1 - core)):
        sums_ref[part, :, 0:128] = part_ref[0:72, :]
        sums_ref[part, :, 128:grid_rows] = jnp.transpose(part_ref[72:80, :])[0:72, :]
    real = sums_ref[0]
    imag = sums_ref[1]
    real_cos, real_sin, real_flat = real[0:32], real[32:64], real[64:72]
    imag_cos, imag_sin, imag_flat = imag[0:32], imag[32:64], imag[64:72]
    weight_up = weight_ref[0:32, :]
    weight_down = weight_ref[32:64, :]
    weight_flat = weight_ref[64:72, :]
    up_re, up_im = real_cos - imag_sin, imag_cos + real_sin
    down_re, down_im = real_cos + imag_sin, imag_cos - real_sin
    up_im_w, up_re_w = weight_up * up_im, weight_up * up_re
    down_im_w, down_re_w = weight_down * down_im, weight_down * down_re
    flat_im_w, flat_re_w = weight_flat * imag_flat, weight_flat * real_flat
    power = up_im_w * up_im + up_re_w * up_re + down_im_w * down_im + down_re_w * down_re
    flat_power = flat_im_w * imag_flat + flat_re_w * real_flat
    power = jnp.sum(power, axis=0, keepdims=True) + jnp.sum(flat_power, axis=0, keepdims=True)
    energy_ref[...] = (0.5 * scale) * jnp.sum(power, axis=1, keepdims=True)

    im_sum, im_diff = up_im_w + down_im_w, up_im_w - down_im_w
    re_sum, re_diff = up_re_w + down_re_w, down_re_w - up_re_w
    even_real = jnp.concatenate([im_sum, re_diff, flat_im_w], axis=0)
    even_imag = jnp.concatenate([-re_sum, -im_diff, -flat_re_w], axis=0)
    m2 = (lax.broadcasted_iota(jnp.int32, (32, grid_rows), 0) % 8 + 1).astype(f32)
    odd_real = jnp.concatenate([m2 * im_diff, -m2 * re_sum], axis=0)
    odd_imag = jnp.concatenate([m2 * re_diff, -m2 * im_sum], axis=0)
    lane = lax.broadcasted_iota(jnp.int32, (72, grid_rows), 1)
    m0 = (lane % 8 + 1).astype(f32)
    m1 = (lane // 8 - kmax).astype(f32)
    with_real = jnp.concatenate([even_real * m0, even_real * m1, odd_real], axis=0).astype(bf16)
    with_imag = jnp.concatenate([even_imag * m0, even_imag * m1, odd_imag], axis=0).astype(bf16)
    back = dot_nn(with_real, phase_ref[0]) + dot_nn(with_imag, phase_ref[1])
    lattice = lattice_ref[...]
    for axis in range(3):
        rows = 64 if axis == 2 else 72
        terms = lattice[0:rows] * back[72 * axis : 72 * axis + rows]
        gradient = jnp.sum(terms, axis=0, keepdims=True)
        forces_ref[axis : axis + 1, :] = factor_ref[axis : axis + 1, :] * gradient


def call(kernel, outs, *args, smem=(), scratch=(), cost=None):
    specs = [
        pl.BlockSpec(memory_space=pltpu.SMEM if i in smem else pltpu.VMEM)
        for i in range(len(args))
    ]
    return pl.pallas_call(
        kernel,
        out_shape=[jax.ShapeDtypeStruct(shape, dtype) for shape, dtype in outs],
        in_specs=specs,
        out_specs=[pl.BlockSpec(memory_space=pltpu.VMEM)] * len(outs),
        scratch_shapes=list(scratch),
        compiler_params=params,
        cost_estimate=cost,
    )(*args)


def matched(first, second, axis):
    count = lax.axis_size(axis)
    ways = (-1, 1) if axis == "wide" else (1, -1)
    one = lax.ppermute(first, axis, [(i, (i + ways[i % 2]) % count) for i in range(count)])
    two = lax.ppermute(second, axis, [(i, (i - ways[i % 2]) % count) for i in range(count)])
    return one, two


def flipped(block, wide_step, narrow_step):
    wide, narrow = lax.axis_size("wide"), lax.axis_size("narrow")
    pairs = [
        (w * narrow + z, (w ^ wide_step) * narrow + (z ^ narrow_step))
        for w in range(wide)
        for z in range(narrow)
    ]
    return lax.ppermute(block, ("wide", "narrow"), pairs)


def summed(send, keep, beside):
    stages = []
    for axis, step in (("wide", 2), ("narrow", 1)):
        while step < lax.axis_size(axis):
            if 2 * step < lax.axis_size(axis):
                stage = (2 * step, 3 * step, step) if axis == "wide" else (3 * step, 2 * step, step)
            else:
                stage = (step,)
            stages.append([(bits, 0) if axis == "wide" else (0, bits) for bits in stage])
            step *= 4
    block = keep + flipped(send, 1, 0)
    for i, stage in enumerate(stages):
        if i == len(stages) - 1:
            block, beside = lax.optimization_barrier((block, beside))
        received = [flipped(block, *steps) for steps in stage]
        block = block + functools.reduce(jnp.add, received)
    return block, flipped(block, 1, 0), beside


def per_device(
    fractions,
    cell_lengths,
    features,
    atom_counts,
    send_index,
    senders,
    radial,
    self_weight,
    message_weight,
    charge_weight,
    wave_numbers,
):
    atoms, width = features.shape
    ghosts = send_index.shape[1]
    rows = atoms + 4 * ghosts
    total_atoms = atoms * lax.axis_size("wide") * lax.axis_size("narrow")
    scale = 4.0 / math.sqrt(total_atoms * wave_numbers.shape[1])
    picked_outs = [((width, ghosts), f32)] * 2
    hidden_out = [((width, atoms), bf16)]
    sum_out = [((width, atoms), f32)]
    busy = pl.CostEstimate(flops=10**9, bytes_accessed=20 * 2**20, transcendentals=0)
    readout = charge_weight.T
    counts = atom_counts.reshape(1, 1)

    (opened,) = call(opening_kernel, [((8, 128), f32)], cost=busy)
    hidden, p2, p3 = call(
        first_kernel,
        hidden_out + picked_outs,
        opened,
        features,
        send_index,
        cost=busy,
    )
    g2, g3 = matched(p2, p3, "narrow")
    p0, p1 = call(wide_kernel, picked_outs, hidden, send_index, cost=busy)
    g0, g1 = matched(p0, p1, "wide")
    layers = self_weight.shape[0]
    near_edges, far_edges, self_rows, message_rows, picks = call(
        edge_kernel,
        [
            ((rows - 2 * ghosts, atoms), bf16),
            ((2 * ghosts, atoms), bf16),
            ((layers, width, width), bf16),
            ((layers, width, 2 * width), bf16),
            ((atoms, 2 * ghosts), bf16),
        ],
        senders,
        radial,
        self_weight,
        message_weight,
        send_index,
        cost=busy,
    )
    for layer in range(layers):
        own, gathered = call(
            functools.partial(local_kernel, layer), sum_out * 2, hidden, near_edges, self_rows, cost=busy
        )
        (gathered,) = call(near_kernel, sum_out, gathered, g2, g3, near_edges)
        if layer == layers - 1:
            break
        hidden, p2, p3 = call(
            functools.partial(layer_kernel, layer),
            hidden_out + picked_outs,
            hidden,
            own,
            gathered,
            g0,
            g1,
            far_edges,
            message_rows,
            picks,
            cost=busy,
        )
        g2, g3 = matched(p2, p3, "narrow")
        p0, p1 = call(wide_kernel, picked_outs, hidden, send_index, cost=busy)
        g0, g1 = matched(p0, p1, "wide")
    phases, third = call(
        phase_kernel,
        [((2, grid_rows, atoms), bf16), ((24, atoms), f32)],
        fractions,
        hidden,
        cost=busy,
    )
    weights, factor = call(
        functools.partial(weight_kernel, scale),
        [((72, grid_rows), f32), ((8, atoms), f32)],
        cell_lengths,
        wave_numbers,
        counts,
        hidden,
        smem=(0,),
        scratch=[pltpu.VMEM((32, grid_rows), f32)],
        cost=busy,
    )
    send, lattice = call(
        functools.partial(last_kernel, layers - 1),
        [((half_rows, 128), f32), ((72, atoms), f32)],
        hidden,
        own,
        gathered,
        g0,
        g1,
        far_edges,
        message_rows,
        readout,
        counts,
        phases,
        third,
        factor,
    )
    born_charges, done = call(
        born_kernel, [((3, atoms), f32), ((8, 128), f32)], lattice, third, cost=busy
    )
    (keep,) = call(keep_kernel, [((half_rows, 128), f32)], lattice, phases, cost=busy)
    half, other, done = summed(send, keep, done)
    forces, energy = call(
        functools.partial(force_kernel, scale),
        [((3, atoms), f32), ((1, 1), f32)],
        half,
        other,
        lattice,
        phases,
        weights,
        factor,
        scratch=[pltpu.VMEM((2, 72, grid_rows), f32)],
    )
    return (forces, born_charges, energy[0, 0])


def solution(mesh):
    return jax.shard_map(
        per_device,
        mesh=mesh,
        in_specs=(
            P(None, ("wide", "narrow")),
            P(),
            P(("wide", "narrow"), None),
            P(("wide", "narrow")),
            P(("wide", "narrow"), None),
            P(None, ("wide", "narrow")),
            P(None, ("wide", "narrow")),
            P(),
            P(),
            P(),
            P(),
        ),
        out_specs=(P(None, ("wide", "narrow")), P(None, ("wide", "narrow")), P()),
        check_vma=False,
    )
```
